256 devices in a mesh: dp: 32 (over z, y), mp: 8 (over x, core).
Axes of the slice: x: 4, y: 4, z: 8, core: 2. Of those that a mesh axis runs over, the one named last changes fastest.
Arguments:
- loaded: bfloat16 [5, 8192, 8192], P(None, ('dp', 'mp')), may hold values from -6 to 6
- row_plan: int32 [8192], P(('dp', 'mp')), may hold values from 0 to 8191, as said below
- lengths: int32 [3], replicated, may hold values from 1 to 4096, 8192 in all
- se_filter: bfloat16 [7, 512], P(None, 'mp'), may hold values from -2 to 2
- mr_filter: bfloat16 [128, 512], P(None, 'mp'), may hold values from -0.5 to 0.5
- grad_out: bfloat16 [8192, 8192], P('dp', 'mp'), may hold values from -6 to 6
Outputs:
- grad_loaded: bfloat16 [5, 8192, 8192], P(None, ('dp', 'mp'))
- se_grad: float32 [7, 512], P(None, 'mp')
- mr_grad: float32 [128, 512], P(None, 'mp')
The draws below stay inside these ranges and needn't reach their ends.
Inputs may be any that keep to these rules, and one draw needn't show every extreme that they name: row_plan is a permutation of the 8192 packed rows; of the 256 loaded rows of one dp index at most 16 go to the packed rows k * 256 to (k + 1) * 256 - 1 of any one k, and exactly 16 to some k.
All inputs are finite; a program needn't handle non-finite values.
Results may differ from the reference program's by a relative error of at most 0.0075.
Values may be sent and summed in bfloat16 or wider, within the bound.
No kernel may reach another device: no remote copies, remote signals or barrier semaphores. Data moves between devices by JAX's collectives and lax.ppermute only.
A program may use at most 128 MiB of HBM per device.

```python
import math
import jax
import jax.numpy as jnp
import numpy as np
from jax import lax

D = 8192
GROUPS = 512
SE_TAPS = 7
MR_TAPS = 128
ROWS = 256
NSEQ = 3
TOTAL = 8192
CAP = 16


def draw_row_plan(key, part):
    key = jax.random.fold_in(key, 7)
    shards = TOTAL // ROWS
    subkeys = jax.random.split(key, 5)
    cells = jax.random.permutation(subkeys[0], (shards - 1) * CAP).astype(jnp.int32)
    chosen = cells[:ROWS - CAP] // CAP
    others = jnp.sum((chosen[:, None] == jnp.arange(shards - 1, dtype=jnp.int32)[None, :]).astype(jnp.int32), axis=0)
    widths = jnp.concatenate([jnp.full((1,), CAP, jnp.int32), others.astype(jnp.int32)])
    source_order = jax.random.permutation(subkeys[1], shards).astype(jnp.int32)
    target_order = jax.random.permutation(subkeys[2], shards).astype(jnp.int32)
    counts = widths[jnp.remainder(target_order[None, :] - source_order[:, None], shards)]
    upper = jnp.cumsum(counts, axis=1)
    lower = upper - counts
    placed = jnp.arange(ROWS, dtype=jnp.int32)
    shard_of = jnp.sum((upper[:, None, :] <= placed[None, :, None]).astype(jnp.int32), axis=2)
    offset = placed[None, :] - jnp.take_along_axis(lower, shard_of, axis=1)
    column_base = jnp.cumsum(counts, axis=0) - counts
    slot_index = jnp.take_along_axis(column_base, shard_of, axis=1) + offset
    slot_orders = jax.vmap(lambda sub: jax.random.permutation(sub, ROWS))(jax.random.split(subkeys[3], shards)).astype(jnp.int32)
    slots = slot_orders[shard_of, slot_index]
    targets = (shard_of * ROWS + slots).astype(jnp.int32)
    row_orders = jax.vmap(lambda sub: jax.random.permutation(sub, ROWS))(jax.random.split(subkeys[4], shards)).astype(jnp.int32)
    result = jnp.zeros((shards, ROWS), jnp.int32).at[jnp.arange(shards, dtype=jnp.int32)[:, None], row_orders].set(targets)
    return result.reshape(TOTAL)


def shard_levels(rng, dims, pieces, least, top_value):
    def one(dim, shards_of):
        draws = jax.random.uniform(jax.random.fold_in(jax.random.fold_in(rng, 6), dim), (shards_of,), jnp.float32, least / len(pieces), top_value / len(pieces))
        return jnp.repeat(jnp.exp(draws), dims[dim] // shards_of).reshape((-1,) + (1,) * (len(dims) - dim - 1))

    loudness = one(*pieces[0])
    for cut in pieces[1:]:
        loudness = loudness * one(*cut)
    return loudness


def split_up(count, total, reach, slope):
    weights = [(1 << 20) // math.isqrt(rank ** slope) + 1 for rank in range(2, count + 1)]
    spare, given = total - reach - (count - 1), [1] * (count - 1)
    while spare > 0:
        candidates = [i for i in range(count - 1) if given[i] < reach]
        pool, budget = sum([weights[i] for i in candidates]), spare
        for i in candidates:
            addition = min(reach - given[i], max(1, budget * weights[i] // pool), spare)
            given[i] = given[i] + addition
            spare = spare - addition
    return np.array([reach] + given)


def ragged(key, number_of, total, reach, skew):
    if number_of == 2:
        one = jax.random.randint(key, (), max(1, total - reach), min(reach, total - 1) + 1)
        return jnp.stack([one, total - one])
    sizes = jnp.asarray(split_up(number_of, total, reach, skew), jnp.int32)
    twos = (number_of - 1) // 2
    donor, receiver = sizes[1:1 + 2 * twos:2], sizes[2:2 + 2 * twos:2]
    slack = jnp.minimum(donor - 1, reach - receiver)
    shifted = jax.random.randint(jax.random.fold_in(key, 1), (twos,), 0, 1 << 20) % (slack + 1)
    sizes = sizes.at[1:1 + 2 * twos:2].set(donor - shifted).at[2:2 + 2 * twos:2].set(receiver + shifted)
    return sizes[jax.random.permutation(jax.random.fold_in(key, 2), number_of)]


def noise(stream_key, extent, deviation, limit, cuts=(), kind=jnp.bfloat16):
    entries = jax.random.normal(stream_key, extent, jnp.float32) * deviation
    if len(cuts) > 0:
        entries = shard_levels(stream_key, extent, cuts, -0.22, 0.18) * entries
    return jnp.clip(entries, min=-limit, max=limit).astype(kind)


def setup_inputs(seed: int = 0) -> dict:
    keys = jax.random.split(jax.random.key(seed), 7)
    loaded = noise(keys[0], (5, TOTAL, D), 1.0, 6.0, ((1, 256),))
    row_plan = draw_row_plan(jax.random.fold_in(keys[6], 71), 0)
    lengths = ragged(keys[2], NSEQ, TOTAL, TOTAL // 2, 2).astype(jnp.int32)
    se_filter = noise(keys[3], (SE_TAPS, GROUPS), SE_TAPS ** -0.5, 2.0, ((1, 8),))
    mr_filter = noise(keys[4], (MR_TAPS, GROUPS), MR_TAPS ** -0.5, 0.5, ((1, 8),))
    grad_out = noise(keys[5], (TOTAL, D), 1.0, 6.0, ((0, 32), (1, 8)))
    return {"loaded": loaded, "row_plan": row_plan, "lengths": lengths, "se_filter": se_filter, "mr_filter": mr_filter, "grad_out": grad_out}


def band_tiles(taps_by_group, causal):
    tap_count, group_count = taps_by_group.shape
    columns = jnp.transpose(taps_by_group)
    if causal:
        head_row = jnp.concatenate([jnp.zeros((group_count, 1), taps_by_group.dtype), columns[:, ::-1], jnp.zeros((group_count, tap_count), taps_by_group.dtype)], axis=1)
    else:
        head_row = jnp.concatenate([columns, jnp.zeros((group_count, tap_count + 1), taps_by_group.dtype)], axis=1)
    repeated = jnp.tile(head_row, (1, tap_count))
    return repeated[:, : 2 * tap_count * tap_count].reshape(group_count, tap_count, 2 * tap_count)


def lag_sums(blocks):
    group_count, tap_count, span_width = blocks.shape
    flat_rows = blocks.reshape(group_count, tap_count * span_width)
    flat_rows = jnp.concatenate([flat_rows, jnp.zeros((group_count, tap_count), blocks.dtype)], axis=1)
    skewed = flat_rows.reshape(group_count, tap_count, span_width + 1)
    return jnp.transpose(jnp.sum(skewed[:, :, 1: tap_count + 1], axis=1)[:, ::-1])


def reference(loaded, row_plan, lengths, se_filter, mr_filter, grad_out):
    row_count = loaded.shape[1]
    channels = loaded.shape[2]
    group_count = se_filter.shape[1]
    per_group = channels // group_count
    short_taps = se_filter.shape[0]
    long_taps = mr_filter.shape[0]
    seq_count = lengths.shape[0]
    slab_width = math.gcd(channels, 1024)
    slab_groups = slab_width // per_group
    positions = jnp.arange(row_count, dtype=jnp.int32)
    finish = jnp.cumsum(lengths).astype(jnp.int32)
    seq_index = jnp.sum((finish[None, :] <= positions[:, None]).astype(jnp.int32), axis=1)
    spread_at = (positions + long_taps * (seq_index + 1)).astype(jnp.int32)
    spread_len = row_count + long_taps * (seq_count + 1)
    tile_count = spread_len // long_taps
    forward_all = band_tiles(mr_filter, True)
    backward_all = band_tiles(mr_filter, False)
    unit_scale = (row_count * per_group) ** -0.5

    def spread(values):
        return jnp.zeros((spread_len, values.shape[1]), values.dtype).at[spread_at].set(values)

    def delayed(values, step_lag):
        return jnp.concatenate([jnp.zeros((step_lag, values.shape[1]), values.dtype), values[: spread_len - step_lag]], axis=0)

    def advanced(values, step_lag):
        return jnp.concatenate([values[step_lag:], jnp.zeros((step_lag, values.shape[1]), values.dtype)], axis=0)

    def windows(values, causal):
        filler = jnp.zeros((long_taps, values.shape[1]), values.dtype)
        joined = jnp.concatenate([filler, values] if causal else [values, filler], axis=0)
        lower = joined[:-long_taps].reshape(tile_count, long_taps, slab_groups, per_group)
        upper = joined[long_taps:].reshape(tile_count, long_taps, slab_groups, per_group)
        return jnp.concatenate([lower, upper], axis=1)

    def one_slab(slab_index, carry):
        grads, short_sums, long_sums = carry
        slab_start = slab_index * slab_width
        group_start = slab_index * slab_groups
        streams = lax.dynamic_slice_in_dim(loaded, slab_start, slab_width, 2)
        arranged = jnp.zeros_like(streams).at[:, row_plan, :].set(streams)
        gate_one = arranged[0].astype(jnp.float32)
        key_one = arranged[1].astype(jnp.float32)
        value_one = arranged[2].astype(jnp.float32)
        gate_two = arranged[3].astype(jnp.float32)
        key_two = arranged[4].astype(jnp.float32)
        cotangent = lax.dynamic_slice_in_dim(grad_out, slab_start, slab_width, 1).astype(jnp.float32)
        short_weights = jnp.repeat(lax.dynamic_slice_in_dim(se_filter, group_start, slab_groups, 1).astype(jnp.float32), per_group, axis=1)
        forward_tiles = lax.dynamic_slice_in_dim(forward_all, group_start, slab_groups, 0).astype(jnp.float32)
        backward_tiles = lax.dynamic_slice_in_dim(backward_all, group_start, slab_groups, 0).astype(jnp.float32)

        inner_one = (key_one * value_one).astype(jnp.bfloat16)
        inner_one_p = spread(inner_one)
        short_mix_p = jnp.zeros((spread_len, slab_width), jnp.float32)
        for step_lag in range(short_taps):
            short_mix_p = short_mix_p + delayed(inner_one_p, step_lag).astype(jnp.float32) * short_weights[step_lag][None, :]
        short_mix = short_mix_p[spread_at]
        middle = (gate_one * short_mix).astype(jnp.bfloat16)
        inner_two = (key_two * middle.astype(jnp.float32)).astype(jnp.bfloat16)
        inner_two_win = windows(spread(inner_two), True).astype(jnp.float32)
        long_mix = jnp.einsum("gim,bmgc->bigc", forward_tiles, inner_two_win, precision=lax.Precision.HIGHEST).reshape(spread_len, slab_width)[spread_at]

        grad_mix_two = (cotangent * gate_two).astype(jnp.bfloat16)
        grad_gate_two = (cotangent * long_mix).astype(jnp.bfloat16)
        grad_mix_two_p = spread(grad_mix_two)
        grad_win = windows(grad_mix_two_p, False).astype(jnp.float32)
        grad_inner_two = jnp.einsum("gim,bmgc->bigc", backward_tiles, grad_win, precision=lax.Precision.HIGHEST).reshape(spread_len, slab_width)[spread_at]
        grad_key_two = (grad_inner_two * middle.astype(jnp.float32)).astype(jnp.bfloat16)
        grad_middle = grad_inner_two * key_two
        grad_gate_one = (grad_middle * short_mix).astype(jnp.bfloat16)
        grad_mix_one = (grad_middle * gate_one).astype(jnp.bfloat16)
        grad_mix_one_p = spread(grad_mix_one)
        grad_inner_p = jnp.zeros((spread_len, slab_width), jnp.float32)
        for step_lag in range(short_taps):
            grad_inner_p = grad_inner_p + advanced(grad_mix_one_p, step_lag).astype(jnp.float32) * short_weights[step_lag][None, :]
        grad_inner_one = grad_inner_p[spread_at].astype(jnp.bfloat16)
        grad_key_one = (grad_inner_one.astype(jnp.float32) * value_one).astype(jnp.bfloat16)
        grad_value_one = (grad_inner_one.astype(jnp.float32) * key_one).astype(jnp.bfloat16)

        grad_blocks = grad_mix_two_p.astype(jnp.float32).reshape(tile_count, long_taps, slab_groups, per_group)
        lag_grid = jnp.einsum("bigc,bmgc->gim", grad_blocks, inner_two_win, precision=lax.Precision.HIGHEST)
        long_part = lag_sums(lag_grid)
        short_rows = []
        for step_lag in range(short_taps):
            terms = grad_mix_one_p.astype(jnp.float32) * delayed(inner_one_p, step_lag).astype(jnp.float32)
            short_rows.append(jnp.sum(terms.reshape(spread_len, slab_groups, per_group), axis=(0, 2)))
        short_part = jnp.stack(short_rows)
        stacked = jnp.stack([grad_gate_one, grad_key_one, grad_value_one, grad_gate_two, grad_key_two])[:, row_plan, :]
        grads = lax.dynamic_update_slice_in_dim(grads, stacked, slab_start, 2)
        short_sums = lax.dynamic_update_slice_in_dim(short_sums, short_part, group_start, 1)
        long_sums = lax.dynamic_update_slice_in_dim(long_sums, long_part, group_start, 1)
        return grads, short_sums, long_sums

    initial = (jnp.zeros_like(loaded), jnp.zeros(se_filter.shape, jnp.float32), jnp.zeros(mr_filter.shape, jnp.float32))
    grads, short_sums, long_sums = lax.fori_loop(0, channels // slab_width, one_slab, initial)
    return grads, short_sums * unit_scale, long_sums * unit_scale
```

```python
import functools

import jax
import jax.numpy as jnp
from jax import lax
from jax.experimental import pallas as pl
from jax.experimental.pallas import tpu as pltpu
from jax.sharding import Mesh, PartitionSpec as P

PLANES = 8
QUARTERS = 4
PEERS = 32
PLANE_ROWS = 1024
WIDTH = 128
CHUNKS = 2
PER_GROUP = 16
GROUPS = WIDTH // PER_GROUP
STREAMS = 5
OWN_ROWS = 32
TAPS = 128
SHORT = 7
SPAN = 2 * TAPS
SLABS = PLANE_ROWS // TAPS
FULL_CAP = 256
LEAN_CAP = 160
ALL_AXES = ("z", "y", "x", "c")
IN_PLANE = ("y", "x", "c")
BF = jnp.bfloat16
F32 = jnp.float32
I32 = jnp.int32


def iota(shape, dim):
    return lax.broadcasted_iota(I32, shape, dim)


def one_hot(mask):
    return jnp.where(mask, 1.0, 0.0).astype(BF)


def call(body, out_shape, n_in_smem=0, n_in=0, scratch=(), flops=0, bytes_accessed=0):
    smem = [pl.BlockSpec(memory_space=pltpu.SMEM)] * n_in_smem
    vmem = [pl.BlockSpec(memory_space=pltpu.VMEM)] * n_in
    outs = jax.tree.map(lambda s: pl.BlockSpec(memory_space=pltpu.VMEM), out_shape)
    return pl.pallas_call(
        body,
        out_shape=out_shape,
        in_specs=smem + vmem,
        out_specs=outs,
        scratch_shapes=list(scratch),
        compiler_params=pltpu.CompilerParams(vmem_limit_bytes=48 * 2**20),
        cost_estimate=pl.CostEstimate(
            flops=flops, bytes_accessed=bytes_accessed, transcendentals=0
        ),
    )


def peer_column(peer, chunk):
    quarter, column = peer // 8, peer % 8
    return (column * QUARTERS + quarter) * CHUNKS * WIDTH + chunk * WIDTH


def split_kernel(chunk, loaded_ref, out_ref):
    for peer in range(PEERS):
        first = peer_column(peer, chunk)
        for stream in range(STREAMS):
            out_ref[peer, stream * OWN_ROWS : (stream + 1) * OWN_ROWS, :] = loaded_ref[
                stream, :, first : first + WIDTH
            ]


def split_channels(loaded, chunk):
    return call(
        functools.partial(split_kernel, chunk),
        jax.ShapeDtypeStruct((PEERS, STREAMS * OWN_ROWS, WIDTH), BF),
        n_in=1,
        bytes_accessed=4 * 2**20,
    )(loaded)


def merge_kernel(*refs):
    out_ref = refs[-1]
    for chunk in range(CHUNKS):
        for peer in range(PEERS):
            first = peer_column(peer, chunk)
            for stream in range(STREAMS):
                out_ref[stream, :, first : first + WIDTH] = refs[chunk][
                    peer, stream * OWN_ROWS : (stream + 1) * OWN_ROWS, :
                ]


def merge_channels(parts):
    return call(
        merge_kernel,
        jax.ShapeDtypeStruct((STREAMS, OWN_ROWS, PEERS * CHUNKS * WIDTH), BF),
        n_in=CHUNKS,
        bytes_accessed=6 * 2**20,
    )(*parts)


def before_matrix():
    shape = (PLANE_ROWS, PLANE_ROWS)
    return one_hot(iota(shape, 0) < iota(shape, 1))


def sender_kernel(here_ref, plan_ref, code_row_ref, code_col_ref, most_ref):
    plane = here_ref[0]
    shape = (PLANES, PLANE_ROWS)
    mine = plan_ref[pl.ds(plane, 1), :]
    target = mine // PLANE_ROWS
    match = target == iota(shape, 0)
    earlier = jnp.dot(one_hot(match), before_matrix(), preferred_element_type=F32)
    rank = jnp.sum(jnp.where(match, earlier, 0.0), axis=0, keepdims=True)
    code = target * FULL_CAP + rank.astype(I32)
    code_row_ref[...] = code
    tall = jnp.broadcast_to(code.astype(F32), (WIDTH, PLANE_ROWS))
    code_col_ref[...] = jnp.transpose(tall).astype(I32)
    every = plan_ref[...] // PLANE_ROWS
    most = jnp.zeros((PLANES, 1), I32)
    for goal in range(PLANES):
        found = jnp.sum((every == goal).astype(I32), axis=1, keepdims=True)
        most = jnp.maximum(most, found)
    most_ref[...] = jnp.broadcast_to(jnp.max(most, axis=0, keepdims=True), (8, 128))


def sender_codes(here, plan):
    return call(
        sender_kernel,
        (
            jax.ShapeDtypeStruct((1, PLANE_ROWS), I32),
            jax.ShapeDtypeStruct((PLANE_ROWS, WIDTH), I32),
            jax.ShapeDtypeStruct((8, 128), I32),
        ),
        n_in_smem=1,
        n_in=1,
        flops=2 * 16 * 2**20,
        bytes_accessed=2**20,
    )(here, plan)


def receiver_kernel(here_ref, plan_ref, spot_row_ref, spot_col_ref):
    plane = here_ref[0]
    every = plan_ref[...]
    arriving = (every // PLANE_ROWS) == plane
    ranks = jnp.dot(one_hot(arriving), before_matrix(), preferred_element_type=F32)
    ranks = jnp.where(arriving, ranks.astype(I32), -1)
    local = every % PLANE_ROWS
    rows = iota((FULL_CAP, PLANE_ROWS), 0)
    kind = iota((8, PLANE_ROWS), 0)
    for source in range(PLANES):
        held = one_hot(rows == ranks[source : source + 1, :])
        spot = local[source : source + 1, :]
        parts = jnp.where(kind == 0, spot // 32, jnp.where(kind == 1, spot % 32, 1))
        read = lax.dot_general(
            parts.astype(F32).astype(BF),
            held,
            (((1,), (1,)), ((), ())),
            preferred_element_type=F32,
        )
        value = read[0:1] * 32.0 + read[1:2] + (read[2:3] - 1.0) * 4096.0
        spot_row_ref[source : source + 1, :] = value.astype(I32)
        tall = jnp.broadcast_to(value, (WIDTH, FULL_CAP))
        spot_col_ref[source] = jnp.transpose(tall).astype(I32)


def receiver_spots(here, plan):
    return call(
        receiver_kernel,
        (
            jax.ShapeDtypeStruct((PLANES, FULL_CAP), I32),
            jax.ShapeDtypeStruct((PLANES, FULL_CAP, WIDTH), I32),
        ),
        n_in_smem=1,
        n_in=1,
        flops=2 * 64 * 2**20,
        bytes_accessed=2 * 2**20,
    )(here, plan)


def pack_kernel(cap, here_ref, rows_ref, code_ref, *rest):
    outs, (field_ref, pick_ref) = rest[:PLANES], rest[PLANES:]
    plane = here_ref[0]
    for stream in range(STREAMS):
        field_ref[:, stream * WIDTH : (stream + 1) * WIDTH] = rows_ref[
            :, stream * OWN_ROWS : (stream + 1) * OWN_ROWS, :
        ].reshape(PLANE_ROWS, WIDTH)
    code = code_ref[...]
    for step in range(PLANES):
        goal = (plane + step) % PLANES
        wanted = iota((cap, PLANE_ROWS), 0) + goal * FULL_CAP
        pick_ref[step * cap : (step + 1) * cap, :] = one_hot(wanted == code)
    for step in range(PLANES):
        packed = jnp.dot(
            pick_ref[step * cap : (step + 1) * cap, :],
            field_ref[...],
            preferred_element_type=F32,
        ).astype(BF)
        for stream in range(STREAMS):
            outs[step][stream] = packed[:, stream * WIDTH : (stream + 1) * WIDTH]


def pack(cap, here, rows, code_row):
    return call(
        functools.partial(pack_kernel, cap),
        tuple(jax.ShapeDtypeStruct((STREAMS, cap, WIDTH), BF) for _ in range(PLANES)),
        n_in_smem=1,
        n_in=2,
        scratch=[
            pltpu.VMEM((PLANE_ROWS, STREAMS * WIDTH), BF),
            pltpu.VMEM((PLANES * cap, PLANE_ROWS), BF),
        ],
        flops=2 * PLANES * cap * PLANE_ROWS * STREAMS * WIDTH,
        bytes_accessed=3 * 2**20,
    )(here, rows, code_row)


def unpack_kernel(cap, here_ref, code_ref, *rest):
    parcels, (out_ref, field_ref, pick_ref) = rest[:PLANES], rest[PLANES:]
    plane = here_ref[0]
    code = code_ref[...]
    blocks = -(-cap // WIDTH)
    for step in range(PLANES):
        goal = (plane + step) % PLANES
        for stream in range(STREAMS):
            field_ref[
                step * cap : (step + 1) * cap, stream * WIDTH : (stream + 1) * WIDTH
            ] = parcels[step][stream]
        for block in range(blocks):
            first = block * WIDTH
            width = min(WIDTH, cap - first)
            wanted = iota((PLANE_ROWS, WIDTH), 1) + (goal * FULL_CAP + first)
            pick_ref[:, step * cap + first : step * cap + first + width] = one_hot(
                wanted == code
            )[:, :width]
    for part in range(4):
        rows = PLANE_ROWS // 4
        found = jnp.dot(
            pick_ref[part * rows : (part + 1) * rows, :],
            field_ref[...],
            preferred_element_type=F32,
        ).astype(BF)
        peers = rows // OWN_ROWS
        for stream in range(STREAMS):
            out_ref[
                part * peers : (part + 1) * peers,
                stream * OWN_ROWS : (stream + 1) * OWN_ROWS,
                :,
            ] = found[:, stream * WIDTH : (stream + 1) * WIDTH].reshape(
                peers, OWN_ROWS, WIDTH
            )


def unpack(cap, here, code_col, parcels):
    return call(
        functools.partial(unpack_kernel, cap),
        jax.ShapeDtypeStruct((PEERS, STREAMS * OWN_ROWS, WIDTH), BF),
        n_in_smem=1,
        n_in=1 + PLANES,
        scratch=[
            pltpu.VMEM((PLANES * cap, STREAMS * WIDTH), BF),
            pltpu.VMEM((PLANE_ROWS, PLANES * cap), BF),
        ],
        flops=2 * PLANES * cap * PLANE_ROWS * STREAMS * WIDTH,
        bytes_accessed=3 * 2**20,
    )(here, code_col, *parcels)


def starts_of(rows, lengths_ref):
    first, second, third = lengths_ref[0], lengths_ref[1], lengths_ref[2]
    total = jnp.where(rows >= first, first, 0)
    total = total + jnp.where(rows >= first + second, second, 0)
    return total + jnp.where(rows >= first + second + third, third, 0)


def band(base_row, rows):
    wide = jnp.broadcast_to(base_row, (rows, SPAN))
    return pltpu.roll(wide, 0, 1, stride=1, stride_axis=0).astype(BF)


def forward_mask(anchor, lengths_ref):
    shape = (TAPS, SPAN)
    begin = starts_of(anchor + iota(shape, 0), lengths_ref)
    return anchor - TAPS + iota(shape, 1) >= begin


def backward_mask(anchor, rows, lengths_ref):
    shape = (rows, SPAN)
    begin = starts_of(anchor + iota(shape, 1), lengths_ref)
    return anchor + iota(shape, 0) >= begin


def by_group(stacked, rows):
    lane_group = iota((rows, WIDTH), 1) // PER_GROUP
    total = stacked[0:rows]
    for group in range(1, GROUPS):
        total = jnp.where(
            lane_group == group, stacked[group * rows : (group + 1) * rows], total
        )
    return total


def short_sum(window, weights, anchor, rows, lengths_ref):
    targets = anchor + iota((rows, WIDTH), 0)
    reach = targets - starts_of(targets, lengths_ref)
    total = jnp.zeros((rows, WIDTH), F32)
    for lag in range(SHORT):
        source = window[8:] if lag == 0 else pltpu.roll(window, lag, 0)[8:]
        total = total + jnp.where(reach >= lag, source * weights[lag : lag + 1, :], 0.0)
    return total


def context_kernel(cap, here_ref, lengths_ref, spot_ref, cot_ref, se_ref, back_ref, *rest):
    parcels = rest[:PLANES]
    ctx_ref, ahead_ref, behind_ref, field_ref, pick_ref = rest[PLANES:]
    plane = here_ref[0]
    for step in range(PLANES):
        source = (plane + PLANES - step) % PLANES
        for stream in range(STREAMS):
            field_ref[
                step * cap : (step + 1) * cap, stream * WIDTH : (stream + 1) * WIDTH
            ] = parcels[step][stream]
        spot = spot_ref[pl.ds(source, 1), :][:, :cap]
        pick_ref[:, step * cap : (step + 1) * cap] = one_hot(
            iota((PLANE_ROWS, cap), 0) == spot
        )
    for part in range(4):
        rows = PLANE_ROWS // 4
        found = jnp.dot(
            pick_ref[part * rows : (part + 1) * rows, :],
            field_ref[...],
            preferred_element_type=F32,
        ).astype(BF)
        for stream in range(STREAMS):
            ctx_ref[stream, part * rows : (part + 1) * rows, :] = found[
                :, stream * WIDTH : (stream + 1) * WIDTH
            ]
    weights = se_ref[...]
    anchor = plane * PLANE_ROWS
    tail = PLANE_ROWS - TAPS
    low = tail - 16
    inner = (ctx_ref[1, low:, :].astype(F32) * ctx_ref[2, low:, :].astype(F32)).astype(BF)
    window = inner.astype(F32)[8:]
    mix = short_sum(window, weights, anchor + tail, TAPS, lengths_ref)
    middle = (ctx_ref[0, tail:, :].astype(F32) * mix).astype(BF)
    ahead_ref[0:TAPS, :] = (
        ctx_ref[4, tail:, :].astype(F32) * middle.astype(F32)
    ).astype(BF)
    ahead_ref[TAPS : TAPS + 16, :] = inner[TAPS:]
    grad_two = (
        cot_ref[0:SPAN, :].astype(F32) * ctx_ref[3, 0:SPAN, :].astype(F32)
    ).astype(BF)
    behind_ref[0:TAPS, :] = grad_two[0:TAPS]
    mask = backward_mask(anchor, 16, lengths_ref)
    tiles = []
    for group in range(GROUPS):
        tile = band(back_ref[group : group + 1, :], 16).astype(F32)
        tiles.append(jnp.where(mask, tile, 0.0).astype(BF))
    stacked = jnp.dot(
        jnp.concatenate(tiles, axis=0), grad_two, preferred_element_type=F32
    )
    grad_inner = by_group(stacked, 16)
    grad_middle = grad_inner * ctx_ref[4, 0:16, :].astype(F32)
    behind_ref[TAPS : TAPS + 16, :] = (
        grad_middle * ctx_ref[0, 0:16, :].astype(F32)
    ).astype(BF)


def context(cap, here, lengths, spot_row, cot, weights, back_base, parcels):
    return call(
        functools.partial(context_kernel, cap),
        (
            jax.ShapeDtypeStruct((STREAMS, PLANE_ROWS, WIDTH), BF),
            jax.ShapeDtypeStruct((TAPS + 16, WIDTH), BF),
            jax.ShapeDtypeStruct((TAPS + 16, WIDTH), BF),
        ),
        n_in_smem=2,
        n_in=4 + PLANES,
        scratch=[
            pltpu.VMEM((PLANES * cap, STREAMS * WIDTH), BF),
            pltpu.VMEM((PLANE_ROWS, PLANES * cap), BF),
        ],
        flops=2 * PLANES * cap * PLANE_ROWS * STREAMS * WIDTH,
        bytes_accessed=3 * 2**20,
    )(here, lengths, spot_row, cot, weights, back_base, *parcels)


def operator_kernel(
    cap, here_ref, lengths_ref, spot_ref, cot_ref, se_ref, fore_ref, back_ref,
    ctx_ref, ahead_ref, behind_ref, *rest,
):
    outs = rest[:PLANES]
    (
        long_ref, short_ref, one_ref, mix_ref, mid_ref, two_ref, gtwo_ref, gone_ref,
        fore_tile_ref, back_tile_ref, grid_ref, grads_ref, pick_ref,
    ) = rest[PLANES:]
    plane = here_ref[0]
    origin = plane * PLANE_ROWS
    weights = se_ref[...]
    for group in range(GROUPS):
        at = slice(group * TAPS, (group + 1) * TAPS)
        fore_tile_ref[at, :] = band(fore_ref[group : group + 1, :], TAPS)
        back_tile_ref[at, :] = band(back_ref[group : group + 1, :], TAPS)
    for step in range(PLANES):
        source = (plane + PLANES - step) % PLANES
        for block in range(PLANE_ROWS // WIDTH):
            spots = spot_ref[source, :cap, :]
            pick_ref[
                step * cap : (step + 1) * cap, block * WIDTH : (block + 1) * WIDTH
            ] = one_hot(iota((cap, WIDTH), 1) + block * WIDTH == spots)
    one_ref[0:8, :] = ahead_ref[TAPS : TAPS + 16, :].astype(F32)[8:]
    two_ref[0:TAPS, :] = ahead_ref[0:TAPS, :]
    gtwo_ref[PLANE_ROWS:, :] = behind_ref[0:TAPS, :]
    gone_ref[PLANE_ROWS:, :] = behind_ref[TAPS : TAPS + 16, :].astype(F32)[0:8]
    grid_ref[...] = jnp.zeros_like(grid_ref)
    short_ref[...] = jnp.zeros_like(short_ref)

    def first_pass(slab, carry):
        at = pl.multiple_of(slab * TAPS, TAPS)
        here = pl.ds(at, TAPS)
        inner = (ctx_ref[1, here, :].astype(F32) * ctx_ref[2, here, :].astype(F32)).astype(BF)
        one_ref[pl.ds(at + 8, TAPS), :] = inner.astype(F32)
        window = one_ref[pl.ds(at, TAPS + 8), :]
        mix = short_sum(window, weights, origin + at, TAPS, lengths_ref)
        mix_ref[here, :] = mix
        middle = (ctx_ref[0, here, :].astype(F32) * mix).astype(BF)
        mid_ref[here, :] = middle
        two_ref[pl.ds(at + TAPS, TAPS), :] = (
            ctx_ref[4, here, :].astype(F32) * middle.astype(F32)
        ).astype(BF)
        gtwo_ref[here, :] = (
            cot_ref[here, :].astype(F32) * ctx_ref[3, here, :].astype(F32)
        ).astype(BF)
        return carry

    lax.fori_loop(0, SLABS, first_pass, 0)
    lane_group = iota((TAPS, WIDTH), 1) // PER_GROUP

    def second_pass(slab, carry):
        at = pl.multiple_of(slab * TAPS, TAPS)
        here = pl.ds(at, TAPS)
        anchor = origin + at
        keep_fore = forward_mask(anchor, lengths_ref)
        keep_back = backward_mask(anchor, TAPS, lengths_ref)
        fore = one_hot(keep_fore)
        back = one_hot(keep_back)
        past = two_ref[pl.ds(at, SPAN), :]
        later = gtwo_ref[pl.ds(at, SPAN), :]
        fore_tiles = jnp.concatenate(
            [fore_tile_ref[g * TAPS : (g + 1) * TAPS, :] * fore for g in range(GROUPS)], axis=0
        )
        long_mix = by_group(jnp.dot(fore_tiles, past, preferred_element_type=F32), TAPS)
        back_tiles = jnp.concatenate(
            [back_tile_ref[g * TAPS : (g + 1) * TAPS, :] * back for g in range(GROUPS)], axis=0
        )
        grad_inner = by_group(jnp.dot(back_tiles, later, preferred_element_type=F32), TAPS)
        cot = cot_ref[here, :].astype(F32)
        grads_ref[here, 3 * WIDTH : 4 * WIDTH] = (cot * long_mix).astype(BF)
        grads_ref[here, 4 * WIDTH : 5 * WIDTH] = (
            grad_inner * mid_ref[here, :].astype(F32)
        ).astype(BF)
        grad_middle = grad_inner * ctx_ref[4, here, :].astype(F32)
        mix = mix_ref[here, :]
        grads_ref[here, 0:WIDTH] = (grad_middle * mix).astype(BF)
        grad_one = (grad_middle * ctx_ref[0, here, :].astype(F32)).astype(BF).astype(F32)
        gone_ref[here, :] = grad_one
        window = one_ref[pl.ds(at, TAPS + 8), :]
        targets = anchor + iota((TAPS, WIDTH), 0)
        reach = targets - starts_of(targets, lengths_ref)
        for lag in range(SHORT):
            source = window[8:] if lag == 0 else pltpu.roll(window, lag, 0)[8:]
            terms = jnp.where(reach >= lag, source * grad_one, 0.0)
            short_ref[lag : lag + 1, :] += jnp.sum(terms, axis=0, keepdims=True)
        now = later[0:TAPS]
        split = jnp.concatenate(
            [now * one_hot(lane_group == g) for g in range(GROUPS)], axis=0
        )
        grid = lax.dot_general(
            split, past, (((1,), (1,)), ((), ())), preferred_element_type=F32
        )
        for g in range(GROUPS):
            rows = slice(g * TAPS, (g + 1) * TAPS)
            grid_ref[rows, :] += jnp.where(keep_fore, grid[rows], 0.0)
        return carry

    lax.fori_loop(0, SLABS, second_pass, 0)

    def third_pass(slab, carry):
        at = pl.multiple_of(slab * TAPS, TAPS)
        here = pl.ds(at, TAPS)
        window = gone_ref[pl.ds(at, TAPS + 8), :]
        rows = origin + at + iota((TAPS, WIDTH), 0)
        total = jnp.zeros((TAPS, WIDTH), F32)
        for lag in range(SHORT):
            later = window if lag == 0 else pltpu.roll(window, TAPS + 8 - lag, 0)
            keep = rows >= starts_of(rows + lag, lengths_ref)
            total = total + jnp.where(
                keep, later[0:TAPS] * weights[lag : lag + 1, :], 0.0
            )
        grad_inner = total.astype(BF).astype(F32)
        grads_ref[here, WIDTH : 2 * WIDTH] = (
            grad_inner * ctx_ref[2, here, :].astype(F32)
        ).astype(BF)
        grads_ref[here, 2 * WIDTH : 3 * WIDTH] = (
            grad_inner * ctx_ref[1, here, :].astype(F32)
        ).astype(BF)
        return carry

    lax.fori_loop(0, SLABS, third_pass, 0)
    for step in range(PLANES):
        packed = jnp.dot(
            pick_ref[step * cap : (step + 1) * cap, :],
            grads_ref[...],
            preferred_element_type=F32,
        ).astype(BF)
        for stream in range(STREAMS):
            outs[step][stream] = packed[:, stream * WIDTH : (stream + 1) * WIDTH]
    for group in range(GROUPS):
        total = jnp.zeros((8, SPAN), F32)
        for block in range(TAPS // 8):
            first = group * TAPS + block * 8
            piece = grid_ref[first : first + 8, :]
            piece = jnp.where(in_band(block), piece, 0.0)
            total = total + (piece if block == 0 else pltpu.roll(piece, SPAN - 8 * block, 1))
        line = total[0:1]
        for row in range(1, 8):
            line = line + pltpu.roll(total, SPAN - row, 1)[row : row + 1]
        long_ref[group : group + 1, :] = line


def in_band(block):
    lag = block * 8 + iota((8, SPAN), 0) + TAPS - iota((8, SPAN), 1)
    return (lag >= 0) & (lag < TAPS)


def operators(cap, here, lengths, spot_col, cot, weights, fore_base, back_base, ctx, ahead, behind):
    dense = PLANE_ROWS * WIDTH
    return call(
        functools.partial(operator_kernel, cap),
        tuple(jax.ShapeDtypeStruct((STREAMS, cap, WIDTH), BF) for _ in range(PLANES))
        + (
            jax.ShapeDtypeStruct((GROUPS, SPAN), F32),
            jax.ShapeDtypeStruct((8, WIDTH), F32),
        ),
        n_in_smem=2,
        n_in=8,
        scratch=[
            pltpu.VMEM((PLANE_ROWS + 8, WIDTH), F32),
            pltpu.VMEM((PLANE_ROWS, WIDTH), F32),
            pltpu.VMEM((PLANE_ROWS, WIDTH), BF),
            pltpu.VMEM((PLANE_ROWS + TAPS, WIDTH), BF),
            pltpu.VMEM((PLANE_ROWS + TAPS, WIDTH), BF),
            pltpu.VMEM((PLANE_ROWS + 8, WIDTH), F32),
            pltpu.VMEM((GROUPS * TAPS, SPAN), BF),
            pltpu.VMEM((GROUPS * TAPS, SPAN), BF),
            pltpu.VMEM((GROUPS * TAPS, SPAN), F32),
            pltpu.VMEM((PLANE_ROWS, STREAMS * WIDTH), BF),
            pltpu.VMEM((PLANES * cap, PLANE_ROWS), BF),
        ],
        flops=2 * dense * (PLANES * cap * STREAMS + 3 * GROUPS * SPAN),
        bytes_accessed=6 * 2**20,
    )(here, lengths, spot_col, cot, weights, fore_base, back_base, ctx, ahead, behind)


def around(value, step):
    return lax.ppermute(value, "z", [(i, (i + step) % PLANES) for i in range(PLANES)])


def onward(value, step):
    pairs = [(i, i + step) for i in range(PLANES) if 0 <= i + step < PLANES]
    return lax.ppermute(value, "z", pairs)


def swap_in_plane(value):
    return lax.all_to_all(value, IN_PLANE, 0, 0, tiled=True)


def after_plan(cap, here, lengths, plan, code_row, code_col, se_filter, mr_filter, grad_out, rows_a, loaded):
    quarter = lax.axis_index("y")
    groups = CHUNKS * GROUPS
    spot_row, spot_col = receiver_spots(here, plan)
    cot_parts = jnp.transpose(
        grad_out.reshape(grad_out.shape[0], QUARTERS, CHUNKS * WIDTH), (1, 0, 2)
    )
    cot = lax.all_to_all(cot_parts, "y", 0, 0, tiled=True).reshape(PLANE_ROWS, CHUNKS * WIDTH)
    short_taps = lax.dynamic_slice_in_dim(se_filter, quarter * groups, groups, 1)
    short_taps = jnp.repeat(short_taps.astype(F32), PER_GROUP, axis=1)
    short_taps = jnp.concatenate([short_taps, jnp.zeros((1, CHUNKS * WIDTH), F32)], axis=0)
    taps = lax.dynamic_slice_in_dim(mr_filter, quarter * groups, groups, 1)
    taps = jnp.transpose(taps.astype(F32))
    fore_base = jnp.pad(taps[:, ::-1], ((0, 0), (1, TAPS - 1)))
    back_base = jnp.pad(taps, ((0, 0), (0, TAPS)))

    rows = [rows_a]
    for chunk in range(1, CHUNKS):
        rows.append(swap_in_plane(split_channels(loaded, chunk)))
    long_parts, short_parts, back = [], [], []
    for chunk in range(CHUNKS):
        lanes = slice(chunk * WIDTH, (chunk + 1) * WIDTH)
        mine = slice(chunk * GROUPS, (chunk + 1) * GROUPS)
        sent = pack(cap, here, rows[chunk], code_row)
        parcels = [sent[0]] + [around(sent[s], s) for s in range(1, PLANES)]
        ctx, ahead, behind = context(
            cap, here, lengths, spot_row, cot[:, lanes], short_taps[:, lanes],
            back_base[mine], parcels,
        )
        made = operators(
            cap, here, lengths, spot_col, cot[:, lanes], short_taps[:, lanes],
            fore_base[mine], back_base[mine], ctx, onward(ahead, 1), onward(behind, -1),
        )
        long_parts.append(made[PLANES])
        short_parts.append(made[PLANES + 1])
        returned = [made[0]] + [around(made[s], -s) for s in range(1, PLANES)]
        home = unpack(cap, here, code_col, returned)
        back.append(swap_in_plane(home))
    restored = merge_channels(back)

    long_here = jnp.concatenate(long_parts, axis=0)[:, 1 : TAPS + 1][:, ::-1]
    short_here = jnp.concatenate(short_parts, axis=1).reshape(8, groups, PER_GROUP).sum(axis=2)
    together = jnp.concatenate(
        [long_here, jnp.pad(short_here, ((0, 0), (0, TAPS - groups)))], axis=0
    )
    spread = jnp.broadcast_to(together[None], (PEERS,) + together.shape)
    gathered = lax.all_to_all(spread, ("z", "y"), 0, 0, tiled=True)
    summed = gathered.reshape(PLANES, QUARTERS, groups + 8, TAPS).sum(axis=0)
    scale = (PLANES * PLANE_ROWS * PER_GROUP) ** -0.5
    summed = summed * scale
    long_total = jnp.transpose(summed[:, :groups, :], (2, 0, 1)).reshape(TAPS, QUARTERS * groups)
    short_total = jnp.transpose(summed[:, groups : groups + SHORT, :groups], (1, 0, 2)).reshape(
        SHORT, QUARTERS * groups
    )
    return restored, short_total, long_total


def on_device(loaded, row_plan, lengths, se_filter, mr_filter, grad_out):
    here = lax.axis_index("z").astype(I32).reshape(1)
    devices = PLANES * PEERS
    plan = lax.all_to_all(
        jnp.broadcast_to(row_plan[None], (devices, OWN_ROWS)), ALL_AXES, 0, 0, tiled=True
    ).reshape(PLANES, PLANE_ROWS)
    rows_a = swap_in_plane(split_channels(loaded, 0))
    code_row, code_col, most = sender_codes(here, plan)
    args = (
        here, lengths, plan, code_row, code_col, se_filter, mr_filter, grad_out, rows_a, loaded,
    )
    return lax.cond(
        most[0, 0] <= LEAN_CAP,
        functools.partial(after_plan, LEAN_CAP),
        functools.partial(after_plan, FULL_CAP),
        *args,
    )


def solution(mesh):
    grid = Mesh(mesh.devices.reshape(PLANES, QUARTERS, 4, 2), ALL_AXES)
    placed = (
        P(None, ALL_AXES, None),
        P(ALL_AXES),
        P(),
        P(None, ("x", "c")),
        P(None, ("x", "c")),
        P(("z", "y"), ("x", "c")),
    )
    return jax.shard_map(
        on_device,
        mesh=grid,
        in_specs=placed,
        out_specs=(P(None, ALL_AXES, None), P(None, ("x", "c")), P(None, ("x", "c"))),
        check_vma=False,
    )
```

```python
import functools

import jax
import jax.numpy as jnp
from jax import lax
from jax.experimental import pallas as pl
from jax.experimental.pallas import tpu as pltpu
from jax.sharding import Mesh, PartitionSpec as P

PLANES = 8
QUARTERS = 4
PEERS = 32
PLANE_ROWS = 1024
WIDTH = 128
CHUNKS = 2
PER_GROUP = 16
GROUPS = WIDTH // PER_GROUP
STREAMS = 5
OWN_ROWS = 32
DATA_ROWS = STREAMS * OWN_ROWS
NOTE_ROWS = 16
TAPS = 128
SHORT = 7
SPAN = 2 * TAPS
SLABS = PLANE_ROWS // TAPS
FULL_CAP = 256
LEAN_CAP = 160
RING_B = False
RING_BACK_A = False
ALL_AXES = ("z", "y", "x", "c")
IN_PLANE = ("y", "x", "c")
BF = jnp.bfloat16
F32 = jnp.float32
I32 = jnp.int32


def iota(shape, dim):
    return lax.broadcasted_iota(I32, shape, dim)


def one_hot(mask):
    return jnp.where(mask, 1.0, 0.0).astype(BF)


def call(body, out_shape, n_in_smem=0, n_in=0, n_any=0, scratch=(), flops=0, bytes_accessed=0):
    smem = [pl.BlockSpec(memory_space=pltpu.SMEM)] * n_in_smem
    vmem = [pl.BlockSpec(memory_space=pltpu.VMEM)] * n_in
    outs = jax.tree.map(lambda s: pl.BlockSpec(memory_space=pltpu.VMEM), out_shape)
    return pl.pallas_call(
        body,
        out_shape=out_shape,
        in_specs=smem + vmem + [pl.BlockSpec(memory_space=pl.ANY)] * n_any,
        out_specs=outs,
        scratch_shapes=list(scratch),
        compiler_params=pltpu.CompilerParams(vmem_limit_bytes=48 * 2**20),
        cost_estimate=pl.CostEstimate(
            flops=flops, bytes_accessed=bytes_accessed, transcendentals=0
        ),
    )


def peer_column(peer, chunk):
    quarter, column = peer // 8, peer % 8
    return (column * QUARTERS + quarter) * CHUNKS * WIDTH + chunk * WIDTH


def split_kernel(chunk, loaded_ref, note_ref, out_ref):
    for peer in range(PEERS):
        first = peer_column(peer, chunk)
        for stream in range(STREAMS):
            out_ref[peer, stream * OWN_ROWS : (stream + 1) * OWN_ROWS, :] = loaded_ref[
                stream, :, first : first + WIDTH
            ]
        out_ref[peer, DATA_ROWS:, :] = note_ref[...]


def split_channels(loaded, chunk, note):
    return call(
        functools.partial(split_kernel, chunk),
        jax.ShapeDtypeStruct((PEERS, DATA_ROWS + NOTE_ROWS, WIDTH), BF),
        n_in=2,
        bytes_accessed=4 * 2**20,
    )(loaded, note)


def write_note(numbers):
    high, low = numbers // 128, numbers % 128
    digits = jnp.concatenate([high, low], axis=0).astype(BF)
    return jnp.pad(digits, ((0, NOTE_ROWS - digits.shape[0]), (0, WIDTH - digits.shape[1])))


def read_note(notes, rows, width):
    high = notes[:, DATA_ROWS : DATA_ROWS + rows, :width].astype(I32)
    low = notes[:, DATA_ROWS + rows : DATA_ROWS + 2 * rows, :width].astype(I32)
    return high * 128 + low


def merge_kernel(*refs):
    out_ref = refs[-1]
    for chunk in range(CHUNKS):
        for peer in range(PEERS):
            first = peer_column(peer, chunk)
            for stream in range(STREAMS):
                out_ref[stream, :, first : first + WIDTH] = refs[chunk][
                    peer, stream * OWN_ROWS : (stream + 1) * OWN_ROWS, :
                ]


def merge_channels(parts):
    return call(
        merge_kernel,
        jax.ShapeDtypeStruct((STREAMS, OWN_ROWS, PEERS * CHUNKS * WIDTH), BF),
        n_in=CHUNKS,
        bytes_accessed=6 * 2**20,
    )(*parts)


def pass_on_kernel(*refs):
    pass


def pass_on(values, after):
    anywhere = pl.BlockSpec(memory_space=pl.ANY)
    return pl.pallas_call(
        pass_on_kernel,
        out_shape=tuple(jax.ShapeDtypeStruct(v.shape, v.dtype) for v in values),
        in_specs=[anywhere] * (len(values) + len(after)),
        out_specs=tuple(anywhere for _ in values),
        input_output_aliases={i: i for i in range(len(values))},
    )(*values, *after)


def before_matrix():
    shape = (PLANE_ROWS, PLANE_ROWS)
    return one_hot(iota(shape, 0) < iota(shape, 1))


def sender_kernel(mine_ref, code_row_ref, code_col_ref):
    shape = (PLANES, PLANE_ROWS)
    target = mine_ref[...] // PLANE_ROWS
    match = target == iota(shape, 0)
    earlier = jnp.dot(one_hot(match), before_matrix(), preferred_element_type=F32)
    rank = jnp.sum(jnp.where(match, earlier, 0.0), axis=0, keepdims=True)
    code = target * FULL_CAP + rank.astype(I32)
    code_row_ref[...] = code
    tall = jnp.broadcast_to(code.astype(F32), (WIDTH, PLANE_ROWS))
    code_col_ref[...] = jnp.transpose(tall).astype(I32)


def sender_codes(mine):
    return call(
        sender_kernel,
        (
            jax.ShapeDtypeStruct((1, PLANE_ROWS), I32),
            jax.ShapeDtypeStruct((PLANE_ROWS, WIDTH), I32),
        ),
        n_in=1,
        flops=2 * 16 * 2**20,
        bytes_accessed=2**20,
    )(mine)


def receiver_kernel(here_ref, plan_ref, spot_row_ref, spot_col_ref, most_ref):
    plane = here_ref[0]
    every = plan_ref[...]
    goals = every // PLANE_ROWS
    arriving = goals == plane
    ranks = jnp.dot(one_hot(arriving), before_matrix(), preferred_element_type=F32)
    ranks = jnp.where(arriving, ranks.astype(I32), -1)
    local = every % PLANE_ROWS
    rows = iota((FULL_CAP, PLANE_ROWS), 0)
    kind = iota((8, PLANE_ROWS), 0)
    for step in range(PLANES):
        source = (plane + PLANES - step) % PLANES
        held = one_hot(rows == ranks[step : step + 1, :])
        spot = local[step : step + 1, :]
        parts = jnp.where(kind == 0, spot // 32, jnp.where(kind == 1, spot % 32, 1))
        read = lax.dot_general(
            parts.astype(F32).astype(BF),
            held,
            (((1,), (1,)), ((), ())),
            preferred_element_type=F32,
        )
        value = read[0:1] * 32.0 + read[1:2] + (read[2:3] - 1.0) * 4096.0
        spot_row_ref[pl.ds(source, 1), :] = value.astype(I32)
        tall = jnp.broadcast_to(value, (WIDTH, FULL_CAP))
        spot_col_ref[source] = jnp.transpose(tall).astype(I32)
    most = jnp.zeros((PLANES, 1), I32)
    for goal in range(PLANES):
        found = jnp.sum((goals == goal).astype(I32), axis=1, keepdims=True)
        most = jnp.maximum(most, found)
    most_ref[...] = jnp.broadcast_to(jnp.max(most, axis=0, keepdims=True), (8, 128))


def receiver_spots(here, plan):
    return call(
        receiver_kernel,
        (
            jax.ShapeDtypeStruct((PLANES, FULL_CAP), I32),
            jax.ShapeDtypeStruct((PLANES, FULL_CAP, WIDTH), I32),
            jax.ShapeDtypeStruct((8, 128), I32),
        ),
        n_in_smem=1,
        n_in=1,
        flops=2 * 64 * 2**20,
        bytes_accessed=2 * 2**20,
    )(here, plan)


def parcels_shape(cap, ring):
    if ring:
        return tuple(jax.ShapeDtypeStruct((STREAMS, cap, WIDTH), BF) for _ in range(PLANES))
    return (jax.ShapeDtypeStruct((PLANES, STREAMS, cap, WIDTH), BF),)


def take_parcels(refs, ring):
    count = PLANES if ring else 1
    return (refs[:PLANES] if ring else [refs[0].at[p] for p in range(PLANES)]), refs[count:]


def plane_at(plane, step, ring, way=1):
    return (plane + PLANES + way * step) % PLANES if ring else step


def pack_kernel(cap, ring, here_ref, rows_ref, code_ref, *rest):
    outs, (field_ref, pick_ref) = take_parcels(rest, ring)
    for stream in range(STREAMS):
        field_ref[:, stream * WIDTH : (stream + 1) * WIDTH] = rows_ref[
            :, stream * OWN_ROWS : (stream + 1) * OWN_ROWS, :
        ].reshape(PLANE_ROWS, WIDTH)
    code = code_ref[...]
    for step in range(PLANES):
        goal = plane_at(here_ref[0], step, ring)
        wanted = iota((cap, PLANE_ROWS), 0) + goal * FULL_CAP
        pick_ref[step * cap : (step + 1) * cap, :] = one_hot(wanted == code)
    for step in range(PLANES):
        packed = jnp.dot(
            pick_ref[step * cap : (step + 1) * cap, :],
            field_ref[...],
            preferred_element_type=F32,
        ).astype(BF)
        for stream in range(STREAMS):
            outs[step][stream] = packed[:, stream * WIDTH : (stream + 1) * WIDTH]


def pack(cap, ring, here, rows, code_row):
    return call(
        functools.partial(pack_kernel, cap, ring),
        parcels_shape(cap, ring),
        n_in_smem=1,
        n_in=2,
        scratch=[
            pltpu.VMEM((PLANE_ROWS, STREAMS * WIDTH), BF),
            pltpu.VMEM((PLANES * cap, PLANE_ROWS), BF),
        ],
        flops=2 * PLANES * cap * PLANE_ROWS * STREAMS * WIDTH,
        bytes_accessed=3 * 2**20,
    )(here, rows, code_row)


def unpack_kernel(cap, ring, here_ref, code_ref, *rest):
    parcels, (out_ref, field_ref, pick_ref) = take_parcels(rest, ring)
    code = code_ref[...]
    blocks = -(-cap // WIDTH)
    for step in range(PLANES):
        goal = plane_at(here_ref[0], step, ring)
        for stream in range(STREAMS):
            field_ref[
                step * cap : (step + 1) * cap, stream * WIDTH : (stream + 1) * WIDTH
            ] = parcels[step][stream]
        for block in range(blocks):
            first = block * WIDTH
            width = min(WIDTH, cap - first)
            wanted = iota((PLANE_ROWS, WIDTH), 1) + (goal * FULL_CAP + first)
            pick_ref[:, step * cap + first : step * cap + first + width] = one_hot(
                wanted == code
            )[:, :width]
    for part in range(4):
        rows = PLANE_ROWS // 4
        found = jnp.dot(
            pick_ref[part * rows : (part + 1) * rows, :],
            field_ref[...],
            preferred_element_type=F32,
        ).astype(BF)
        peers = rows // OWN_ROWS
        for stream in range(STREAMS):
            out_ref[
                part * peers : (part + 1) * peers,
                stream * OWN_ROWS : (stream + 1) * OWN_ROWS,
                :,
            ] = found[:, stream * WIDTH : (stream + 1) * WIDTH].reshape(
                peers, OWN_ROWS, WIDTH
            )


def unpack(cap, ring, here, code_col, parcels):
    return call(
        functools.partial(unpack_kernel, cap, ring),
        jax.ShapeDtypeStruct((PEERS, STREAMS * OWN_ROWS, WIDTH), BF),
        n_in_smem=1,
        n_in=1 + len(parcels),
        scratch=[
            pltpu.VMEM((PLANES * cap, STREAMS * WIDTH), BF),
            pltpu.VMEM((PLANE_ROWS, PLANES * cap), BF),
        ],
        flops=2 * PLANES * cap * PLANE_ROWS * STREAMS * WIDTH,
        bytes_accessed=3 * 2**20,
    )(here, code_col, *parcels)


def starts_of(rows, lengths_ref):
    first, second, third = lengths_ref[0], lengths_ref[1], lengths_ref[2]
    total = jnp.where(rows >= first, first, 0)
    total = total + jnp.where(rows >= first + second, second, 0)
    return total + jnp.where(rows >= first + second + third, third, 0)


def band(base_row, rows):
    wide = jnp.broadcast_to(base_row, (rows, SPAN))
    return pltpu.roll(wide, 0, 1, stride=1, stride_axis=0).astype(BF)


def forward_mask(anchor, lengths_ref):
    shape = (TAPS, SPAN)
    begin = starts_of(anchor + iota(shape, 0), lengths_ref)
    return anchor - TAPS + iota(shape, 1) >= begin


def backward_mask(anchor, rows, lengths_ref):
    shape = (rows, SPAN)
    begin = starts_of(anchor + iota(shape, 1), lengths_ref)
    return anchor + iota(shape, 0) >= begin


def by_group(stacked, rows):
    lane_group = iota((rows, WIDTH), 1) // PER_GROUP
    total = stacked[0:rows]
    for group in range(1, GROUPS):
        total = jnp.where(
            lane_group == group, stacked[group * rows : (group + 1) * rows], total
        )
    return total


def short_sum(window, weights, anchor, rows, lengths_ref):
    targets = anchor + iota((rows, WIDTH), 0)
    reach = targets - starts_of(targets, lengths_ref)
    total = jnp.zeros((rows, WIDTH), F32)
    for lag in range(SHORT):
        source = window[8:] if lag == 0 else pltpu.roll(window, lag, 0)[8:]
        total = total + jnp.where(reach >= lag, source * weights[lag : lag + 1, :], 0.0)
    return total


def context_kernel(
    cap, ring, here_ref, lengths_ref, spot_ref, cot_ref, se_ref, back_ref, *rest
):
    parcels, rest = take_parcels(rest, ring)
    ctx_ref, ahead_ref, behind_ref, field_ref, pick_ref = rest[1:]
    plane = here_ref[0]
    for step in range(PLANES):
        source = plane_at(plane, step, ring, -1)
        for stream in range(STREAMS):
            field_ref[
                step * cap : (step + 1) * cap, stream * WIDTH : (stream + 1) * WIDTH
            ] = parcels[step][stream]
        spot = spot_ref[pl.ds(source, 1), :][:, :cap]
        pick_ref[:, step * cap : (step + 1) * cap] = one_hot(
            iota((PLANE_ROWS, cap), 0) == spot
        )
    for part in range(4):
        rows = PLANE_ROWS // 4
        found = jnp.dot(
            pick_ref[part * rows : (part + 1) * rows, :],
            field_ref[...],
            preferred_element_type=F32,
        ).astype(BF)
        for stream in range(STREAMS):
            ctx_ref[stream, part * rows : (part + 1) * rows, :] = found[
                :, stream * WIDTH : (stream + 1) * WIDTH
            ]
    weights = se_ref[...]
    anchor = plane * PLANE_ROWS
    tail = PLANE_ROWS - TAPS
    low = tail - 16
    inner = (ctx_ref[1, low:, :].astype(F32) * ctx_ref[2, low:, :].astype(F32)).astype(BF)
    window = inner.astype(F32)[8:]
    mix = short_sum(window, weights, anchor + tail, TAPS, lengths_ref)
    middle = (ctx_ref[0, tail:, :].astype(F32) * mix).astype(BF)
    ahead_ref[0:TAPS, :] = (
        ctx_ref[4, tail:, :].astype(F32) * middle.astype(F32)
    ).astype(BF)
    ahead_ref[TAPS : TAPS + 16, :] = inner[TAPS:]
    grad_two = (
        cot_ref[0:SPAN, :].astype(F32) * ctx_ref[3, 0:SPAN, :].astype(F32)
    ).astype(BF)
    behind_ref[0:TAPS, :] = grad_two[0:TAPS]
    mask = backward_mask(anchor, 16, lengths_ref)
    tiles = []
    for group in range(GROUPS):
        tile = band(back_ref[group : group + 1, :], 16).astype(F32)
        tiles.append(jnp.where(mask, tile, 0.0).astype(BF))
    stacked = jnp.dot(
        jnp.concatenate(tiles, axis=0), grad_two, preferred_element_type=F32
    )
    grad_inner = by_group(stacked, 16)
    grad_middle = grad_inner * ctx_ref[4, 0:16, :].astype(F32)
    behind_ref[TAPS : TAPS + 16, :] = (
        grad_middle * ctx_ref[0, 0:16, :].astype(F32)
    ).astype(BF)


def context(cap, ring, here, lengths, spot_row, cot, weights, back_base, parcels, after):
    return call(
        functools.partial(context_kernel, cap, ring),
        (
            jax.ShapeDtypeStruct((STREAMS, PLANE_ROWS, WIDTH), BF),
            jax.ShapeDtypeStruct((TAPS + 16, WIDTH), BF),
            jax.ShapeDtypeStruct((TAPS + 16, WIDTH), BF),
        ),
        n_in_smem=2,
        n_in=4 + len(parcels),
        n_any=1,
        scratch=[
            pltpu.VMEM((PLANES * cap, STREAMS * WIDTH), BF),
            pltpu.VMEM((PLANE_ROWS, PLANES * cap), BF),
        ],
        flops=2 * PLANES * cap * PLANE_ROWS * STREAMS * WIDTH,
        bytes_accessed=3 * 2**20,
    )(here, lengths, spot_row, cot, weights, back_base, *parcels, after)


def operator_kernel(
    cap, ring, here_ref, lengths_ref, spot_ref, cot_ref, se_ref, fore_ref, back_ref,
    ctx_ref, ahead_ref, behind_ref, after_ref, *rest,
):
    outs, rest = take_parcels(rest, ring)
    (
        long_ref, short_ref, one_ref, mix_ref, mid_ref, two_ref, gtwo_ref, gone_ref,
        fore_tile_ref, back_tile_ref, grid_ref, grads_ref, pick_ref,
    ) = rest
    plane = here_ref[0]
    origin = plane * PLANE_ROWS
    weights = se_ref[...]
    for group in range(GROUPS):
        at = slice(group * TAPS, (group + 1) * TAPS)
        fore_tile_ref[at, :] = band(fore_ref[group : group + 1, :], TAPS)
        back_tile_ref[at, :] = band(back_ref[group : group + 1, :], TAPS)
    for step in range(PLANES):
        source = plane_at(plane, step, ring, -1)
        for block in range(PLANE_ROWS // WIDTH):
            spots = spot_ref[source, :cap, :]
            pick_ref[
                step * cap : (step + 1) * cap, block * WIDTH : (block + 1) * WIDTH
            ] = one_hot(iota((cap, WIDTH), 1) + block * WIDTH == spots)
    one_ref[0:8, :] = ahead_ref[TAPS : TAPS + 16, :].astype(F32)[8:]
    two_ref[0:TAPS, :] = ahead_ref[0:TAPS, :]
    gtwo_ref[PLANE_ROWS:, :] = behind_ref[0:TAPS, :]
    gone_ref[PLANE_ROWS:, :] = behind_ref[TAPS : TAPS + 16, :].astype(F32)[0:8]
    grid_ref[...] = jnp.zeros_like(grid_ref)
    short_ref[...] = jnp.zeros_like(short_ref)

    def first_pass(slab, carry):
        at = pl.multiple_of(slab * TAPS, TAPS)
        here = pl.ds(at, TAPS)
        inner = (ctx_ref[1, here, :].astype(F32) * ctx_ref[2, here, :].astype(F32)).astype(BF)
        one_ref[pl.ds(at + 8, TAPS), :] = inner.astype(F32)
        window = one_ref[pl.ds(at, TAPS + 8), :]
        mix = short_sum(window, weights, origin + at, TAPS, lengths_ref)
        mix_ref[here, :] = mix
        middle = (ctx_ref[0, here, :].astype(F32) * mix).astype(BF)
        mid_ref[here, :] = middle
        two_ref[pl.ds(at + TAPS, TAPS), :] = (
            ctx_ref[4, here, :].astype(F32) * middle.astype(F32)
        ).astype(BF)
        gtwo_ref[here, :] = (
            cot_ref[here, :].astype(F32) * ctx_ref[3, here, :].astype(F32)
        ).astype(BF)
        return carry

    lax.fori_loop(0, SLABS, first_pass, 0)
    lane_group = iota((TAPS, WIDTH), 1) // PER_GROUP

    def second_pass(slab, carry):
        at = pl.multiple_of(slab * TAPS, TAPS)
        here = pl.ds(at, TAPS)
        anchor = origin + at
        keep_fore = forward_mask(anchor, lengths_ref)
        keep_back = backward_mask(anchor, TAPS, lengths_ref)
        fore = one_hot(keep_fore)
        back = one_hot(keep_back)
        past = two_ref[pl.ds(at, SPAN), :]
        later = gtwo_ref[pl.ds(at, SPAN), :]
        fore_tiles = jnp.concatenate(
            [fore_tile_ref[g * TAPS : (g + 1) * TAPS, :] * fore for g in range(GROUPS)], axis=0
        )
        long_mix = by_group(jnp.dot(fore_tiles, past, preferred_element_type=F32), TAPS)
        back_tiles = jnp.concatenate(
            [back_tile_ref[g * TAPS : (g + 1) * TAPS, :] * back for g in range(GROUPS)], axis=0
        )
        grad_inner = by_group(jnp.dot(back_tiles, later, preferred_element_type=F32), TAPS)
        cot = cot_ref[here, :].astype(F32)
        grads_ref[here, 3 * WIDTH : 4 * WIDTH] = (cot * long_mix).astype(BF)
        grads_ref[here, 4 * WIDTH : 5 * WIDTH] = (
            grad_inner * mid_ref[here, :].astype(F32)
        ).astype(BF)
        grad_middle = grad_inner * ctx_ref[4, here, :].astype(F32)
        mix = mix_ref[here, :]
        grads_ref[here, 0:WIDTH] = (grad_middle * mix).astype(BF)
        grad_one = (grad_middle * ctx_ref[0, here, :].astype(F32)).astype(BF).astype(F32)
        gone_ref[here, :] = grad_one
        window = one_ref[pl.ds(at, TAPS + 8), :]
        targets = anchor + iota((TAPS, WIDTH), 0)
        reach = targets - starts_of(targets, lengths_ref)
        for lag in range(SHORT):
            source = window[8:] if lag == 0 else pltpu.roll(window, lag, 0)[8:]
            terms = jnp.where(reach >= lag, source * grad_one, 0.0)
            short_ref[lag : lag + 1, :] += jnp.sum(terms, axis=0, keepdims=True)
        now = later[0:TAPS]
        split = jnp.concatenate(
            [now * one_hot(lane_group == g) for g in range(GROUPS)], axis=0
        )
        grid = lax.dot_general(
            split, past, (((1,), (1,)), ((), ())), preferred_element_type=F32
        )
        for g in range(GROUPS):
            rows = slice(g * TAPS, (g + 1) * TAPS)
            grid_ref[rows, :] += jnp.where(keep_fore, grid[rows], 0.0)
        return carry

    lax.fori_loop(0, SLABS, second_pass, 0)

    def third_pass(slab, carry):
        at = pl.multiple_of(slab * TAPS, TAPS)
        here = pl.ds(at, TAPS)
        window = gone_ref[pl.ds(at, TAPS + 8), :]
        rows = origin + at + iota((TAPS, WIDTH), 0)
        total = jnp.zeros((TAPS, WIDTH), F32)
        for lag in range(SHORT):
            later = window if lag == 0 else pltpu.roll(window, TAPS + 8 - lag, 0)
            keep = rows >= starts_of(rows + lag, lengths_ref)
            total = total + jnp.where(
                keep, later[0:TAPS] * weights[lag : lag + 1, :], 0.0
            )
        grad_inner = total.astype(BF).astype(F32)
        grads_ref[here, WIDTH : 2 * WIDTH] = (
            grad_inner * ctx_ref[2, here, :].astype(F32)
        ).astype(BF)
        grads_ref[here, 2 * WIDTH : 3 * WIDTH] = (
            grad_inner * ctx_ref[1, here, :].astype(F32)
        ).astype(BF)
        return carry

    lax.fori_loop(0, SLABS, third_pass, 0)
    for step in range(PLANES):
        packed = jnp.dot(
            pick_ref[step * cap : (step + 1) * cap, :],
            grads_ref[...],
            preferred_element_type=F32,
        ).astype(BF)
        for stream in range(STREAMS):
            outs[step][stream] = packed[:, stream * WIDTH : (stream + 1) * WIDTH]
    for group in range(GROUPS):
        total = jnp.zeros((8, SPAN), F32)
        for block in range(TAPS // 8):
            first = group * TAPS + block * 8
            piece = grid_ref[first : first + 8, :]
            piece = jnp.where(in_band(block), piece, 0.0)
            total = total + (piece if block == 0 else pltpu.roll(piece, SPAN - 8 * block, 1))
        line = total[0:1]
        for row in range(1, 8):
            line = line + pltpu.roll(total, SPAN - row, 1)[row : row + 1]
        long_ref[group : group + 1, :] = line


def in_band(block):
    lag = block * 8 + iota((8, SPAN), 0) + TAPS - iota((8, SPAN), 1)
    return (lag >= 0) & (lag < TAPS)


def operators(
    cap, ring, here, lengths, spot_col, cot, weights, fore_base, back_base, ctx, ahead, behind, after
):
    dense = PLANE_ROWS * WIDTH
    return call(
        functools.partial(operator_kernel, cap, ring),
        parcels_shape(cap, ring)
        + (
            jax.ShapeDtypeStruct((GROUPS, SPAN), F32),
            jax.ShapeDtypeStruct((8, WIDTH), F32),
        ),
        n_in_smem=2,
        n_in=8,
        n_any=1,
        scratch=[
            pltpu.VMEM((PLANE_ROWS + 8, WIDTH), F32),
            pltpu.VMEM((PLANE_ROWS, WIDTH), F32),
            pltpu.VMEM((PLANE_ROWS, WIDTH), BF),
            pltpu.VMEM((PLANE_ROWS + TAPS, WIDTH), BF),
            pltpu.VMEM((PLANE_ROWS + TAPS, WIDTH), BF),
            pltpu.VMEM((PLANE_ROWS + 8, WIDTH), F32),
            pltpu.VMEM((GROUPS * TAPS, SPAN), BF),
            pltpu.VMEM((GROUPS * TAPS, SPAN), BF),
            pltpu.VMEM((GROUPS * TAPS, SPAN), F32),
            pltpu.VMEM((PLANE_ROWS, STREAMS * WIDTH), BF),
            pltpu.VMEM((PLANES * cap, PLANE_ROWS), BF),
        ],
        flops=2 * dense * (PLANES * cap * STREAMS + 3 * GROUPS * SPAN),
        bytes_accessed=6 * 2**20,
    )(here, lengths, spot_col, cot, weights, fore_base, back_base, ctx, ahead, behind, after)


def around(value, step, axis, length):
    return lax.ppermute(value, axis, [(i, (i + step) % length) for i in range(length)])


def onward(value, step):
    pairs = [(i, i + step) for i in range(PLANES) if 0 <= i + step < PLANES]
    return lax.ppermute(value, "z", pairs)


def swap_in_plane(value):
    return lax.all_to_all(value, IN_PLANE, 0, 0, tiled=True)


def in_order(part, axis, length, pieces=None):
    at = lax.axis_index(axis)
    parts = [pieces[s] if pieces else part for s in range(length)]
    parts = parts[:1] + [around(parts[s], s, axis, length) for s in range(1, length)]
    turned = jnp.concatenate(
        [parts[(length - 1 - k) % length] for k in range(2 * length - 1)], axis=0
    )
    rows = parts[0].shape[0]
    return lax.dynamic_slice_in_dim(turned, (length - 1 - at) * rows, length * rows, 0)


def cotangent_of_plane(grad_out):
    quarter = lax.axis_index("y")
    width = CHUNKS * WIDTH
    pieces = [
        lax.dynamic_slice_in_dim(grad_out, ((quarter + s) % QUARTERS) * width, width, 1)
        for s in range(QUARTERS)
    ]
    return in_order(None, "y", QUARTERS, pieces)


def filters_of_device(se_filter, mr_filter):
    quarter = lax.axis_index("y")
    groups = CHUNKS * GROUPS
    short_taps = lax.dynamic_slice_in_dim(se_filter, quarter * groups, groups, 1)
    short_taps = jnp.repeat(short_taps.astype(F32), PER_GROUP, axis=1)
    short_taps = jnp.concatenate([short_taps, jnp.zeros((1, CHUNKS * WIDTH), F32)], axis=0)
    taps = lax.dynamic_slice_in_dim(mr_filter, quarter * groups, groups, 1)
    taps = jnp.transpose(taps.astype(F32))
    fore_base = jnp.pad(taps[:, ::-1], ((0, 0), (1, TAPS - 1)))
    back_base = jnp.pad(taps, ((0, 0), (0, TAPS)))
    return short_taps, fore_base, back_base


def filter_totals(long_parts, short_parts):
    groups = CHUNKS * GROUPS
    long_here = jnp.concatenate(long_parts, axis=0)[:, 1 : TAPS + 1][:, ::-1]
    short_here = jnp.concatenate(short_parts, axis=1).reshape(8, groups, PER_GROUP).sum(axis=2)
    together = jnp.concatenate(
        [long_here, jnp.pad(short_here, ((0, 0), (0, TAPS - groups)))], axis=0
    )
    every_plane = in_order(together[None], "z", PLANES)
    summed = in_order(jnp.sum(every_plane, axis=0)[None], "y", QUARTERS)
    summed = summed * (PLANES * PLANE_ROWS * PER_GROUP) ** -0.5
    long_total = jnp.transpose(summed[:, :groups, :], (2, 0, 1)).reshape(TAPS, QUARTERS * groups)
    short_total = jnp.transpose(summed[:, groups : groups + SHORT, :groups], (1, 0, 2)).reshape(
        SHORT, QUARTERS * groups
    )
    return short_total, long_total


def exchange_and_operate(cap, here, lengths, codes, spots, cot, filters, rows):
    short_taps, fore_base, back_base = filters
    lanes = [slice(c * WIDTH, (c + 1) * WIDTH) for c in range(CHUNKS)]
    mine = [slice(c * GROUPS, (c + 1) * GROUPS) for c in range(CHUNKS)]

    def exchange(ring, parts, way):
        if not ring:
            return [lax.all_to_all(parts[0], "z", 0, 0, tiled=True)]
        moved = {s: around(parts[s], way * s, "z", PLANES) for s in (4, 3, 5, 2, 6, 1, 7)}
        return [parts[0]] + [moved[s] for s in range(1, PLANES)]

    def arrive(ring, chunk, parcels, after):
        return context(
            cap, ring, here, lengths, spots[0], cot[:, lanes[chunk]],
            short_taps[:, lanes[chunk]], back_base[mine[chunk]], parcels, after,
        )

    def operate(ring, chunk, after, ctx, ahead, behind):
        *parcels, longs, shorts = operators(
            cap, ring, here, lengths, spots[1], cot[:, lanes[chunk]],
            short_taps[:, lanes[chunk]], fore_base[mine[chunk]], back_base[mine[chunk]],
            ctx, onward(ahead, 1), onward(behind, -1), after,
        )
        return parcels, longs, shorts

    sent_a = pack(cap, True, here, rows[0], codes[0])
    parcels_a = exchange(True, sent_a, 1)
    sent_b = pack(cap, RING_B, here, rows[1], codes[0])
    parcels_b = exchange(RING_B, sent_b, 1)
    made_a, long_a, short_a = operate(
        RING_BACK_A, 0, sent_b[0], *arrive(True, 0, parcels_a, sent_b[0])
    )
    returned_a = exchange(RING_BACK_A, made_a, -1)
    made_b, long_b, short_b = operate(
        True, 1, made_a[0], *arrive(RING_B, 1, parcels_b, made_a[0])
    )
    leaving_b = pass_on(made_b[1:], returned_a[1:] if RING_BACK_A else returned_a)
    returned_b = exchange(True, [made_b[0], *leaving_b], -1)
    back_a = swap_in_plane(unpack(cap, RING_BACK_A, here, codes[1], returned_a))
    back_b = swap_in_plane(unpack(cap, True, here, codes[1], returned_b))
    totals = filter_totals([long_a, long_b], [short_a, short_b])
    return (back_a, back_b), totals


def on_device(loaded, row_plan, lengths, se_filter, mr_filter, grad_out):
    here = lax.axis_index("z").astype(I32).reshape(1)
    own = row_plan.reshape(1, OWN_ROWS)
    rows_a = swap_in_plane(split_channels(loaded, 0, write_note(own)))
    along = [own] + [around(own, s, "z", PLANES) for s in range(1, PLANES)]
    along = jnp.concatenate(along, axis=1).reshape(2, WIDTH)
    rows_b = swap_in_plane(split_channels(loaded, 1, write_note(along)))
    cot = cotangent_of_plane(grad_out)
    filters = filters_of_device(se_filter, mr_filter)
    mine = read_note(rows_a, 1, OWN_ROWS).reshape(1, PLANE_ROWS)
    codes = sender_codes(mine)
    plan = read_note(rows_b, 2, WIDTH).reshape(PEERS, PLANES, OWN_ROWS)
    plan = jnp.transpose(plan, (1, 0, 2)).reshape(PLANES, PLANE_ROWS)
    spot_row, spot_col, most = receiver_spots(here, plan)
    given = (here, lengths, codes, (spot_row, spot_col), cot, filters, (rows_a, rows_b))
    lean = exchange_and_operate(LEAN_CAP, *given)

    def finish(lean, given):
        return (merge_channels(lean[0]),) + lean[1]

    def again(lean, given):
        return finish(exchange_and_operate(FULL_CAP, *given), given)

    return lax.cond(most[0, 0] <= LEAN_CAP, finish, again, lean, given)


def solution(mesh):
    grid = Mesh(mesh.devices.reshape(PLANES, QUARTERS, 4, 2), ALL_AXES)
    placed = (
        P(None, ALL_AXES, None),
        P(ALL_AXES),
        P(),
        P(None, ("x", "c")),
        P(None, ("x", "c")),
        P(("z", "y"), ("x", "c")),
    )
    return jax.shard_map(
        on_device,
        mesh=grid,
        in_specs=placed,
        out_specs=(P(None, ALL_AXES, None), P(None, ("x", "c")), P(None, ("x", "c"))),
        check_vma=False,
    )
```

```python
import functools

import jax
import jax.numpy as jnp
from jax import lax
from jax.experimental import pallas as pl
from jax.experimental.pallas import tpu as pltpu
from jax.sharding import Mesh, PartitionSpec as P

PLANES = 8
QUARTERS = 4
PEERS = 32
PLANE_ROWS = 1024
WIDTH = 128
CHUNKS = 2
PER_GROUP = 16
GROUPS = WIDTH // PER_GROUP
STREAMS = 5
OWN_ROWS = 32
DATA_ROWS = STREAMS * OWN_ROWS
NOTE_ROWS = 16
TAPS = 128
SHORT = 7
SPAN = 2 * TAPS
SLABS = PLANE_ROWS // TAPS
FULL_CAP = 256
LEAN_CAP = 160
RING_B = False
RING_BACK_A = False
ALL_AXES = ("z", "y", "x", "c")
IN_PLANE = ("y", "x", "c")
BF = jnp.bfloat16
F32 = jnp.float32
I32 = jnp.int32


def iota(shape, dim):
    return lax.broadcasted_iota(I32, shape, dim)


def one_hot(mask):
    return jnp.where(mask, 1.0, 0.0).astype(BF)


def call(body, out_shape, n_in_smem=0, n_in=0, n_any=0, scratch=(), flops=0, bytes_accessed=0):
    smem = [pl.BlockSpec(memory_space=pltpu.SMEM)] * n_in_smem
    vmem = [pl.BlockSpec(memory_space=pltpu.VMEM)] * n_in
    outs = jax.tree.map(lambda s: pl.BlockSpec(memory_space=pltpu.VMEM), out_shape)
    return pl.pallas_call(
        body,
        out_shape=out_shape,
        in_specs=smem + vmem + [pl.BlockSpec(memory_space=pl.ANY)] * n_any,
        out_specs=outs,
        scratch_shapes=list(scratch),
        compiler_params=pltpu.CompilerParams(vmem_limit_bytes=48 * 2**20),
        cost_estimate=pl.CostEstimate(
            flops=flops, bytes_accessed=bytes_accessed, transcendentals=0
        ),
    )


def peer_column(peer, chunk):
    quarter, column = peer // 8, peer % 8
    return (column * QUARTERS + quarter) * CHUNKS * WIDTH + chunk * WIDTH


def split_kernel(chunk, loaded_ref, note_ref, after_ref, out_ref):
    for peer in range(PEERS):
        first = peer_column(peer, chunk)
        for stream in range(STREAMS):
            out_ref[peer, stream * OWN_ROWS : (stream + 1) * OWN_ROWS, :] = loaded_ref[
                stream, :, first : first + WIDTH
            ]
        out_ref[peer, DATA_ROWS:, :] = note_ref[...]


def split_channels(loaded, chunk, note, after):
    return call(
        functools.partial(split_kernel, chunk),
        jax.ShapeDtypeStruct((PEERS, DATA_ROWS + NOTE_ROWS, WIDTH), BF),
        n_in=2,
        n_any=1,
        bytes_accessed=4 * 2**20,
    )(loaded, note, after)


def write_note(numbers):
    high, low = numbers // 128, numbers % 128
    digits = jnp.concatenate([high, low], axis=0).astype(BF)
    return jnp.pad(digits, ((0, NOTE_ROWS - digits.shape[0]), (0, WIDTH - digits.shape[1])))


def read_note(notes, rows, width):
    high = notes[:, DATA_ROWS : DATA_ROWS + rows, :width].astype(I32)
    low = notes[:, DATA_ROWS + rows : DATA_ROWS + 2 * rows, :width].astype(I32)
    return high * 128 + low


def merge_kernel(*refs):
    out_ref = refs[-1]
    for chunk in range(CHUNKS):
        for peer in range(PEERS):
            first = peer_column(peer, chunk)
            for stream in range(STREAMS):
                out_ref[stream, :, first : first + WIDTH] = refs[chunk][
                    peer, stream * OWN_ROWS : (stream + 1) * OWN_ROWS, :
                ]


def merge_channels(parts):
    return call(
        merge_kernel,
        jax.ShapeDtypeStruct((STREAMS, OWN_ROWS, PEERS * CHUNKS * WIDTH), BF),
        n_in=CHUNKS,
        bytes_accessed=6 * 2**20,
    )(*parts)


def pass_on_kernel(*refs):
    pass


def pass_on(value, *after):
    anywhere = pl.BlockSpec(memory_space=pl.ANY)
    return pl.pallas_call(
        pass_on_kernel,
        out_shape=jax.ShapeDtypeStruct(value.shape, value.dtype),
        in_specs=[anywhere] * (1 + len(after)),
        out_specs=anywhere,
        input_output_aliases={0: 0},
    )(value, *after)


def before_matrix():
    shape = (PLANE_ROWS, PLANE_ROWS)
    return one_hot(iota(shape, 0) < iota(shape, 1))


def sender_kernel(mine_ref, code_row_ref, code_col_ref):
    shape = (PLANES, PLANE_ROWS)
    target = mine_ref[...] // PLANE_ROWS
    match = target == iota(shape, 0)
    earlier = jnp.dot(one_hot(match), before_matrix(), preferred_element_type=F32)
    rank = jnp.sum(jnp.where(match, earlier, 0.0), axis=0, keepdims=True)
    code = target * FULL_CAP + rank.astype(I32)
    code_row_ref[...] = code
    tall = jnp.broadcast_to(code.astype(F32), (WIDTH, PLANE_ROWS))
    code_col_ref[...] = jnp.transpose(tall).astype(I32)


def sender_codes(mine):
    return call(
        sender_kernel,
        (
            jax.ShapeDtypeStruct((1, PLANE_ROWS), I32),
            jax.ShapeDtypeStruct((PLANE_ROWS, WIDTH), I32),
        ),
        n_in=1,
        flops=2 * 16 * 2**20,
        bytes_accessed=2**20,
    )(mine)


def receiver_kernel(here_ref, plan_ref, spot_row_ref, spot_col_ref, most_ref):
    plane = here_ref[0]
    every = plan_ref[...]
    goals = every // PLANE_ROWS
    arriving = goals == plane
    ranks = jnp.dot(one_hot(arriving), before_matrix(), preferred_element_type=F32)
    ranks = jnp.where(arriving, ranks.astype(I32), -1)
    local = every % PLANE_ROWS
    rows = iota((FULL_CAP, PLANE_ROWS), 0)
    kind = iota((8, PLANE_ROWS), 0)
    for step in range(PLANES):
        source = (plane + PLANES - step) % PLANES
        held = one_hot(rows == ranks[step : step + 1, :])
        spot = local[step : step + 1, :]
        parts = jnp.where(kind == 0, spot // 32, jnp.where(kind == 1, spot % 32, 1))
        read = lax.dot_general(
            parts.astype(F32).astype(BF),
            held,
            (((1,), (1,)), ((), ())),
            preferred_element_type=F32,
        )
        value = read[0:1] * 32.0 + read[1:2] + (read[2:3] - 1.0) * 4096.0
        spot_row_ref[pl.ds(source, 1), :] = value.astype(I32)
        tall = jnp.broadcast_to(value, (WIDTH, FULL_CAP))
        spot_col_ref[source] = jnp.transpose(tall).astype(I32)
    most = jnp.zeros((PLANES, 1), I32)
    for goal in range(PLANES):
        found = jnp.sum((goals == goal).astype(I32), axis=1, keepdims=True)
        most = jnp.maximum(most, found)
    most_ref[...] = jnp.broadcast_to(jnp.max(most, axis=0, keepdims=True), (8, 128))


def receiver_spots(here, plan):
    return call(
        receiver_kernel,
        (
            jax.ShapeDtypeStruct((PLANES, FULL_CAP), I32),
            jax.ShapeDtypeStruct((PLANES, FULL_CAP, WIDTH), I32),
            jax.ShapeDtypeStruct((8, 128), I32),
        ),
        n_in_smem=1,
        n_in=1,
        flops=2 * 64 * 2**20,
        bytes_accessed=2 * 2**20,
    )(here, plan)


def parcels_shape(cap, ring):
    if ring:
        return tuple(jax.ShapeDtypeStruct((STREAMS, cap, WIDTH), BF) for _ in range(PLANES))
    return (jax.ShapeDtypeStruct((PLANES, STREAMS, cap, WIDTH), BF),)


def take_parcels(refs, ring):
    count = PLANES if ring else 1
    return (refs[:PLANES] if ring else [refs[0].at[p] for p in range(PLANES)]), refs[count:]


def plane_at(plane, step, ring, way=1):
    return (plane + PLANES + way * step) % PLANES if ring else step


def pack_kernel(cap, ring, here_ref, rows_ref, code_ref, *rest):
    outs, (field_ref, pick_ref) = take_parcels(rest, ring)
    for stream in range(STREAMS):
        field_ref[:, stream * WIDTH : (stream + 1) * WIDTH] = rows_ref[
            :, stream * OWN_ROWS : (stream + 1) * OWN_ROWS, :
        ].reshape(PLANE_ROWS, WIDTH)
    code = code_ref[...]
    for step in range(PLANES):
        goal = plane_at(here_ref[0], step, ring)
        wanted = iota((cap, PLANE_ROWS), 0) + goal * FULL_CAP
        pick_ref[step * cap : (step + 1) * cap, :] = one_hot(wanted == code)
    for step in range(PLANES):
        packed = jnp.dot(
            pick_ref[step * cap : (step + 1) * cap, :],
            field_ref[...],
            preferred_element_type=F32,
        ).astype(BF)
        for stream in range(STREAMS):
            outs[step][stream] = packed[:, stream * WIDTH : (stream + 1) * WIDTH]


def pack(cap, ring, here, rows, code_row):
    return list(call(
        functools.partial(pack_kernel, cap, ring),
        parcels_shape(cap, ring),
        n_in_smem=1,
        n_in=2,
        scratch=[
            pltpu.VMEM((PLANE_ROWS, STREAMS * WIDTH), BF),
            pltpu.VMEM((PLANES * cap, PLANE_ROWS), BF),
        ],
        flops=2 * PLANES * cap * PLANE_ROWS * STREAMS * WIDTH,
        bytes_accessed=3 * 2**20,
    )(here, rows, code_row))


def unpack_kernel(cap, ring, here_ref, code_ref, *rest):
    parcels, (*_, out_ref, field_ref, pick_ref) = take_parcels(rest, ring)
    code = code_ref[...]
    blocks = -(-cap // WIDTH)
    for step in range(PLANES):
        goal = plane_at(here_ref[0], step, ring)
        for stream in range(STREAMS):
            field_ref[
                step * cap : (step + 1) * cap, stream * WIDTH : (stream + 1) * WIDTH
            ] = parcels[step][stream]
        for block in range(blocks):
            first = block * WIDTH
            width = min(WIDTH, cap - first)
            wanted = iota((PLANE_ROWS, WIDTH), 1) + (goal * FULL_CAP + first)
            pick_ref[:, step * cap + first : step * cap + first + width] = one_hot(
                wanted == code
            )[:, :width]
    for part in range(4):
        rows = PLANE_ROWS // 4
        found = jnp.dot(
            pick_ref[part * rows : (part + 1) * rows, :],
            field_ref[...],
            preferred_element_type=F32,
        ).astype(BF)
        peers = rows // OWN_ROWS
        for stream in range(STREAMS):
            out_ref[
                part * peers : (part + 1) * peers,
                stream * OWN_ROWS : (stream + 1) * OWN_ROWS,
                :,
            ] = found[:, stream * WIDTH : (stream + 1) * WIDTH].reshape(
                peers, OWN_ROWS, WIDTH
            )


def unpack(cap, ring, here, code_col, parcels, *after):
    return call(
        functools.partial(unpack_kernel, cap, ring),
        jax.ShapeDtypeStruct((PEERS, STREAMS * OWN_ROWS, WIDTH), BF),
        n_in_smem=1,
        n_in=1 + len(parcels),
        n_any=len(after),
        scratch=[
            pltpu.VMEM((PLANES * cap, STREAMS * WIDTH), BF),
            pltpu.VMEM((PLANE_ROWS, PLANES * cap), BF),
        ],
        flops=2 * PLANES * cap * PLANE_ROWS * STREAMS * WIDTH,
        bytes_accessed=3 * 2**20,
    )(here, code_col, *parcels, *after)


def starts_of(rows, lengths_ref):
    first, second, third = lengths_ref[0], lengths_ref[1], lengths_ref[2]
    total = jnp.where(rows >= first, first, 0)
    total = total + jnp.where(rows >= first + second, second, 0)
    return total + jnp.where(rows >= first + second + third, third, 0)


def band(base_row, rows):
    wide = jnp.broadcast_to(base_row, (rows, SPAN))
    return pltpu.roll(wide, 0, 1, stride=1, stride_axis=0).astype(BF)


def forward_mask(anchor, lengths_ref):
    shape = (TAPS, SPAN)
    begin = starts_of(anchor + iota(shape, 0), lengths_ref)
    return anchor - TAPS + iota(shape, 1) >= begin


def backward_mask(anchor, rows, lengths_ref):
    shape = (rows, SPAN)
    begin = starts_of(anchor + iota(shape, 1), lengths_ref)
    return anchor + iota(shape, 0) >= begin


def by_group(stacked, rows):
    lane_group = iota((rows, WIDTH), 1) // PER_GROUP
    total = stacked[0:rows]
    for group in range(1, GROUPS):
        total = jnp.where(
            lane_group == group, stacked[group * rows : (group + 1) * rows], total
        )
    return total


def short_sum(window, weights, anchor, rows, lengths_ref):
    targets = anchor + iota((rows, WIDTH), 0)
    reach = targets - starts_of(targets, lengths_ref)
    total = jnp.zeros((rows, WIDTH), F32)
    for lag in range(SHORT):
        source = window[8:] if lag == 0 else pltpu.roll(window, lag, 0)[8:]
        total = total + jnp.where(reach >= lag, source * weights[lag : lag + 1, :], 0.0)
    return total


def context_kernel(
    cap, ring, here_ref, lengths_ref, spot_ref, cot_ref, se_ref, back_ref, *rest
):
    parcels, rest = take_parcels(rest, ring)
    ctx_ref, ahead_ref, behind_ref, field_ref, pick_ref = rest[1:]
    plane = here_ref[0]
    for step in range(PLANES):
        source = plane_at(plane, step, ring, -1)
        for stream in range(STREAMS):
            field_ref[
                step * cap : (step + 1) * cap, stream * WIDTH : (stream + 1) * WIDTH
            ] = parcels[step][stream]
        spot = spot_ref[pl.ds(source, 1), :][:, :cap]
        pick_ref[:, step * cap : (step + 1) * cap] = one_hot(
            iota((PLANE_ROWS, cap), 0) == spot
        )
    for part in range(4):
        rows = PLANE_ROWS // 4
        found = jnp.dot(
            pick_ref[part * rows : (part + 1) * rows, :],
            field_ref[...],
            preferred_element_type=F32,
        ).astype(BF)
        for stream in range(STREAMS):
            ctx_ref[stream, part * rows : (part + 1) * rows, :] = found[
                :, stream * WIDTH : (stream + 1) * WIDTH
            ]
    weights = se_ref[...]
    anchor = plane * PLANE_ROWS
    tail = PLANE_ROWS - TAPS
    low = tail - 16
    inner = (ctx_ref[1, low:, :].astype(F32) * ctx_ref[2, low:, :].astype(F32)).astype(BF)
    window = inner.astype(F32)[8:]
    mix = short_sum(window, weights, anchor + tail, TAPS, lengths_ref)
    middle = (ctx_ref[0, tail:, :].astype(F32) * mix).astype(BF)
    ahead_ref[0:TAPS, :] = (
        ctx_ref[4, tail:, :].astype(F32) * middle.astype(F32)
    ).astype(BF)
    ahead_ref[TAPS : TAPS + 16, :] = inner[TAPS:]
    grad_two = (
        cot_ref[0:SPAN, :].astype(F32) * ctx_ref[3, 0:SPAN, :].astype(F32)
    ).astype(BF)
    behind_ref[0:TAPS, :] = grad_two[0:TAPS]
    mask = backward_mask(anchor, 16, lengths_ref)
    tiles = []
    for group in range(GROUPS):
        tile = band(back_ref[group : group + 1, :], 16).astype(F32)
        tiles.append(jnp.where(mask, tile, 0.0).astype(BF))
    stacked = jnp.dot(
        jnp.concatenate(tiles, axis=0), grad_two, preferred_element_type=F32
    )
    grad_inner = by_group(stacked, 16)
    grad_middle = grad_inner * ctx_ref[4, 0:16, :].astype(F32)
    behind_ref[TAPS : TAPS + 16, :] = (
        grad_middle * ctx_ref[0, 0:16, :].astype(F32)
    ).astype(BF)


def context(cap, ring, here, lengths, spot_row, cot, weights, back_base, parcels, after):
    return call(
        functools.partial(context_kernel, cap, ring),
        (
            jax.ShapeDtypeStruct((STREAMS, PLANE_ROWS, WIDTH), BF),
            jax.ShapeDtypeStruct((TAPS + 16, WIDTH), BF),
            jax.ShapeDtypeStruct((TAPS + 16, WIDTH), BF),
        ),
        n_in_smem=2,
        n_in=4 + len(parcels),
        n_any=1,
        scratch=[
            pltpu.VMEM((PLANES * cap, STREAMS * WIDTH), BF),
            pltpu.VMEM((PLANE_ROWS, PLANES * cap), BF),
        ],
        flops=2 * PLANES * cap * PLANE_ROWS * STREAMS * WIDTH,
        bytes_accessed=3 * 2**20,
    )(here, lengths, spot_row, cot, weights, back_base, *parcels, after)


def operator_kernel(
    cap, ring, here_ref, lengths_ref, spot_ref, cot_ref, se_ref, fore_ref, back_ref,
    ctx_ref, ahead_ref, behind_ref, after_ref, *rest,
):
    outs, rest = take_parcels(rest, ring)
    (
        long_ref, short_ref, one_ref, mix_ref, mid_ref, two_ref, gtwo_ref, gone_ref,
        fore_tile_ref, back_tile_ref, grid_ref, grads_ref, pick_ref,
    ) = rest
    plane = here_ref[0]
    origin = plane * PLANE_ROWS
    weights = se_ref[...]
    for group in range(GROUPS):
        at = slice(group * TAPS, (group + 1) * TAPS)
        fore_tile_ref[at, :] = band(fore_ref[group : group + 1, :], TAPS)
        back_tile_ref[at, :] = band(back_ref[group : group + 1, :], TAPS)
    for step in range(PLANES):
        source = plane_at(plane, step, ring, -1)
        for block in range(PLANE_ROWS // WIDTH):
            spots = spot_ref[source, :cap, :]
            pick_ref[
                step * cap : (step + 1) * cap, block * WIDTH : (block + 1) * WIDTH
            ] = one_hot(iota((cap, WIDTH), 1) + block * WIDTH == spots)
    one_ref[0:8, :] = ahead_ref[TAPS : TAPS + 16, :].astype(F32)[8:]
    two_ref[0:TAPS, :] = ahead_ref[0:TAPS, :]
    gtwo_ref[PLANE_ROWS:, :] = behind_ref[0:TAPS, :]
    gone_ref[PLANE_ROWS:, :] = behind_ref[TAPS : TAPS + 16, :].astype(F32)[0:8]
    grid_ref[...] = jnp.zeros_like(grid_ref)
    short_ref[...] = jnp.zeros_like(short_ref)

    def first_pass(slab, carry):
        at = pl.multiple_of(slab * TAPS, TAPS)
        here = pl.ds(at, TAPS)
        inner = (ctx_ref[1, here, :].astype(F32) * ctx_ref[2, here, :].astype(F32)).astype(BF)
        one_ref[pl.ds(at + 8, TAPS), :] = inner.astype(F32)
        window = one_ref[pl.ds(at, TAPS + 8), :]
        mix = short_sum(window, weights, origin + at, TAPS, lengths_ref)
        mix_ref[here, :] = mix
        middle = (ctx_ref[0, here, :].astype(F32) * mix).astype(BF)
        mid_ref[here, :] = middle
        two_ref[pl.ds(at + TAPS, TAPS), :] = (
            ctx_ref[4, here, :].astype(F32) * middle.astype(F32)
        ).astype(BF)
        gtwo_ref[here, :] = (
            cot_ref[here, :].astype(F32) * ctx_ref[3, here, :].astype(F32)
        ).astype(BF)
        return carry

    lax.fori_loop(0, SLABS, first_pass, 0)
    lane_group = iota((TAPS, WIDTH), 1) // PER_GROUP

    def second_pass(slab, carry):
        at = pl.multiple_of(slab * TAPS, TAPS)
        here = pl.ds(at, TAPS)
        anchor = origin + at
        keep_fore = forward_mask(anchor, lengths_ref)
        keep_back = backward_mask(anchor, TAPS, lengths_ref)
        fore = one_hot(keep_fore)
        back = one_hot(keep_back)
        past = two_ref[pl.ds(at, SPAN), :]
        later = gtwo_ref[pl.ds(at, SPAN), :]
        fore_tiles = jnp.concatenate(
            [fore_tile_ref[g * TAPS : (g + 1) * TAPS, :] * fore for g in range(GROUPS)], axis=0
        )
        long_mix = by_group(jnp.dot(fore_tiles, past, preferred_element_type=F32), TAPS)
        back_tiles = jnp.concatenate(
            [back_tile_ref[g * TAPS : (g + 1) * TAPS, :] * back for g in range(GROUPS)], axis=0
        )
        grad_inner = by_group(jnp.dot(back_tiles, later, preferred_element_type=F32), TAPS)
        cot = cot_ref[here, :].astype(F32)
        grads_ref[here, 3 * WIDTH : 4 * WIDTH] = (cot * long_mix).astype(BF)
        grads_ref[here, 4 * WIDTH : 5 * WIDTH] = (
            grad_inner * mid_ref[here, :].astype(F32)
        ).astype(BF)
        grad_middle = grad_inner * ctx_ref[4, here, :].astype(F32)
        mix = mix_ref[here, :]
        grads_ref[here, 0:WIDTH] = (grad_middle * mix).astype(BF)
        grad_one = (grad_middle * ctx_ref[0, here, :].astype(F32)).astype(BF).astype(F32)
        gone_ref[here, :] = grad_one
        window = one_ref[pl.ds(at, TAPS + 8), :]
        targets = anchor + iota((TAPS, WIDTH), 0)
        reach = targets - starts_of(targets, lengths_ref)
        for lag in range(SHORT):
            source = window[8:] if lag == 0 else pltpu.roll(window, lag, 0)[8:]
            terms = jnp.where(reach >= lag, source * grad_one, 0.0)
            short_ref[lag : lag + 1, :] += jnp.sum(terms, axis=0, keepdims=True)
        now = later[0:TAPS]
        split = jnp.concatenate(
            [now * one_hot(lane_group == g) for g in range(GROUPS)], axis=0
        )
        grid = lax.dot_general(
            split, past, (((1,), (1,)), ((), ())), preferred_element_type=F32
        )
        for g in range(GROUPS):
            rows = slice(g * TAPS, (g + 1) * TAPS)
            grid_ref[rows, :] += jnp.where(keep_fore, grid[rows], 0.0)
        return carry

    lax.fori_loop(0, SLABS, second_pass, 0)

    def third_pass(slab, carry):
        at = pl.multiple_of(slab * TAPS, TAPS)
        here = pl.ds(at, TAPS)
        window = gone_ref[pl.ds(at, TAPS + 8), :]
        rows = origin + at + iota((TAPS, WIDTH), 0)
        total = jnp.zeros((TAPS, WIDTH), F32)
        for lag in range(SHORT):
            later = window if lag == 0 else pltpu.roll(window, TAPS + 8 - lag, 0)
            keep = rows >= starts_of(rows + lag, lengths_ref)
            total = total + jnp.where(
                keep, later[0:TAPS] * weights[lag : lag + 1, :], 0.0
            )
        grad_inner = total.astype(BF).astype(F32)
        grads_ref[here, WIDTH : 2 * WIDTH] = (
            grad_inner * ctx_ref[2, here, :].astype(F32)
        ).astype(BF)
        grads_ref[here, 2 * WIDTH : 3 * WIDTH] = (
            grad_inner * ctx_ref[1, here, :].astype(F32)
        ).astype(BF)
        return carry

    lax.fori_loop(0, SLABS, third_pass, 0)
    for step in range(PLANES):
        packed = jnp.dot(
            pick_ref[step * cap : (step + 1) * cap, :],
            grads_ref[...],
            preferred_element_type=F32,
        ).astype(BF)
        for stream in range(STREAMS):
            outs[step][stream] = packed[:, stream * WIDTH : (stream + 1) * WIDTH]
    for group in range(GROUPS):
        total = jnp.zeros((8, SPAN), F32)
        for block in range(TAPS // 8):
            first = group * TAPS + block * 8
            piece = grid_ref[first : first + 8, :]
            piece = jnp.where(in_band(block), piece, 0.0)
            total = total + (piece if block == 0 else pltpu.roll(piece, SPAN - 8 * block, 1))
        line = total[0:1]
        for row in range(1, 8):
            line = line + pltpu.roll(total, SPAN - row, 1)[row : row + 1]
        long_ref[group : group + 1, :] = line


def in_band(block):
    lag = block * 8 + iota((8, SPAN), 0) + TAPS - iota((8, SPAN), 1)
    return (lag >= 0) & (lag < TAPS)


def operators(
    cap, ring, here, lengths, spot_col, cot, weights, fore_base, back_base, ctx, ahead, behind, after
):
    dense = PLANE_ROWS * WIDTH
    return call(
        functools.partial(operator_kernel, cap, ring),
        parcels_shape(cap, ring)
        + (
            jax.ShapeDtypeStruct((GROUPS, SPAN), F32),
            jax.ShapeDtypeStruct((8, WIDTH), F32),
        ),
        n_in_smem=2,
        n_in=8,
        n_any=1,
        scratch=[
            pltpu.VMEM((PLANE_ROWS + 8, WIDTH), F32),
            pltpu.VMEM((PLANE_ROWS, WIDTH), F32),
            pltpu.VMEM((PLANE_ROWS, WIDTH), BF),
            pltpu.VMEM((PLANE_ROWS + TAPS, WIDTH), BF),
            pltpu.VMEM((PLANE_ROWS + TAPS, WIDTH), BF),
            pltpu.VMEM((PLANE_ROWS + 8, WIDTH), F32),
            pltpu.VMEM((GROUPS * TAPS, SPAN), BF),
            pltpu.VMEM((GROUPS * TAPS, SPAN), BF),
            pltpu.VMEM((GROUPS * TAPS, SPAN), F32),
            pltpu.VMEM((PLANE_ROWS, STREAMS * WIDTH), BF),
            pltpu.VMEM((PLANES * cap, PLANE_ROWS), BF),
        ],
        flops=2 * dense * (PLANES * cap * STREAMS + 3 * GROUPS * SPAN),
        bytes_accessed=6 * 2**20,
    )(here, lengths, spot_col, cot, weights, fore_base, back_base, ctx, ahead, behind, after)


def around(value, step, axis, length):
    return lax.ppermute(value, axis, [(i, (i + step) % length) for i in range(length)])


def onward(value, step):
    pairs = [(i, i + step) for i in range(PLANES) if 0 <= i + step < PLANES]
    return lax.ppermute(value, "z", pairs)


def swap_in_plane(value):
    return lax.all_to_all(value, IN_PLANE, 0, 0, tiled=True)


def in_order(part, axis, length, pieces=None):
    at = lax.axis_index(axis)
    parts = [pieces[s] if pieces else part for s in range(length)]
    parts = parts[:1] + [around(parts[s], s, axis, length) for s in range(1, length)]
    turned = jnp.concatenate(
        [parts[(length - 1 - k) % length] for k in range(2 * length - 1)], axis=0
    )
    rows = parts[0].shape[0]
    return lax.dynamic_slice_in_dim(turned, (length - 1 - at) * rows, length * rows, 0)


def cotangent_of_plane(grad_out):
    quarter = lax.axis_index("y")
    width = CHUNKS * WIDTH
    pieces = [
        lax.dynamic_slice_in_dim(grad_out, ((quarter + s) % QUARTERS) * width, width, 1)
        for s in range(QUARTERS)
    ]
    return in_order(None, "y", QUARTERS, pieces)


def filters_of_device(se_filter, mr_filter):
    quarter = lax.axis_index("y")
    groups = CHUNKS * GROUPS
    short_taps = lax.dynamic_slice_in_dim(se_filter, quarter * groups, groups, 1)
    short_taps = jnp.repeat(short_taps.astype(F32), PER_GROUP, axis=1)
    short_taps = jnp.concatenate([short_taps, jnp.zeros((1, CHUNKS * WIDTH), F32)], axis=0)
    taps = lax.dynamic_slice_in_dim(mr_filter, quarter * groups, groups, 1)
    taps = jnp.transpose(taps.astype(F32))
    fore_base = jnp.pad(taps[:, ::-1], ((0, 0), (1, TAPS - 1)))
    back_base = jnp.pad(taps, ((0, 0), (0, TAPS)))
    return short_taps, fore_base, back_base


def filter_sums(long_parts, short_parts):
    groups = CHUNKS * GROUPS
    long_here = jnp.concatenate(long_parts, axis=0)[:, 1 : TAPS + 1][:, ::-1]
    short_here = jnp.concatenate(short_parts, axis=1).reshape(8, groups, PER_GROUP).sum(axis=2)
    together = jnp.concatenate(
        [long_here, jnp.pad(short_here, ((0, 0), (0, TAPS - groups)))], axis=0
    )
    return in_order(together, "y", QUARTERS)


def filter_totals(plane_sums):
    groups = CHUNKS * GROUPS
    summed = jnp.sum(lax.all_gather(plane_sums, "z"), axis=0).reshape(QUARTERS, groups + 8, TAPS)
    summed = summed * (PLANES * PLANE_ROWS * PER_GROUP) ** -0.5
    long_total = jnp.transpose(summed[:, :groups, :], (2, 0, 1)).reshape(TAPS, QUARTERS * groups)
    short_total = jnp.transpose(summed[:, groups : groups + SHORT, :groups], (1, 0, 2)).reshape(
        SHORT, QUARTERS * groups
    )
    return short_total, long_total


def exchange_and_operate(cap, here, lengths, codes, spots, cot, filters, rows, sent_a):
    short_taps, fore_base, back_base = filters
    lanes = [slice(c * WIDTH, (c + 1) * WIDTH) for c in range(CHUNKS)]
    mine = [slice(c * GROUPS, (c + 1) * GROUPS) for c in range(CHUNKS)]

    def exchange(ring, parts, way):
        if not ring:
            return [lax.all_to_all(parts[0], "z", 0, 0, tiled=True)]
        moved = {s: around(parts[s], way * s, "z", PLANES) for s in (1, 7, 4, 3, 5, 2, 6)}
        return [parts[0]] + [moved[s] for s in range(1, PLANES)]

    def arrive(ring, chunk, parcels, after):
        return context(
            cap, ring, here, lengths, spots[0], cot[:, lanes[chunk]],
            short_taps[:, lanes[chunk]], back_base[mine[chunk]], parcels, after,
        )

    def operate(ring, chunk, after, ctx, ahead, behind):
        *parcels, longs, shorts = operators(
            cap, ring, here, lengths, spots[1], cot[:, lanes[chunk]],
            short_taps[:, lanes[chunk]], fore_base[mine[chunk]], back_base[mine[chunk]],
            ctx, onward(ahead, 1), onward(behind, -1), after,
        )
        return parcels, longs, shorts

    if sent_a is None:
        sent_a = pack(cap, True, here, rows[0], codes[0])
    parcels_a = exchange(True, sent_a, 1)
    sent_b = pack(cap, RING_B, here, rows[1], codes[0])
    sent_b[0] = pass_on(sent_b[0], *parcels_a[1:], cot)
    parcels_b = exchange(RING_B, sent_b, 1)
    made_a, long_a, short_a = operate(
        RING_BACK_A, 0, sent_b[0], *arrive(True, 0, parcels_a, sent_b[0])
    )
    made_a[0] = pass_on(made_a[0], parcels_b[-1])
    returned_a = exchange(RING_BACK_A, made_a, -1)
    made_b, long_b, short_b = operate(
        True, 1, made_a[0], *arrive(RING_B, 1, parcels_b, made_a[0])
    )
    plane_sums = filter_sums([long_a, long_b], [short_a, short_b])
    made_b[4] = pass_on(made_b[4], returned_a[-1], plane_sums)
    returned_b = exchange(True, made_b, -1)
    back_a = swap_in_plane(unpack(cap, RING_BACK_A, here, codes[1], returned_a, made_b[4]))
    back_b = swap_in_plane(unpack(cap, True, here, codes[1], returned_b, back_a))
    totals = filter_totals(plane_sums)
    return (back_a, back_b), totals


def on_device(loaded, row_plan, lengths, se_filter, mr_filter, grad_out):
    here = lax.axis_index("z").astype(I32).reshape(1)
    own = row_plan.reshape(1, OWN_ROWS)
    rows_a = swap_in_plane(split_channels(loaded, 0, write_note(own), lengths))
    along = [own] + [around(own, s, "z", PLANES) for s in range(1, PLANES)]
    along = jnp.concatenate(along, axis=1).reshape(2, WIDTH)
    cot = cotangent_of_plane(grad_out)
    filters = filters_of_device(se_filter, mr_filter)
    mine = read_note(rows_a, 1, OWN_ROWS).reshape(1, PLANE_ROWS)
    codes = sender_codes(mine)
    sent_a = pack(LEAN_CAP, True, here, rows_a, codes[0])
    rows_b = swap_in_plane(split_channels(loaded, 1, write_note(along), sent_a[1]))
    plan = read_note(rows_b, 2, WIDTH).reshape(PEERS, PLANES, OWN_ROWS)
    plan = jnp.transpose(plan, (1, 0, 2)).reshape(PLANES, PLANE_ROWS)
    spot_row, spot_col, most = receiver_spots(here, plan)
    given = (here, lengths, codes, (spot_row, spot_col), cot, filters, (rows_a, rows_b))
    lean = exchange_and_operate(LEAN_CAP, *given, sent_a)

    def finish(lean, given):
        return (merge_channels(lean[0]),) + lean[1]

    def again(lean, given):
        return finish(exchange_and_operate(FULL_CAP, *given, None), given)

    return lax.cond(most[0, 0] <= LEAN_CAP, finish, again, lean, given)


def solution(mesh):
    grid = Mesh(mesh.devices.reshape(PLANES, QUARTERS, 4, 2), ALL_AXES)
    placed = (
        P(None, ALL_AXES, None),
        P(ALL_AXES),
        P(),
        P(None, ("x", "c")),
        P(None, ("x", "c")),
        P(("z", "y"), ("x", "c")),
    )
    return jax.shard_map(
        on_device,
        mesh=grid,
        in_specs=placed,
        out_specs=(P(None, ALL_AXES, None), P(None, ("x", "c")), P(None, ("x", "c"))),
        check_vma=False,
    )
```

```python
import functools

import jax
import jax.numpy as jnp
from jax import lax
from jax.experimental import pallas as pl
from jax.experimental.pallas import tpu as pltpu
from jax.sharding import Mesh, PartitionSpec as P

PLANES = 8
QUARTERS = 4
PEERS = 32
PLANE_ROWS = 1024
WIDTH = 128
CHUNKS = 2
PER_GROUP = 16
GROUPS = WIDTH // PER_GROUP
STREAMS = 5
OWN_ROWS = 32
DATA_ROWS = STREAMS * OWN_ROWS
NOTE_ROWS = 16
TAPS = 128
SHORT = 7
SPAN = 2 * TAPS
SLABS = PLANE_ROWS // TAPS
FULL_CAP = 256
LEAN_CAP = 160
RING_B = False
RING_BACK_A = False
ALL_AXES = ("z", "y", "x", "c")
IN_PLANE = ("y", "x", "c")
BF = jnp.bfloat16
F32 = jnp.float32
I32 = jnp.int32


def iota(shape, dim):
    return lax.broadcasted_iota(I32, shape, dim)


def one_hot(mask):
    return jnp.where(mask, 1.0, 0.0).astype(BF)


def call(body, out_shape, n_in_smem=0, n_in=0, n_any=0, scratch=(), flops=0, bytes_accessed=0):
    smem = [pl.BlockSpec(memory_space=pltpu.SMEM)] * n_in_smem
    vmem = [pl.BlockSpec(memory_space=pltpu.VMEM)] * n_in
    outs = jax.tree.map(lambda s: pl.BlockSpec(memory_space=pltpu.VMEM), out_shape)
    return pl.pallas_call(
        body,
        out_shape=out_shape,
        in_specs=smem + vmem + [pl.BlockSpec(memory_space=pl.ANY)] * n_any,
        out_specs=outs,
        scratch_shapes=list(scratch),
        compiler_params=pltpu.CompilerParams(vmem_limit_bytes=48 * 2**20),
        cost_estimate=pl.CostEstimate(
            flops=flops, bytes_accessed=bytes_accessed, transcendentals=0
        ),
    )


def peer_column(peer, chunk):
    quarter, column = peer // 8, peer % 8
    return (column * QUARTERS + quarter) * CHUNKS * WIDTH + chunk * WIDTH


def split_kernel(chunk, loaded_ref, note_ref, after_ref, out_ref):
    for peer in range(PEERS):
        first = peer_column(peer, chunk)
        for stream in range(STREAMS):
            out_ref[peer, stream * OWN_ROWS : (stream + 1) * OWN_ROWS, :] = loaded_ref[
                stream, :, first : first + WIDTH
            ]
        out_ref[peer, DATA_ROWS:, :] = note_ref[...]


def split_channels(loaded, chunk, note, after):
    return call(
        functools.partial(split_kernel, chunk),
        jax.ShapeDtypeStruct((PEERS, DATA_ROWS + NOTE_ROWS, WIDTH), BF),
        n_in=2,
        n_any=1,
        bytes_accessed=4 * 2**20,
    )(loaded, note, after)


def write_note(numbers):
    high, low = numbers // 128, numbers % 128
    digits = jnp.concatenate([high, low], axis=0).astype(BF)
    return jnp.pad(digits, ((0, NOTE_ROWS - digits.shape[0]), (0, WIDTH - digits.shape[1])))


def read_note(notes, rows, width):
    high = notes[:, DATA_ROWS : DATA_ROWS + rows, :width].astype(I32)
    low = notes[:, DATA_ROWS + rows : DATA_ROWS + 2 * rows, :width].astype(I32)
    return high * 128 + low


def merge_kernel(*refs):
    out_ref = refs[-1]
    for chunk in range(CHUNKS):
        for peer in range(PEERS):
            first = peer_column(peer, chunk)
            for stream in range(STREAMS):
                out_ref[stream, :, first : first + WIDTH] = refs[chunk][
                    peer, stream * OWN_ROWS : (stream + 1) * OWN_ROWS, :
                ]


def merge_channels(parts):
    return call(
        merge_kernel,
        jax.ShapeDtypeStruct((STREAMS, OWN_ROWS, PEERS * CHUNKS * WIDTH), BF),
        n_in=CHUNKS,
        bytes_accessed=6 * 2**20,
    )(*parts)


def pass_on_kernel(*refs):
    pass


def pass_on(value, *after):
    anywhere = pl.BlockSpec(memory_space=pl.ANY)
    return pl.pallas_call(
        pass_on_kernel,
        out_shape=jax.ShapeDtypeStruct(value.shape, value.dtype),
        in_specs=[anywhere] * (1 + len(after)),
        out_specs=anywhere,
        input_output_aliases={0: 0},
    )(value, *after)


def before_matrix():
    shape = (PLANE_ROWS, PLANE_ROWS)
    return one_hot(iota(shape, 0) < iota(shape, 1))


def sender_kernel(mine_ref, code_row_ref, code_col_ref):
    shape = (PLANES, PLANE_ROWS)
    target = mine_ref[...] // PLANE_ROWS
    match = target == iota(shape, 0)
    earlier = jnp.dot(one_hot(match), before_matrix(), preferred_element_type=F32)
    rank = jnp.sum(jnp.where(match, earlier, 0.0), axis=0, keepdims=True)
    code = target * FULL_CAP + rank.astype(I32)
    code_row_ref[...] = code
    tall = jnp.broadcast_to(code.astype(F32), (WIDTH, PLANE_ROWS))
    code_col_ref[...] = jnp.transpose(tall).astype(I32)


def sender_codes(mine):
    return call(
        sender_kernel,
        (
            jax.ShapeDtypeStruct((1, PLANE_ROWS), I32),
            jax.ShapeDtypeStruct((PLANE_ROWS, WIDTH), I32),
        ),
        n_in=1,
        flops=2 * 16 * 2**20,
        bytes_accessed=2**20,
    )(mine)


def receiver_kernel(here_ref, plan_ref, spot_row_ref, spot_col_ref, most_ref):
    plane = here_ref[0]
    every = plan_ref[...]
    goals = every // PLANE_ROWS
    arriving = goals == plane
    ranks = jnp.dot(one_hot(arriving), before_matrix(), preferred_element_type=F32)
    ranks = jnp.where(arriving, ranks.astype(I32), -1)
    local = every % PLANE_ROWS
    rows = iota((FULL_CAP, PLANE_ROWS), 0)
    kind = iota((8, PLANE_ROWS), 0)
    for step in range(PLANES):
        source = (plane + PLANES - step) % PLANES
        held = one_hot(rows == ranks[step : step + 1, :])
        spot = local[step : step + 1, :]
        parts = jnp.where(kind == 0, spot // 32, jnp.where(kind == 1, spot % 32, 1))
        read = lax.dot_general(
            parts.astype(F32).astype(BF),
            held,
            (((1,), (1,)), ((), ())),
            preferred_element_type=F32,
        )
        value = read[0:1] * 32.0 + read[1:2] + (read[2:3] - 1.0) * 4096.0
        spot_row_ref[pl.ds(source, 1), :] = value.astype(I32)
        tall = jnp.broadcast_to(value, (WIDTH, FULL_CAP))
        spot_col_ref[source] = jnp.transpose(tall).astype(I32)
    most = jnp.zeros((PLANES, 1), I32)
    for goal in range(PLANES):
        found = jnp.sum((goals == goal).astype(I32), axis=1, keepdims=True)
        most = jnp.maximum(most, found)
    most_ref[...] = jnp.broadcast_to(jnp.max(most, axis=0, keepdims=True), (8, 128))


def receiver_spots(here, plan):
    return call(
        receiver_kernel,
        (
            jax.ShapeDtypeStruct((PLANES, FULL_CAP), I32),
            jax.ShapeDtypeStruct((PLANES, FULL_CAP, WIDTH), I32),
            jax.ShapeDtypeStruct((8, 128), I32),
        ),
        n_in_smem=1,
        n_in=1,
        flops=2 * 64 * 2**20,
        bytes_accessed=2 * 2**20,
    )(here, plan)


def parcels_shape(cap, ring):
    if ring:
        return tuple(jax.ShapeDtypeStruct((STREAMS, cap, WIDTH), BF) for _ in range(PLANES))
    return (jax.ShapeDtypeStruct((PLANES, STREAMS, cap, WIDTH), BF),)


def take_parcels(refs, ring):
    count = PLANES if ring else 1
    return (refs[:PLANES] if ring else [refs[0].at[p] for p in range(PLANES)]), refs[count:]


def fetch_parcels(parcels, field_ref, cap, sems):
    copies = []
    for step in range(PLANES):
        for stream in range(STREAMS):
            copies.append(
                pltpu.make_async_copy(
                    parcels[step].at[stream],
                    field_ref.at[
                        pl.ds(step * cap, cap), pl.ds(stream * WIDTH, WIDTH)
                    ],
                    sems.at[step * STREAMS + stream],
                )
            )
            copies[-1].start()
    return copies


def plane_at(plane, step, ring, way=1):
    return (plane + PLANES + way * step) % PLANES if ring else step


def pack_kernel(cap, ring, here_ref, rows_ref, code_ref, after_ref, *rest):
    outs, (field_ref, pick_ref) = take_parcels(rest, ring)
    for stream in range(STREAMS):
        field_ref[:, stream * WIDTH : (stream + 1) * WIDTH] = rows_ref[
            :, stream * OWN_ROWS : (stream + 1) * OWN_ROWS, :
        ].reshape(PLANE_ROWS, WIDTH)
    code = code_ref[...]
    for step in range(PLANES):
        goal = plane_at(here_ref[0], step, ring)
        wanted = iota((cap, PLANE_ROWS), 0) + goal * FULL_CAP
        pick_ref[step * cap : (step + 1) * cap, :] = one_hot(wanted == code)
    for step in range(PLANES):
        packed = jnp.dot(
            pick_ref[step * cap : (step + 1) * cap, :],
            field_ref[...],
            preferred_element_type=F32,
        ).astype(BF)
        for stream in range(STREAMS):
            outs[step][stream] = packed[:, stream * WIDTH : (stream + 1) * WIDTH]


def pack(cap, ring, here, rows, code_row, after):
    return list(call(
        functools.partial(pack_kernel, cap, ring),
        parcels_shape(cap, ring),
        n_in_smem=1,
        n_in=2,
        n_any=1,
        scratch=[
            pltpu.VMEM((PLANE_ROWS, STREAMS * WIDTH), BF),
            pltpu.VMEM((PLANES * cap, PLANE_ROWS), BF),
        ],
        flops=2 * PLANES * cap * PLANE_ROWS * STREAMS * WIDTH,
        bytes_accessed=3 * 2**20,
    )(here, rows, code_row, after))


def unpack_kernel(cap, ring, here_ref, code_ref, *rest):
    parcels, (*_, out_ref, field_ref, pick_ref, sems) = take_parcels(rest, ring)
    copies = fetch_parcels(parcels, field_ref, cap, sems)
    code = code_ref[...]
    blocks = -(-cap // WIDTH)
    for step in range(PLANES):
        goal = plane_at(here_ref[0], step, ring)
        for block in range(blocks):
            first = block * WIDTH
            width = min(WIDTH, cap - first)
            wanted = iota((PLANE_ROWS, WIDTH), 1) + (goal * FULL_CAP + first)
            pick_ref[:, step * cap + first : step * cap + first + width] = one_hot(
                wanted == code
            )[:, :width]
    for copy in copies:
        copy.wait()
    for part in range(4):
        rows = PLANE_ROWS // 4
        found = jnp.dot(
            pick_ref[part * rows : (part + 1) * rows, :],
            field_ref[...],
            preferred_element_type=F32,
        ).astype(BF)
        peers = rows // OWN_ROWS
        for stream in range(STREAMS):
            out_ref[
                part * peers : (part + 1) * peers,
                stream * OWN_ROWS : (stream + 1) * OWN_ROWS,
                :,
            ] = found[:, stream * WIDTH : (stream + 1) * WIDTH].reshape(
                peers, OWN_ROWS, WIDTH
            )


def unpack(cap, ring, here, code_col, parcels, *after):
    return call(
        functools.partial(unpack_kernel, cap, ring),
        jax.ShapeDtypeStruct((PEERS, STREAMS * OWN_ROWS, WIDTH), BF),
        n_in_smem=1,
        n_in=1,
        n_any=len(parcels) + len(after),
        scratch=[
            pltpu.VMEM((PLANES * cap, STREAMS * WIDTH), BF),
            pltpu.VMEM((PLANE_ROWS, PLANES * cap), BF),
            pltpu.SemaphoreType.DMA((PLANES * STREAMS,)),
        ],
        flops=2 * PLANES * cap * PLANE_ROWS * STREAMS * WIDTH,
        bytes_accessed=3 * 2**20,
    )(here, code_col, *parcels, *after)


def starts_of(rows, lengths_ref):
    first, second, third = lengths_ref[0], lengths_ref[1], lengths_ref[2]
    total = jnp.where(rows >= first, first, 0)
    total = total + jnp.where(rows >= first + second, second, 0)
    return total + jnp.where(rows >= first + second + third, third, 0)


def band(base_row, rows):
    wide = jnp.broadcast_to(base_row, (rows, SPAN))
    return pltpu.roll(wide, 0, 1, stride=1, stride_axis=0).astype(BF)


def forward_mask(anchor, lengths_ref):
    shape = (TAPS, SPAN)
    begin = starts_of(anchor + iota(shape, 0), lengths_ref)
    return anchor - TAPS + iota(shape, 1) >= begin


def backward_mask(anchor, rows, lengths_ref):
    shape = (rows, SPAN)
    begin = starts_of(anchor + iota(shape, 1), lengths_ref)
    return anchor + iota(shape, 0) >= begin


def by_group(stacked, rows):
    lane_group = iota((rows, WIDTH), 1) // PER_GROUP
    total = stacked[0:rows]
    for group in range(1, GROUPS):
        total = jnp.where(
            lane_group == group, stacked[group * rows : (group + 1) * rows], total
        )
    return total


def short_sum(window, weights, anchor, rows, lengths_ref):
    targets = anchor + iota((rows, WIDTH), 0)
    reach = targets - starts_of(targets, lengths_ref)
    total = jnp.zeros((rows, WIDTH), F32)
    for lag in range(SHORT):
        source = window[8:] if lag == 0 else pltpu.roll(window, lag, 0)[8:]
        total = total + jnp.where(reach >= lag, source * weights[lag : lag + 1, :], 0.0)
    return total


def context_kernel(
    cap, ring, here_ref, lengths_ref, spot_ref, cot_ref, se_ref, back_ref, *rest
):
    parcels, rest = take_parcels(rest, ring)
    ctx_ref, ahead_ref, behind_ref, field_ref, pick_ref, sems = rest[1:]
    copies = fetch_parcels(parcels, field_ref, cap, sems)
    plane = here_ref[0]
    for step in range(PLANES):
        source = plane_at(plane, step, ring, -1)
        spot = spot_ref[pl.ds(source, 1), :][:, :cap]
        pick_ref[:, step * cap : (step + 1) * cap] = one_hot(
            iota((PLANE_ROWS, cap), 0) == spot
        )
    for copy in copies:
        copy.wait()
    for part in range(4):
        rows = PLANE_ROWS // 4
        found = jnp.dot(
            pick_ref[part * rows : (part + 1) * rows, :],
            field_ref[...],
            preferred_element_type=F32,
        ).astype(BF)
        for stream in range(STREAMS):
            ctx_ref[stream, part * rows : (part + 1) * rows, :] = found[
                :, stream * WIDTH : (stream + 1) * WIDTH
            ]
    weights = se_ref[...]
    anchor = plane * PLANE_ROWS
    tail = PLANE_ROWS - TAPS
    low = tail - 16
    inner = (ctx_ref[1, low:, :].astype(F32) * ctx_ref[2, low:, :].astype(F32)).astype(BF)
    window = inner.astype(F32)[8:]
    mix = short_sum(window, weights, anchor + tail, TAPS, lengths_ref)
    middle = (ctx_ref[0, tail:, :].astype(F32) * mix).astype(BF)
    ahead_ref[0:TAPS, :] = (
        ctx_ref[4, tail:, :].astype(F32) * middle.astype(F32)
    ).astype(BF)
    ahead_ref[TAPS : TAPS + 16, :] = inner[TAPS:]
    grad_two = (
        cot_ref[0:SPAN, :].astype(F32) * ctx_ref[3, 0:SPAN, :].astype(F32)
    ).astype(BF)
    behind_ref[0:TAPS, :] = grad_two[0:TAPS]
    mask = backward_mask(anchor, 16, lengths_ref)
    tiles = []
    for group in range(GROUPS):
        tile = band(back_ref[group : group + 1, :], 16).astype(F32)
        tiles.append(jnp.where(mask, tile, 0.0).astype(BF))
    stacked = jnp.dot(
        jnp.concatenate(tiles, axis=0), grad_two, preferred_element_type=F32
    )
    grad_inner = by_group(stacked, 16)
    grad_middle = grad_inner * ctx_ref[4, 0:16, :].astype(F32)
    behind_ref[TAPS : TAPS + 16, :] = (
        grad_middle * ctx_ref[0, 0:16, :].astype(F32)
    ).astype(BF)


def context(cap, ring, here, lengths, spot_row, cot, weights, back_base, parcels, after):
    return call(
        functools.partial(context_kernel, cap, ring),
        (
            jax.ShapeDtypeStruct((STREAMS, PLANE_ROWS, WIDTH), BF),
            jax.ShapeDtypeStruct((TAPS + 16, WIDTH), BF),
            jax.ShapeDtypeStruct((TAPS + 16, WIDTH), BF),
        ),
        n_in_smem=2,
        n_in=4,
        n_any=len(parcels) + 1,
        scratch=[
            pltpu.VMEM((PLANES * cap, STREAMS * WIDTH), BF),
            pltpu.VMEM((PLANE_ROWS, PLANES * cap), BF),
            pltpu.SemaphoreType.DMA((PLANES * STREAMS,)),
        ],
        flops=2 * PLANES * cap * PLANE_ROWS * STREAMS * WIDTH,
        bytes_accessed=3 * 2**20,
    )(here, lengths, spot_row, cot, weights, back_base, *parcels, after)


def operator_kernel(
    cap, ring, here_ref, lengths_ref, spot_ref, cot_ref, se_ref, fore_ref, back_ref,
    ctx_ref, ahead_ref, behind_ref, after_ref, *rest,
):
    outs, rest = take_parcels(rest, ring)
    (
        long_ref, short_ref, one_ref, mix_ref, mid_ref, two_ref, gtwo_ref, gone_ref,
        fore_tile_ref, back_tile_ref, grid_ref, grads_ref, pick_ref,
    ) = rest
    plane = here_ref[0]
    origin = plane * PLANE_ROWS
    weights = se_ref[...]
    for group in range(GROUPS):
        at = slice(group * TAPS, (group + 1) * TAPS)
        fore_tile_ref[at, :] = band(fore_ref[group : group + 1, :], TAPS)
        back_tile_ref[at, :] = band(back_ref[group : group + 1, :], TAPS)
    for step in range(PLANES):
        source = plane_at(plane, step, ring, -1)
        for block in range(PLANE_ROWS // WIDTH):
            spots = spot_ref[source, :cap, :]
            pick_ref[
                step * cap : (step + 1) * cap, block * WIDTH : (block + 1) * WIDTH
            ] = one_hot(iota((cap, WIDTH), 1) + block * WIDTH == spots)
    one_ref[0:8, :] = ahead_ref[TAPS : TAPS + 16, :].astype(F32)[8:]
    two_ref[0:TAPS, :] = ahead_ref[0:TAPS, :]
    gtwo_ref[PLANE_ROWS:, :] = behind_ref[0:TAPS, :]
    gone_ref[PLANE_ROWS:, :] = behind_ref[TAPS : TAPS + 16, :].astype(F32)[0:8]
    grid_ref[...] = jnp.zeros_like(grid_ref)
    short_ref[...] = jnp.zeros_like(short_ref)

    def first_pass(slab, carry):
        at = pl.multiple_of(slab * TAPS, TAPS)
        here = pl.ds(at, TAPS)
        inner = (ctx_ref[1, here, :].astype(F32) * ctx_ref[2, here, :].astype(F32)).astype(BF)
        one_ref[pl.ds(at + 8, TAPS), :] = inner.astype(F32)
        window = one_ref[pl.ds(at, TAPS + 8), :]
        mix = short_sum(window, weights, origin + at, TAPS, lengths_ref)
        mix_ref[here, :] = mix
        middle = (ctx_ref[0, here, :].astype(F32) * mix).astype(BF)
        mid_ref[here, :] = middle
        two_ref[pl.ds(at + TAPS, TAPS), :] = (
            ctx_ref[4, here, :].astype(F32) * middle.astype(F32)
        ).astype(BF)
        gtwo_ref[here, :] = (
            cot_ref[here, :].astype(F32) * ctx_ref[3, here, :].astype(F32)
        ).astype(BF)
        return carry

    lax.fori_loop(0, SLABS, first_pass, 0)
    lane_group = iota((TAPS, WIDTH), 1) // PER_GROUP

    def second_pass(slab, carry):
        at = pl.multiple_of(slab * TAPS, TAPS)
        here = pl.ds(at, TAPS)
        anchor = origin + at
        keep_fore = forward_mask(anchor, lengths_ref)
        keep_back = backward_mask(anchor, TAPS, lengths_ref)
        fore = one_hot(keep_fore)
        back = one_hot(keep_back)
        past = two_ref[pl.ds(at, SPAN), :]
        later = gtwo_ref[pl.ds(at, SPAN), :]
        fore_tiles = jnp.concatenate(
            [fore_tile_ref[g * TAPS : (g + 1) * TAPS, :] * fore for g in range(GROUPS)], axis=0
        )
        long_mix = by_group(jnp.dot(fore_tiles, past, preferred_element_type=F32), TAPS)
        back_tiles = jnp.concatenate(
            [back_tile_ref[g * TAPS : (g + 1) * TAPS, :] * back for g in range(GROUPS)], axis=0
        )
        grad_inner = by_group(jnp.dot(back_tiles, later, preferred_element_type=F32), TAPS)
        cot = cot_ref[here, :].astype(F32)
        grads_ref[here, 3 * WIDTH : 4 * WIDTH] = (cot * long_mix).astype(BF)
        grads_ref[here, 4 * WIDTH : 5 * WIDTH] = (
            grad_inner * mid_ref[here, :].astype(F32)
        ).astype(BF)
        grad_middle = grad_inner * ctx_ref[4, here, :].astype(F32)
        mix = mix_ref[here, :]
        grads_ref[here, 0:WIDTH] = (grad_middle * mix).astype(BF)
        grad_one = (grad_middle * ctx_ref[0, here, :].astype(F32)).astype(BF).astype(F32)
        gone_ref[here, :] = grad_one
        window = one_ref[pl.ds(at, TAPS + 8), :]
        targets = anchor + iota((TAPS, WIDTH), 0)
        reach = targets - starts_of(targets, lengths_ref)
        for lag in range(SHORT):
            source = window[8:] if lag == 0 else pltpu.roll(window, lag, 0)[8:]
            terms = jnp.where(reach >= lag, source * grad_one, 0.0)
            short_ref[lag : lag + 1, :] += jnp.sum(terms, axis=0, keepdims=True)
        now = later[0:TAPS]
        split = jnp.concatenate(
            [now * one_hot(lane_group == g) for g in range(GROUPS)], axis=0
        )
        grid = lax.dot_general(
            split, past, (((1,), (1,)), ((), ())), preferred_element_type=F32
        )
        for g in range(GROUPS):
            rows = slice(g * TAPS, (g + 1) * TAPS)
            grid_ref[rows, :] += jnp.where(keep_fore, grid[rows], 0.0)
        return carry

    lax.fori_loop(0, SLABS, second_pass, 0)

    def third_pass(slab, carry):
        at = pl.multiple_of(slab * TAPS, TAPS)
        here = pl.ds(at, TAPS)
        window = gone_ref[pl.ds(at, TAPS + 8), :]
        rows = origin + at + iota((TAPS, WIDTH), 0)
        total = jnp.zeros((TAPS, WIDTH), F32)
        for lag in range(SHORT):
            later = window if lag == 0 else pltpu.roll(window, TAPS + 8 - lag, 0)
            keep = rows >= starts_of(rows + lag, lengths_ref)
            total = total + jnp.where(
                keep, later[0:TAPS] * weights[lag : lag + 1, :], 0.0
            )
        grad_inner = total.astype(BF).astype(F32)
        grads_ref[here, WIDTH : 2 * WIDTH] = (
            grad_inner * ctx_ref[2, here, :].astype(F32)
        ).astype(BF)
        grads_ref[here, 2 * WIDTH : 3 * WIDTH] = (
            grad_inner * ctx_ref[1, here, :].astype(F32)
        ).astype(BF)
        return carry

    lax.fori_loop(0, SLABS, third_pass, 0)
    for step in range(PLANES):
        packed = jnp.dot(
            pick_ref[step * cap : (step + 1) * cap, :],
            grads_ref[...],
            preferred_element_type=F32,
        ).astype(BF)
        for stream in range(STREAMS):
            outs[step][stream] = packed[:, stream * WIDTH : (stream + 1) * WIDTH]
    for group in range(GROUPS):
        total = jnp.zeros((8, SPAN), F32)
        for block in range(TAPS // 8):
            first = group * TAPS + block * 8
            piece = grid_ref[first : first + 8, :]
            piece = jnp.where(in_band(block), piece, 0.0)
            total = total + (piece if block == 0 else pltpu.roll(piece, SPAN - 8 * block, 1))
        line = total[0:1]
        for row in range(1, 8):
            line = line + pltpu.roll(total, SPAN - row, 1)[row : row + 1]
        long_ref[group : group + 1, :] = line


def in_band(block):
    lag = block * 8 + iota((8, SPAN), 0) + TAPS - iota((8, SPAN), 1)
    return (lag >= 0) & (lag < TAPS)


def operators(
    cap, ring, here, lengths, spot_col, cot, weights, fore_base, back_base, ctx, ahead, behind, after
):
    dense = PLANE_ROWS * WIDTH
    return call(
        functools.partial(operator_kernel, cap, ring),
        parcels_shape(cap, ring)
        + (
            jax.ShapeDtypeStruct((GROUPS, SPAN), F32),
            jax.ShapeDtypeStruct((8, WIDTH), F32),
        ),
        n_in_smem=2,
        n_in=8,
        n_any=1,
        scratch=[
            pltpu.VMEM((PLANE_ROWS + 8, WIDTH), F32),
            pltpu.VMEM((PLANE_ROWS, WIDTH), F32),
            pltpu.VMEM((PLANE_ROWS, WIDTH), BF),
            pltpu.VMEM((PLANE_ROWS + TAPS, WIDTH), BF),
            pltpu.VMEM((PLANE_ROWS + TAPS, WIDTH), BF),
            pltpu.VMEM((PLANE_ROWS + 8, WIDTH), F32),
            pltpu.VMEM((GROUPS * TAPS, SPAN), BF),
            pltpu.VMEM((GROUPS * TAPS, SPAN), BF),
            pltpu.VMEM((GROUPS * TAPS, SPAN), F32),
            pltpu.VMEM((PLANE_ROWS, STREAMS * WIDTH), BF),
            pltpu.VMEM((PLANES * cap, PLANE_ROWS), BF),
        ],
        flops=2 * dense * (PLANES * cap * STREAMS + 3 * GROUPS * SPAN),
        bytes_accessed=6 * 2**20,
    )(here, lengths, spot_col, cot, weights, fore_base, back_base, ctx, ahead, behind, after)


def around(value, step, axis, length):
    return lax.ppermute(value, axis, [(i, (i + step) % length) for i in range(length)])


def onward(value, step):
    pairs = [(i, i + step) for i in range(PLANES) if 0 <= i + step < PLANES]
    return lax.ppermute(value, "z", pairs)


def swap_in_plane(value):
    return lax.all_to_all(value, IN_PLANE, 0, 0, tiled=True)


def in_order(part, axis, length, pieces=None):
    at = lax.axis_index(axis)
    parts = [pieces[s] if pieces else part for s in range(length)]
    parts = parts[:1] + [around(parts[s], s, axis, length) for s in range(1, length)]
    turned = jnp.concatenate(
        [parts[(length - 1 - k) % length] for k in range(2 * length - 1)], axis=0
    )
    rows = parts[0].shape[0]
    return lax.dynamic_slice_in_dim(turned, (length - 1 - at) * rows, length * rows, 0)


def cotangent_of_plane(grad_out):
    quarter = lax.axis_index("y")
    width = CHUNKS * WIDTH
    pieces = [
        lax.dynamic_slice_in_dim(grad_out, ((quarter + s) % QUARTERS) * width, width, 1)
        for s in range(QUARTERS)
    ]
    return in_order(None, "y", QUARTERS, pieces)


def filters_of_device(se_filter, mr_filter):
    quarter = lax.axis_index("y")
    groups = CHUNKS * GROUPS
    short_taps = lax.dynamic_slice_in_dim(se_filter, quarter * groups, groups, 1)
    short_taps = jnp.repeat(short_taps.astype(F32), PER_GROUP, axis=1)
    short_taps = jnp.concatenate([short_taps, jnp.zeros((1, CHUNKS * WIDTH), F32)], axis=0)
    taps = lax.dynamic_slice_in_dim(mr_filter, quarter * groups, groups, 1)
    taps = jnp.transpose(taps.astype(F32))
    fore_base = jnp.pad(taps[:, ::-1], ((0, 0), (1, TAPS - 1)))
    back_base = jnp.pad(taps, ((0, 0), (0, TAPS)))
    return short_taps, fore_base, back_base


def filter_sums(long_parts, short_parts):
    groups = CHUNKS * GROUPS
    long_here = jnp.concatenate(long_parts, axis=0)[:, 1 : TAPS + 1][:, ::-1]
    short_here = jnp.concatenate(short_parts, axis=1).reshape(8, groups, PER_GROUP).sum(axis=2)
    together = jnp.concatenate(
        [long_here, jnp.pad(short_here, ((0, 0), (0, TAPS - groups)))], axis=0
    )
    return jnp.sum(lax.all_gather(together, "z"), axis=0)


def filter_totals(sums):
    groups = CHUNKS * GROUPS
    summed = lax.all_gather(sums, "y") * (PLANES * PLANE_ROWS * PER_GROUP) ** -0.5
    long_total = jnp.transpose(summed[:, :groups, :], (2, 0, 1)).reshape(TAPS, QUARTERS * groups)
    short_total = jnp.transpose(summed[:, groups : groups + SHORT, :groups], (1, 0, 2)).reshape(
        SHORT, QUARTERS * groups
    )
    return short_total, long_total


def exchange_and_operate(cap, here, lengths, codes, spots, cot, filters, rows, sent_a):
    short_taps, fore_base, back_base = filters
    lanes = [slice(c * WIDTH, (c + 1) * WIDTH) for c in range(CHUNKS)]
    mine = [slice(c * GROUPS, (c + 1) * GROUPS) for c in range(CHUNKS)]

    def exchange(ring, parts, way):
        if not ring:
            return [lax.all_to_all(parts[0], "z", 0, 0, tiled=True)]
        moved = {s: around(parts[s], way * s, "z", PLANES) for s in (1, 7, 4, 3, 5, 2, 6)}
        return [parts[0]] + [moved[s] for s in range(1, PLANES)]

    def arrive(ring, chunk, parcels, after):
        ctx, ahead, behind = context(
            cap, ring, here, lengths, spots[0], cot[:, lanes[chunk]],
            short_taps[:, lanes[chunk]], back_base[mine[chunk]], parcels, after,
        )
        return ctx, onward(ahead, 1), onward(behind, -1)

    def operate(ring, chunk, after, ctx, ahead, behind):
        *parcels, longs, shorts = operators(
            cap, ring, here, lengths, spots[1], cot[:, lanes[chunk]],
            short_taps[:, lanes[chunk]], fore_base[mine[chunk]], back_base[mine[chunk]],
            ctx, ahead, behind, after,
        )
        return parcels, longs, shorts

    if sent_a is None:
        sent_a = pack(cap, True, here, rows[0], codes[0], here)
    parcels_a = exchange(True, sent_a, 1)
    sent_b = pack(cap, RING_B, here, rows[1], codes[0], here)
    sent_b[0] = pass_on(sent_b[0], *parcels_a[1:], *spots, *filters)
    parcels_b = exchange(RING_B, sent_b, 1)
    made_a, long_a, short_a = operate(
        RING_BACK_A, 0, sent_b[0], *arrive(True, 0, parcels_a, sent_b[0])
    )
    arrived_b = arrive(RING_B, 1, parcels_b, made_a[0])
    made_a[0] = pass_on(made_a[0], *arrived_b[1:])
    returned_a = exchange(RING_BACK_A, made_a, -1)
    made_b, long_b, short_b = operate(True, 1, here, *arrived_b)
    sums = filter_sums([long_a, long_b], [short_a, short_b])
    made_b[4] = pass_on(made_b[4], returned_a[-1], sums)
    returned_b = exchange(True, made_b, -1)
    back_a = swap_in_plane(unpack(cap, RING_BACK_A, here, codes[1], returned_a, made_b[4]))
    back_b = swap_in_plane(unpack(cap, True, here, codes[1], returned_b, back_a))
    totals = filter_totals(sums)
    return (back_a, back_b), totals


def on_device(loaded, row_plan, lengths, se_filter, mr_filter, grad_out):
    here = lax.axis_index("z").astype(I32).reshape(1)
    own = row_plan.reshape(1, OWN_ROWS)
    rows_a = swap_in_plane(split_channels(loaded, 0, write_note(own), lengths))
    along = [own] + [around(own, s, "z", PLANES) for s in range(1, PLANES)]
    along = jnp.concatenate(along, axis=1).reshape(2, WIDTH)
    cot = cotangent_of_plane(grad_out)
    filters = filters_of_device(se_filter, mr_filter)
    mine = read_note(rows_a, 1, OWN_ROWS).reshape(1, PLANE_ROWS)
    codes = sender_codes(mine)
    sent_a = pack(LEAN_CAP, True, here, rows_a, codes[0], cot)
    rows_b = swap_in_plane(split_channels(loaded, 1, write_note(along), sent_a[1]))
    plan = read_note(rows_b, 2, WIDTH).reshape(PEERS, PLANES, OWN_ROWS)
    plan = jnp.transpose(plan, (1, 0, 2)).reshape(PLANES, PLANE_ROWS)
    spot_row, spot_col, most = receiver_spots(here, plan)
    given = (here, lengths, codes, (spot_row, spot_col), cot, filters, (rows_a, rows_b))
    lean = exchange_and_operate(LEAN_CAP, *given, sent_a)

    def finish(lean, given):
        return (merge_channels(lean[0]),) + lean[1]

    def again(lean, given):
        return finish(exchange_and_operate(FULL_CAP, *given, None), given)

    return lax.cond(most[0, 0] <= LEAN_CAP, finish, again, lean, given)


def solution(mesh):
    grid = Mesh(mesh.devices.reshape(PLANES, QUARTERS, 4, 2), ALL_AXES)
    placed = (
        P(None, ALL_AXES, None),
        P(ALL_AXES),
        P(),
        P(None, ("x", "c")),
        P(None, ("x", "c")),
        P(("z", "y"), ("x", "c")),
    )
    return jax.shard_map(
        on_device,
        mesh=grid,
        in_specs=placed,
        out_specs=(P(None, ALL_AXES, None), P(None, ("x", "c")), P(None, ("x", "c"))),
        check_vma=False,
    )
```

```python
import functools

import jax
import jax.numpy as jnp
from jax import lax
from jax.experimental import pallas as pl
from jax.experimental.pallas import tpu as pltpu
from jax.sharding import Mesh, PartitionSpec as P

PLANES = 8
QUARTERS = 4
PEERS = 32
PLANE_ROWS = 1024
WIDTH = 128
CHUNKS = 2
PER_GROUP = 16
GROUPS = WIDTH // PER_GROUP
STREAMS = 5
OWN_ROWS = 32
DATA_ROWS = STREAMS * OWN_ROWS
NOTE_ROWS = 16
TAPS = 128
SHORT = 7
SPAN = 2 * TAPS
SLABS = PLANE_ROWS // TAPS
FULL_CAP = 256
LEAN_CAP = 160
RING_B = False
RING_BACK_A = False
ALL_AXES = ("z", "y", "x", "c")
IN_PLANE = ("y", "x", "c")
BF = jnp.bfloat16
F32 = jnp.float32
I32 = jnp.int32


def iota(shape, dim):
    return lax.broadcasted_iota(I32, shape, dim)


def one_hot(mask):
    return jnp.where(mask, 1.0, 0.0).astype(BF)


def call(body, out_shape, n_in_smem=0, n_in=0, n_any=0, scratch=(), flops=0, bytes_accessed=0):
    smem = [pl.BlockSpec(memory_space=pltpu.SMEM)] * n_in_smem
    vmem = [pl.BlockSpec(memory_space=pltpu.VMEM)] * n_in
    outs = jax.tree.map(lambda s: pl.BlockSpec(memory_space=pltpu.VMEM), out_shape)
    return pl.pallas_call(
        body,
        out_shape=out_shape,
        in_specs=smem + vmem + [pl.BlockSpec(memory_space=pl.ANY)] * n_any,
        out_specs=outs,
        scratch_shapes=list(scratch),
        compiler_params=pltpu.CompilerParams(vmem_limit_bytes=48 * 2**20),
        cost_estimate=pl.CostEstimate(
            flops=flops, bytes_accessed=bytes_accessed, transcendentals=0
        ),
    )


def peer_column(peer, chunk):
    quarter, column = peer // 8, peer % 8
    return (column * QUARTERS + quarter) * CHUNKS * WIDTH + chunk * WIDTH


def split_kernel(chunk, loaded_ref, note_ref, after_ref, out_ref):
    for peer in range(PEERS):
        first = peer_column(peer, chunk)
        for stream in range(STREAMS):
            out_ref[peer, stream * OWN_ROWS : (stream + 1) * OWN_ROWS, :] = loaded_ref[
                stream, :, first : first + WIDTH
            ]
        out_ref[peer, DATA_ROWS:, :] = note_ref[...]


def split_channels(loaded, chunk, note, after):
    return call(
        functools.partial(split_kernel, chunk),
        jax.ShapeDtypeStruct((PEERS, DATA_ROWS + NOTE_ROWS, WIDTH), BF),
        n_in=2,
        n_any=1,
        bytes_accessed=4 * 2**20,
    )(loaded, note, after)


def write_note(numbers):
    high, low = numbers // 128, numbers % 128
    digits = jnp.concatenate([high, low], axis=0).astype(BF)
    return jnp.pad(digits, ((0, NOTE_ROWS - digits.shape[0]), (0, WIDTH - digits.shape[1])))


def read_note(notes, rows, width):
    high = notes[:, DATA_ROWS : DATA_ROWS + rows, :width].astype(I32)
    low = notes[:, DATA_ROWS + rows : DATA_ROWS + 2 * rows, :width].astype(I32)
    return high * 128 + low


def merge_kernel(*refs):
    out_ref = refs[-1]
    for chunk in range(CHUNKS):
        for peer in range(PEERS):
            first = peer_column(peer, chunk)
            for stream in range(STREAMS):
                out_ref[stream, :, first : first + WIDTH] = refs[chunk][
                    peer, stream * OWN_ROWS : (stream + 1) * OWN_ROWS, :
                ]


def merge_channels(parts):
    return call(
        merge_kernel,
        jax.ShapeDtypeStruct((STREAMS, OWN_ROWS, PEERS * CHUNKS * WIDTH), BF),
        n_in=CHUNKS,
        bytes_accessed=6 * 2**20,
    )(*parts)


def pass_on_kernel(*refs):
    pass


def pass_on(value, *after):
    anywhere = pl.BlockSpec(memory_space=pl.ANY)
    return pl.pallas_call(
        pass_on_kernel,
        out_shape=jax.ShapeDtypeStruct(value.shape, value.dtype),
        in_specs=[anywhere] * (1 + len(after)),
        out_specs=anywhere,
        input_output_aliases={0: 0},
    )(value, *after)


def before_matrix():
    shape = (PLANE_ROWS, PLANE_ROWS)
    return one_hot(iota(shape, 0) < iota(shape, 1))


def sender_kernel(mine_ref, code_row_ref, code_col_ref):
    shape = (PLANES, PLANE_ROWS)
    target = mine_ref[...] // PLANE_ROWS
    match = target == iota(shape, 0)
    earlier = jnp.dot(one_hot(match), before_matrix(), preferred_element_type=F32)
    rank = jnp.sum(jnp.where(match, earlier, 0.0), axis=0, keepdims=True)
    code = target * FULL_CAP + rank.astype(I32)
    code_row_ref[...] = code
    tall = jnp.broadcast_to(code.astype(F32), (WIDTH, PLANE_ROWS))
    code_col_ref[...] = jnp.transpose(tall).astype(I32)


def sender_codes(mine):
    return call(
        sender_kernel,
        (
            jax.ShapeDtypeStruct((1, PLANE_ROWS), I32),
            jax.ShapeDtypeStruct((PLANE_ROWS, WIDTH), I32),
        ),
        n_in=1,
        flops=2 * 16 * 2**20,
        bytes_accessed=2**20,
    )(mine)


def receiver_kernel(here_ref, plan_ref, spot_row_ref, spot_col_ref, most_ref):
    plane = here_ref[0]
    every = plan_ref[...]
    goals = every // PLANE_ROWS
    arriving = goals == plane
    ranks = jnp.dot(one_hot(arriving), before_matrix(), preferred_element_type=F32)
    ranks = jnp.where(arriving, ranks.astype(I32), -1)
    local = every % PLANE_ROWS
    rows = iota((FULL_CAP, PLANE_ROWS), 0)
    kind = iota((8, PLANE_ROWS), 0)
    for step in range(PLANES):
        source = (plane + PLANES - step) % PLANES
        held = one_hot(rows == ranks[step : step + 1, :])
        spot = local[step : step + 1, :]
        parts = jnp.where(kind == 0, spot // 32, jnp.where(kind == 1, spot % 32, 1))
        read = lax.dot_general(
            parts.astype(F32).astype(BF),
            held,
            (((1,), (1,)), ((), ())),
            preferred_element_type=F32,
        )
        value = read[0:1] * 32.0 + read[1:2] + (read[2:3] - 1.0) * 4096.0
        spot_row_ref[pl.ds(source, 1), :] = value.astype(I32)
        tall = jnp.broadcast_to(value, (WIDTH, FULL_CAP))
        spot_col_ref[source] = jnp.transpose(tall).astype(I32)
    most = jnp.zeros((PLANES, 1), I32)
    for goal in range(PLANES):
        found = jnp.sum((goals == goal).astype(I32), axis=1, keepdims=True)
        most = jnp.maximum(most, found)
    most_ref[...] = jnp.broadcast_to(jnp.max(most, axis=0, keepdims=True), (8, 128))


def receiver_spots(here, plan):
    return call(
        receiver_kernel,
        (
            jax.ShapeDtypeStruct((PLANES, FULL_CAP), I32),
            jax.ShapeDtypeStruct((PLANES, FULL_CAP, WIDTH), I32),
            jax.ShapeDtypeStruct((8, 128), I32),
        ),
        n_in_smem=1,
        n_in=1,
        flops=2 * 64 * 2**20,
        bytes_accessed=2 * 2**20,
    )(here, plan)


def parcels_shape(cap, ring):
    if ring:
        return tuple(jax.ShapeDtypeStruct((STREAMS, cap, WIDTH), BF) for _ in range(PLANES))
    return (jax.ShapeDtypeStruct((PLANES, STREAMS, cap, WIDTH), BF),)


def take_parcels(refs, ring):
    count = PLANES if ring else 1
    return (refs[:PLANES] if ring else [refs[0].at[p] for p in range(PLANES)]), refs[count:]


def fetch_parcels(parcels, field_ref, cap, sems):
    copies = []
    for step in range(PLANES):
        for stream in range(STREAMS):
            copies.append(
                pltpu.make_async_copy(
                    parcels[step].at[stream],
                    field_ref.at[
                        pl.ds(step * cap, cap), pl.ds(stream * WIDTH, WIDTH)
                    ],
                    sems.at[step * STREAMS + stream],
                )
            )
            copies[-1].start()
    return copies


def plane_at(plane, step, ring, way=1):
    return (plane + PLANES + way * step) % PLANES if ring else step


def pack_kernel(cap, ring, here_ref, rows_ref, code_ref, after_ref, *rest):
    outs, (field_ref, pick_ref) = take_parcels(rest, ring)
    for stream in range(STREAMS):
        field_ref[:, stream * WIDTH : (stream + 1) * WIDTH] = rows_ref[
            :, stream * OWN_ROWS : (stream + 1) * OWN_ROWS, :
        ].reshape(PLANE_ROWS, WIDTH)
    code = code_ref[...]
    for step in range(PLANES):
        goal = plane_at(here_ref[0], step, ring)
        wanted = iota((cap, PLANE_ROWS), 0) + goal * FULL_CAP
        pick_ref[step * cap : (step + 1) * cap, :] = one_hot(wanted == code)
    for step in range(PLANES):
        packed = jnp.dot(
            pick_ref[step * cap : (step + 1) * cap, :],
            field_ref[...],
            preferred_element_type=F32,
        ).astype(BF)
        for stream in range(STREAMS):
            outs[step][stream] = packed[:, stream * WIDTH : (stream + 1) * WIDTH]


def pack(cap, ring, here, rows, code_row, after):
    return list(call(
        functools.partial(pack_kernel, cap, ring),
        parcels_shape(cap, ring),
        n_in_smem=1,
        n_in=2,
        n_any=1,
        scratch=[
            pltpu.VMEM((PLANE_ROWS, STREAMS * WIDTH), BF),
            pltpu.VMEM((PLANES * cap, PLANE_ROWS), BF),
        ],
        flops=2 * PLANES * cap * PLANE_ROWS * STREAMS * WIDTH,
        bytes_accessed=3 * 2**20,
    )(here, rows, code_row, after))


def unpack_kernel(cap, ring, here_ref, code_ref, *rest):
    parcels, (*_, out_ref, field_ref, pick_ref) = take_parcels(rest, ring)
    code = code_ref[...]
    blocks = -(-cap // WIDTH)
    for step in range(PLANES):
        goal = plane_at(here_ref[0], step, ring)
        for stream in range(STREAMS):
            field_ref[
                step * cap : (step + 1) * cap, stream * WIDTH : (stream + 1) * WIDTH
            ] = parcels[step][stream]
        for block in range(blocks):
            first = block * WIDTH
            width = min(WIDTH, cap - first)
            wanted = iota((PLANE_ROWS, WIDTH), 1) + (goal * FULL_CAP + first)
            pick_ref[:, step * cap + first : step * cap + first + width] = one_hot(
                wanted == code
            )[:, :width]
    for part in range(4):
        rows = PLANE_ROWS // 4
        found = jnp.dot(
            pick_ref[part * rows : (part + 1) * rows, :],
            field_ref[...],
            preferred_element_type=F32,
        ).astype(BF)
        peers = rows // OWN_ROWS
        for stream in range(STREAMS):
            out_ref[
                part * peers : (part + 1) * peers,
                stream * OWN_ROWS : (stream + 1) * OWN_ROWS,
                :,
            ] = found[:, stream * WIDTH : (stream + 1) * WIDTH].reshape(
                peers, OWN_ROWS, WIDTH
            )


def unpack(cap, ring, here, code_col, parcels, *after):
    return call(
        functools.partial(unpack_kernel, cap, ring),
        jax.ShapeDtypeStruct((PEERS, STREAMS * OWN_ROWS, WIDTH), BF),
        n_in_smem=1,
        n_in=1 + len(parcels),
        n_any=len(after),
        scratch=[
            pltpu.VMEM((PLANES * cap, STREAMS * WIDTH), BF),
            pltpu.VMEM((PLANE_ROWS, PLANES * cap), BF),
        ],
        flops=2 * PLANES * cap * PLANE_ROWS * STREAMS * WIDTH,
        bytes_accessed=3 * 2**20,
    )(here, code_col, *parcels, *after)


def starts_of(rows, lengths_ref):
    first, second, third = lengths_ref[0], lengths_ref[1], lengths_ref[2]
    total = jnp.where(rows >= first, first, 0)
    total = total + jnp.where(rows >= first + second, second, 0)
    return total + jnp.where(rows >= first + second + third, third, 0)


def band(base_row, rows):
    wide = jnp.broadcast_to(base_row, (rows, SPAN))
    return pltpu.roll(wide, 0, 1, stride=1, stride_axis=0).astype(BF)


def forward_mask(anchor, lengths_ref):
    shape = (TAPS, SPAN)
    begin = starts_of(anchor + iota(shape, 0), lengths_ref)
    return anchor - TAPS + iota(shape, 1) >= begin


def backward_mask(anchor, rows, lengths_ref):
    shape = (rows, SPAN)
    begin = starts_of(anchor + iota(shape, 1), lengths_ref)
    return anchor + iota(shape, 0) >= begin


def by_group(stacked, rows):
    lane_group = iota((rows, WIDTH), 1) // PER_GROUP
    total = stacked[0:rows]
    for group in range(1, GROUPS):
        total = jnp.where(
            lane_group == group, stacked[group * rows : (group + 1) * rows], total
        )
    return total


def short_sum(window, weights, anchor, rows, lengths_ref):
    targets = anchor + iota((rows, WIDTH), 0)
    reach = targets - starts_of(targets, lengths_ref)
    total = jnp.zeros((rows, WIDTH), F32)
    for lag in range(SHORT):
        source = window[8:] if lag == 0 else pltpu.roll(window, lag, 0)[8:]
        total = total + jnp.where(reach >= lag, source * weights[lag : lag + 1, :], 0.0)
    return total


def context_kernel(
    cap, ring, here_ref, lengths_ref, spot_ref, cot_ref, se_ref, back_ref, *rest
):
    parcels, rest = take_parcels(rest, ring)
    ctx_ref, ahead_ref, behind_ref, field_ref, pick_ref, sems = rest[1:]
    copies = fetch_parcels(parcels, field_ref, cap, sems)
    plane = here_ref[0]
    for step in range(PLANES):
        source = plane_at(plane, step, ring, -1)
        spot = spot_ref[pl.ds(source, 1), :][:, :cap]
        pick_ref[:, step * cap : (step + 1) * cap] = one_hot(
            iota((PLANE_ROWS, cap), 0) == spot
        )
    for copy in copies:
        copy.wait()
    for part in range(4):
        rows = PLANE_ROWS // 4
        found = jnp.dot(
            pick_ref[part * rows : (part + 1) * rows, :],
            field_ref[...],
            preferred_element_type=F32,
        ).astype(BF)
        for stream in range(STREAMS):
            ctx_ref[stream, part * rows : (part + 1) * rows, :] = found[
                :, stream * WIDTH : (stream + 1) * WIDTH
            ]
    weights = se_ref[...]
    anchor = plane * PLANE_ROWS
    tail = PLANE_ROWS - TAPS
    low = tail - 16
    inner = (ctx_ref[1, low:, :].astype(F32) * ctx_ref[2, low:, :].astype(F32)).astype(BF)
    window = inner.astype(F32)[8:]
    mix = short_sum(window, weights, anchor + tail, TAPS, lengths_ref)
    middle = (ctx_ref[0, tail:, :].astype(F32) * mix).astype(BF)
    ahead_ref[0:TAPS, :] = (
        ctx_ref[4, tail:, :].astype(F32) * middle.astype(F32)
    ).astype(BF)
    ahead_ref[TAPS : TAPS + 16, :] = inner[TAPS:]
    grad_two = (
        cot_ref[0:SPAN, :].astype(F32) * ctx_ref[3, 0:SPAN, :].astype(F32)
    ).astype(BF)
    behind_ref[0:TAPS, :] = grad_two[0:TAPS]
    mask = backward_mask(anchor, 16, lengths_ref)
    tiles = []
    for group in range(GROUPS):
        tile = band(back_ref[group : group + 1, :], 16).astype(F32)
        tiles.append(jnp.where(mask, tile, 0.0).astype(BF))
    stacked = jnp.dot(
        jnp.concatenate(tiles, axis=0), grad_two, preferred_element_type=F32
    )
    grad_inner = by_group(stacked, 16)
    grad_middle = grad_inner * ctx_ref[4, 0:16, :].astype(F32)
    behind_ref[TAPS : TAPS + 16, :] = (
        grad_middle * ctx_ref[0, 0:16, :].astype(F32)
    ).astype(BF)


def context(cap, ring, here, lengths, spot_row, cot, weights, back_base, parcels, after):
    return call(
        functools.partial(context_kernel, cap, ring),
        (
            jax.ShapeDtypeStruct((STREAMS, PLANE_ROWS, WIDTH), BF),
            jax.ShapeDtypeStruct((TAPS + 16, WIDTH), BF),
            jax.ShapeDtypeStruct((TAPS + 16, WIDTH), BF),
        ),
        n_in_smem=2,
        n_in=4,
        n_any=len(parcels) + 1,
        scratch=[
            pltpu.VMEM((PLANES * cap, STREAMS * WIDTH), BF),
            pltpu.VMEM((PLANE_ROWS, PLANES * cap), BF),
            pltpu.SemaphoreType.DMA((PLANES * STREAMS,)),
        ],
        flops=2 * PLANES * cap * PLANE_ROWS * STREAMS * WIDTH,
        bytes_accessed=3 * 2**20,
    )(here, lengths, spot_row, cot, weights, back_base, *parcels, after)


def operator_kernel(
    cap, ring, here_ref, lengths_ref, spot_ref, cot_ref, se_ref, fore_ref, back_ref,
    ctx_ref, ahead_ref, behind_ref, after_ref, *rest,
):
    outs, rest = take_parcels(rest, ring)
    (
        long_ref, short_ref, one_ref, mix_ref, mid_ref, two_ref, gtwo_ref, gone_ref,
        fore_tile_ref, back_tile_ref, grid_ref, grads_ref, pick_ref,
    ) = rest
    plane = here_ref[0]
    origin = plane * PLANE_ROWS
    weights = se_ref[...]
    for group in range(GROUPS):
        at = slice(group * TAPS, (group + 1) * TAPS)
        fore_tile_ref[at, :] = band(fore_ref[group : group + 1, :], TAPS)
        back_tile_ref[at, :] = band(back_ref[group : group + 1, :], TAPS)
    for step in range(PLANES):
        source = plane_at(plane, step, ring, -1)
        for block in range(PLANE_ROWS // WIDTH):
            spots = spot_ref[source, :cap, :]
            pick_ref[
                step * cap : (step + 1) * cap, block * WIDTH : (block + 1) * WIDTH
            ] = one_hot(iota((cap, WIDTH), 1) + block * WIDTH == spots)
    one_ref[0:8, :] = ahead_ref[TAPS : TAPS + 16, :].astype(F32)[8:]
    two_ref[0:TAPS, :] = ahead_ref[0:TAPS, :]
    gtwo_ref[PLANE_ROWS:, :] = behind_ref[0:TAPS, :]
    gone_ref[PLANE_ROWS:, :] = behind_ref[TAPS : TAPS + 16, :].astype(F32)[0:8]
    grid_ref[...] = jnp.zeros_like(grid_ref)
    short_ref[...] = jnp.zeros_like(short_ref)

    def first_pass(slab, carry):
        at = pl.multiple_of(slab * TAPS, TAPS)
        here = pl.ds(at, TAPS)
        inner = (ctx_ref[1, here, :].astype(F32) * ctx_ref[2, here, :].astype(F32)).astype(BF)
        one_ref[pl.ds(at + 8, TAPS), :] = inner.astype(F32)
        window = one_ref[pl.ds(at, TAPS + 8), :]
        mix = short_sum(window, weights, origin + at, TAPS, lengths_ref)
        mix_ref[here, :] = mix
        middle = (ctx_ref[0, here, :].astype(F32) * mix).astype(BF)
        mid_ref[here, :] = middle
        two_ref[pl.ds(at + TAPS, TAPS), :] = (
            ctx_ref[4, here, :].astype(F32) * middle.astype(F32)
        ).astype(BF)
        gtwo_ref[here, :] = (
            cot_ref[here, :].astype(F32) * ctx_ref[3, here, :].astype(F32)
        ).astype(BF)
        return carry

    lax.fori_loop(0, SLABS, first_pass, 0)
    lane_group = iota((TAPS, WIDTH), 1) // PER_GROUP

    def second_pass(slab, carry):
        at = pl.multiple_of(slab * TAPS, TAPS)
        here = pl.ds(at, TAPS)
        anchor = origin + at
        keep_fore = forward_mask(anchor, lengths_ref)
        keep_back = backward_mask(anchor, TAPS, lengths_ref)
        fore = one_hot(keep_fore)
        back = one_hot(keep_back)
        past = two_ref[pl.ds(at, SPAN), :]
        later = gtwo_ref[pl.ds(at, SPAN), :]
        fore_tiles = jnp.concatenate(
            [fore_tile_ref[g * TAPS : (g + 1) * TAPS, :] * fore for g in range(GROUPS)], axis=0
        )
        long_mix = by_group(jnp.dot(fore_tiles, past, preferred_element_type=F32), TAPS)
        back_tiles = jnp.concatenate(
            [back_tile_ref[g * TAPS : (g + 1) * TAPS, :] * back for g in range(GROUPS)], axis=0
        )
        grad_inner = by_group(jnp.dot(back_tiles, later, preferred_element_type=F32), TAPS)
        cot = cot_ref[here, :].astype(F32)
        grads_ref[here, 3 * WIDTH : 4 * WIDTH] = (cot * long_mix).astype(BF)
        grads_ref[here, 4 * WIDTH : 5 * WIDTH] = (
            grad_inner * mid_ref[here, :].astype(F32)
        ).astype(BF)
        grad_middle = grad_inner * ctx_ref[4, here, :].astype(F32)
        mix = mix_ref[here, :]
        grads_ref[here, 0:WIDTH] = (grad_middle * mix).astype(BF)
        grad_one = (grad_middle * ctx_ref[0, here, :].astype(F32)).astype(BF).astype(F32)
        gone_ref[here, :] = grad_one
        window = one_ref[pl.ds(at, TAPS + 8), :]
        targets = anchor + iota((TAPS, WIDTH), 0)
        reach = targets - starts_of(targets, lengths_ref)
        for lag in range(SHORT):
            source = window[8:] if lag == 0 else pltpu.roll(window, lag, 0)[8:]
            terms = jnp.where(reach >= lag, source * grad_one, 0.0)
            short_ref[lag : lag + 1, :] += jnp.sum(terms, axis=0, keepdims=True)
        now = later[0:TAPS]
        split = jnp.concatenate(
            [now * one_hot(lane_group == g) for g in range(GROUPS)], axis=0
        )
        grid = lax.dot_general(
            split, past, (((1,), (1,)), ((), ())), preferred_element_type=F32
        )
        for g in range(GROUPS):
            rows = slice(g * TAPS, (g + 1) * TAPS)
            grid_ref[rows, :] += jnp.where(keep_fore, grid[rows], 0.0)
        return carry

    lax.fori_loop(0, SLABS, second_pass, 0)

    def third_pass(slab, carry):
        at = pl.multiple_of(slab * TAPS, TAPS)
        here = pl.ds(at, TAPS)
        window = gone_ref[pl.ds(at, TAPS + 8), :]
        rows = origin + at + iota((TAPS, WIDTH), 0)
        total = jnp.zeros((TAPS, WIDTH), F32)
        for lag in range(SHORT):
            later = window if lag == 0 else pltpu.roll(window, TAPS + 8 - lag, 0)
            keep = rows >= starts_of(rows + lag, lengths_ref)
            total = total + jnp.where(
                keep, later[0:TAPS] * weights[lag : lag + 1, :], 0.0
            )
        grad_inner = total.astype(BF).astype(F32)
        grads_ref[here, WIDTH : 2 * WIDTH] = (
            grad_inner * ctx_ref[2, here, :].astype(F32)
        ).astype(BF)
        grads_ref[here, 2 * WIDTH : 3 * WIDTH] = (
            grad_inner * ctx_ref[1, here, :].astype(F32)
        ).astype(BF)
        return carry

    lax.fori_loop(0, SLABS, third_pass, 0)
    for step in range(PLANES):
        packed = jnp.dot(
            pick_ref[step * cap : (step + 1) * cap, :],
            grads_ref[...],
            preferred_element_type=F32,
        ).astype(BF)
        for stream in range(STREAMS):
            outs[step][stream] = packed[:, stream * WIDTH : (stream + 1) * WIDTH]
    for group in range(GROUPS):
        total = jnp.zeros((8, SPAN), F32)
        for block in range(TAPS // 8):
            first = group * TAPS + block * 8
            piece = grid_ref[first : first + 8, :]
            piece = jnp.where(in_band(block), piece, 0.0)
            total = total + (piece if block == 0 else pltpu.roll(piece, SPAN - 8 * block, 1))
        line = total[0:1]
        for row in range(1, 8):
            line = line + pltpu.roll(total, SPAN - row, 1)[row : row + 1]
        long_ref[group : group + 1, :] = line


def in_band(block):
    lag = block * 8 + iota((8, SPAN), 0) + TAPS - iota((8, SPAN), 1)
    return (lag >= 0) & (lag < TAPS)


def operators(
    cap, ring, here, lengths, spot_col, cot, weights, fore_base, back_base, ctx, ahead, behind, after
):
    dense = PLANE_ROWS * WIDTH
    return call(
        functools.partial(operator_kernel, cap, ring),
        parcels_shape(cap, ring)
        + (
            jax.ShapeDtypeStruct((GROUPS, SPAN), F32),
            jax.ShapeDtypeStruct((8, WIDTH), F32),
        ),
        n_in_smem=2,
        n_in=8,
        n_any=1,
        scratch=[
            pltpu.VMEM((PLANE_ROWS + 8, WIDTH), F32),
            pltpu.VMEM((PLANE_ROWS, WIDTH), F32),
            pltpu.VMEM((PLANE_ROWS, WIDTH), BF),
            pltpu.VMEM((PLANE_ROWS + TAPS, WIDTH), BF),
            pltpu.VMEM((PLANE_ROWS + TAPS, WIDTH), BF),
            pltpu.VMEM((PLANE_ROWS + 8, WIDTH), F32),
            pltpu.VMEM((GROUPS * TAPS, SPAN), BF),
            pltpu.VMEM((GROUPS * TAPS, SPAN), BF),
            pltpu.VMEM((GROUPS * TAPS, SPAN), F32),
            pltpu.VMEM((PLANE_ROWS, STREAMS * WIDTH), BF),
            pltpu.VMEM((PLANES * cap, PLANE_ROWS), BF),
        ],
        flops=2 * dense * (PLANES * cap * STREAMS + 3 * GROUPS * SPAN),
        bytes_accessed=6 * 2**20,
    )(here, lengths, spot_col, cot, weights, fore_base, back_base, ctx, ahead, behind, after)


def around(value, step, axis, length):
    return lax.ppermute(value, axis, [(i, (i + step) % length) for i in range(length)])


def onward(value, step):
    pairs = [(i, i + step) for i in range(PLANES) if 0 <= i + step < PLANES]
    return lax.ppermute(value, "z", pairs)


def swap_in_plane(value):
    return lax.all_to_all(value, IN_PLANE, 0, 0, tiled=True)


def in_order(part, axis, length, pieces=None):
    at = lax.axis_index(axis)
    parts = [pieces[s] if pieces else part for s in range(length)]
    parts = parts[:1] + [around(parts[s], s, axis, length) for s in range(1, length)]
    turned = jnp.concatenate(
        [parts[(length - 1 - k) % length] for k in range(2 * length - 1)], axis=0
    )
    rows = parts[0].shape[0]
    return lax.dynamic_slice_in_dim(turned, (length - 1 - at) * rows, length * rows, 0)


def cotangent_of_plane(grad_out):
    quarter = lax.axis_index("y")
    width = CHUNKS * WIDTH
    pieces = [
        lax.dynamic_slice_in_dim(grad_out, ((quarter + s) % QUARTERS) * width, width, 1)
        for s in range(QUARTERS)
    ]
    return in_order(None, "y", QUARTERS, pieces)


def filters_of_device(se_filter, mr_filter):
    quarter = lax.axis_index("y")
    groups = CHUNKS * GROUPS
    short_taps = lax.dynamic_slice_in_dim(se_filter, quarter * groups, groups, 1)
    short_taps = jnp.repeat(short_taps.astype(F32), PER_GROUP, axis=1)
    short_taps = jnp.concatenate([short_taps, jnp.zeros((1, CHUNKS * WIDTH), F32)], axis=0)
    taps = lax.dynamic_slice_in_dim(mr_filter, quarter * groups, groups, 1)
    taps = jnp.transpose(taps.astype(F32))
    fore_base = jnp.pad(taps[:, ::-1], ((0, 0), (1, TAPS - 1)))
    back_base = jnp.pad(taps, ((0, 0), (0, TAPS)))
    return short_taps, fore_base, back_base


def filter_sums(long_parts, short_parts):
    groups = CHUNKS * GROUPS
    long_here = jnp.concatenate(long_parts, axis=0)[:, 1 : TAPS + 1][:, ::-1]
    short_here = jnp.concatenate(short_parts, axis=1).reshape(8, groups, PER_GROUP).sum(axis=2)
    together = jnp.concatenate(
        [long_here, jnp.pad(short_here, ((0, 0), (0, TAPS - groups)))], axis=0
    )
    return jnp.sum(in_order(together[None], "z", PLANES), axis=0)


def filter_totals(sums):
    groups = CHUNKS * GROUPS
    summed = lax.all_gather(sums, "y") * (PLANES * PLANE_ROWS * PER_GROUP) ** -0.5
    long_total = jnp.transpose(summed[:, :groups, :], (2, 0, 1)).reshape(TAPS, QUARTERS * groups)
    short_total = jnp.transpose(summed[:, groups : groups + SHORT, :groups], (1, 0, 2)).reshape(
        SHORT, QUARTERS * groups
    )
    return short_total, long_total


def exchange_and_operate(cap, here, lengths, codes, spots, cot, filters, rows, sent_a):
    short_taps, fore_base, back_base = filters
    lanes = [slice(c * WIDTH, (c + 1) * WIDTH) for c in range(CHUNKS)]
    mine = [slice(c * GROUPS, (c + 1) * GROUPS) for c in range(CHUNKS)]

    def exchange(ring, parts, way):
        if not ring:
            return [lax.all_to_all(parts[0], "z", 0, 0, tiled=True)]
        moved = {s: around(parts[s], way * s, "z", PLANES) for s in (1, 7, 4, 3, 5, 2, 6)}
        return [parts[0]] + [moved[s] for s in range(1, PLANES)]

    def arrive(ring, chunk, parcels, after):
        ctx, ahead, behind = context(
            cap, ring, here, lengths, spots[0], cot[:, lanes[chunk]],
            short_taps[:, lanes[chunk]], back_base[mine[chunk]], parcels, after,
        )
        return ctx, onward(ahead, 1), onward(behind, -1)

    def operate(ring, chunk, after, ctx, ahead, behind):
        *parcels, longs, shorts = operators(
            cap, ring, here, lengths, spots[1], cot[:, lanes[chunk]],
            short_taps[:, lanes[chunk]], fore_base[mine[chunk]], back_base[mine[chunk]],
            ctx, ahead, behind, after,
        )
        return parcels, longs, shorts

    if sent_a is None:
        sent_a = pack(cap, True, here, rows[0], codes[0], here)
    parcels_a = exchange(True, sent_a, 1)
    sent_b = pack(cap, RING_B, here, rows[1], codes[0], here)
    sent_b[0] = pass_on(sent_b[0], *parcels_a[1:], *spots, *filters)
    parcels_b = exchange(RING_B, sent_b, 1)
    arrived_a = arrive(True, 0, parcels_a, sent_b[0])
    arrived_b = arrive(RING_B, 1, parcels_b, arrived_a[0])
    made_a, long_a, short_a = operate(RING_BACK_A, 0, arrived_b[0], *arrived_a)
    made_a[0] = pass_on(made_a[0], *arrived_b[1:])
    returned_a = exchange(RING_BACK_A, made_a, -1)
    made_b, long_b, short_b = operate(True, 1, here, *arrived_b)
    sums = filter_sums([long_a, long_b], [short_a, short_b])
    made_b[4] = pass_on(made_b[4], returned_a[-1], sums)
    returned_b = exchange(True, made_b, -1)
    back_a = swap_in_plane(unpack(cap, RING_BACK_A, here, codes[1], returned_a, made_b[4]))
    back_b = swap_in_plane(unpack(cap, True, here, codes[1], returned_b, back_a))
    totals = filter_totals(sums)
    return (back_a, back_b), totals


def on_device(loaded, row_plan, lengths, se_filter, mr_filter, grad_out):
    here = lax.axis_index("z").astype(I32).reshape(1)
    own = row_plan.reshape(1, OWN_ROWS)
    rows_a = swap_in_plane(split_channels(loaded, 0, write_note(own), lengths))
    along = own
    for step in (4, 2, 1):
        along = jnp.concatenate([along, around(along, step, "z", PLANES)], axis=0)
    along = along.reshape(2, 2, 2, OWN_ROWS).transpose(2, 1, 0, 3).reshape(2, WIDTH)
    cot = cotangent_of_plane(grad_out)
    filters = filters_of_device(se_filter, mr_filter)
    mine = read_note(rows_a, 1, OWN_ROWS).reshape(1, PLANE_ROWS)
    codes = sender_codes(mine)
    sent_a = pack(LEAN_CAP, True, here, rows_a, codes[0], cot)
    rows_b = swap_in_plane(split_channels(loaded, 1, write_note(along), sent_a[1]))
    plan = read_note(rows_b, 2, WIDTH).reshape(PEERS, PLANES, OWN_ROWS)
    plan = jnp.transpose(plan, (1, 0, 2)).reshape(PLANES, PLANE_ROWS)
    spot_row, spot_col, most = receiver_spots(here, plan)
    given = (here, lengths, codes, (spot_row, spot_col), cot, filters, (rows_a, rows_b))
    lean = exchange_and_operate(LEAN_CAP, *given, sent_a)

    def finish(lean, given):
        return (merge_channels(lean[0]),) + lean[1]

    def again(lean, given):
        return finish(exchange_and_operate(FULL_CAP, *given, None), given)

    return lax.cond(most[0, 0] <= LEAN_CAP, finish, again, lean, given)


def solution(mesh):
    grid = Mesh(mesh.devices.reshape(PLANES, QUARTERS, 4, 2), ALL_AXES)
    placed = (
        P(None, ALL_AXES, None),
        P(ALL_AXES),
        P(),
        P(None, ("x", "c")),
        P(None, ("x", "c")),
        P(("z", "y"), ("x", "c")),
    )
    return jax.shard_map(
        on_device,
        mesh=grid,
        in_specs=placed,
        out_specs=(P(None, ALL_AXES, None), P(None, ("x", "c")), P(None, ("x", "c"))),
        check_vma=False,
    )
```

```python
import functools

import jax
import jax.numpy as jnp
from jax import lax
from jax.experimental import pallas as pl
from jax.experimental.pallas import tpu as pltpu
from jax.sharding import Mesh, PartitionSpec as P

PLANES = 8
QUARTERS = 4
PEERS = 32
PLANE_ROWS = 1024
WIDTH = 128
CHUNKS = 2
PER_GROUP = 16
GROUPS = WIDTH // PER_GROUP
STREAMS = 5
OWN_ROWS = 32
DATA_ROWS = STREAMS * OWN_ROWS
NOTE_ROWS = 16
TAPS = 128
SHORT = 7
SPAN = 2 * TAPS
SLABS = PLANE_ROWS // TAPS
FULL_CAP = 256
LEAN_CAP = 160
RING_B = False
RING_BACK_A = False
ALL_AXES = ("z", "y", "x", "c")
IN_PLANE = ("y", "x", "c")
BF = jnp.bfloat16
F32 = jnp.float32
I32 = jnp.int32


def iota(shape, dim):
    return lax.broadcasted_iota(I32, shape, dim)


def one_hot(mask):
    return jnp.where(mask, 1.0, 0.0).astype(BF)


def call(body, out_shape, n_in_smem=0, n_in=0, n_any=0, outer=pl.ANY, scratch=(), flops=0, bytes_accessed=0):
    smem = [pl.BlockSpec(memory_space=pltpu.SMEM)] * n_in_smem
    vmem = [pl.BlockSpec(memory_space=pltpu.VMEM)] * n_in
    outs = jax.tree.map(lambda s: pl.BlockSpec(memory_space=pltpu.VMEM), out_shape)
    return pl.pallas_call(
        body,
        out_shape=out_shape,
        in_specs=smem + vmem + [pl.BlockSpec(memory_space=outer)] * n_any,
        out_specs=outs,
        scratch_shapes=list(scratch),
        compiler_params=pltpu.CompilerParams(vmem_limit_bytes=48 * 2**20),
        cost_estimate=pl.CostEstimate(
            flops=flops, bytes_accessed=bytes_accessed, transcendentals=0
        ),
    )


def peer_column(peer, chunk):
    quarter, column = peer // 8, peer % 8
    return (column * QUARTERS + quarter) * CHUNKS * WIDTH + chunk * WIDTH


def split_kernel(chunk, loaded_ref, note_ref, after_ref, out_ref):
    for peer in range(PEERS):
        first = peer_column(peer, chunk)
        for stream in range(STREAMS):
            out_ref[peer, stream * OWN_ROWS : (stream + 1) * OWN_ROWS, :] = loaded_ref[
                stream, :, first : first + WIDTH
            ]
        out_ref[peer, DATA_ROWS:, :] = note_ref[...]


def split_channels(loaded, chunk, note, after):
    return call(
        functools.partial(split_kernel, chunk),
        jax.ShapeDtypeStruct((PEERS, DATA_ROWS + NOTE_ROWS, WIDTH), BF),
        n_in=2,
        n_any=1,
        bytes_accessed=4 * 2**20,
    )(loaded, note, after)


def write_note(numbers):
    high, low = numbers // 128, numbers % 128
    digits = jnp.concatenate([high, low], axis=0).astype(BF)
    return jnp.pad(digits, ((0, NOTE_ROWS - digits.shape[0]), (0, WIDTH - digits.shape[1])))


def read_note(notes, rows, width):
    high = notes[:, DATA_ROWS : DATA_ROWS + rows, :width].astype(I32)
    low = notes[:, DATA_ROWS + rows : DATA_ROWS + 2 * rows, :width].astype(I32)
    return high * 128 + low


def merge_kernel(*refs):
    out_ref = refs[-1]
    for chunk in range(CHUNKS):
        for peer in range(PEERS):
            first = peer_column(peer, chunk)
            for stream in range(STREAMS):
                out_ref[stream, :, first : first + WIDTH] = refs[chunk][
                    peer, stream * OWN_ROWS : (stream + 1) * OWN_ROWS, :
                ]


def merge_channels(parts):
    return call(
        merge_kernel,
        jax.ShapeDtypeStruct((STREAMS, OWN_ROWS, PEERS * CHUNKS * WIDTH), BF),
        n_in=CHUNKS,
        bytes_accessed=6 * 2**20,
    )(*parts)


def pass_on_kernel(*refs):
    pass


def pass_on(value, *after):
    anywhere = pl.BlockSpec(memory_space=pl.ANY)
    return pl.pallas_call(
        pass_on_kernel,
        out_shape=jax.ShapeDtypeStruct(value.shape, value.dtype),
        in_specs=[anywhere] * (1 + len(after)),
        out_specs=anywhere,
        input_output_aliases={0: 0},
    )(value, *after)


def before_matrix():
    shape = (PLANE_ROWS, PLANE_ROWS)
    return one_hot(iota(shape, 0) < iota(shape, 1))


def sender_kernel(mine_ref, code_row_ref, code_col_ref):
    shape = (PLANES, PLANE_ROWS)
    target = mine_ref[...] // PLANE_ROWS
    match = target == iota(shape, 0)
    earlier = jnp.dot(one_hot(match), before_matrix(), preferred_element_type=F32)
    rank = jnp.sum(jnp.where(match, earlier, 0.0), axis=0, keepdims=True)
    code = target * FULL_CAP + rank.astype(I32)
    code_row_ref[...] = code
    tall = jnp.broadcast_to(code.astype(F32), (WIDTH, PLANE_ROWS))
    code_col_ref[...] = jnp.transpose(tall).astype(I32)


def sender_codes(mine):
    return call(
        sender_kernel,
        (
            jax.ShapeDtypeStruct((1, PLANE_ROWS), I32),
            jax.ShapeDtypeStruct((PLANE_ROWS, WIDTH), I32),
        ),
        n_in=1,
        flops=2 * 16 * 2**20,
        bytes_accessed=2**20,
    )(mine)


def receiver_kernel(here_ref, plan_ref, spot_row_ref, spot_col_ref, most_ref):
    plane = here_ref[0]
    every = plan_ref[...]
    goals = every // PLANE_ROWS
    arriving = goals == plane
    ranks = jnp.dot(one_hot(arriving), before_matrix(), preferred_element_type=F32)
    ranks = jnp.where(arriving, ranks.astype(I32), -1)
    local = every % PLANE_ROWS
    rows = iota((FULL_CAP, PLANE_ROWS), 0)
    kind = iota((8, PLANE_ROWS), 0)
    for step in range(PLANES):
        source = (plane + PLANES - step) % PLANES
        held = one_hot(rows == ranks[step : step + 1, :])
        spot = local[step : step + 1, :]
        parts = jnp.where(kind == 0, spot // 32, jnp.where(kind == 1, spot % 32, 1))
        read = lax.dot_general(
            parts.astype(F32).astype(BF),
            held,
            (((1,), (1,)), ((), ())),
            preferred_element_type=F32,
        )
        value = read[0:1] * 32.0 + read[1:2] + (read[2:3] - 1.0) * 4096.0
        spot_row_ref[pl.ds(source, 1), :] = value.astype(I32)
        tall = jnp.broadcast_to(value, (WIDTH, FULL_CAP))
        spot_col_ref[source] = jnp.transpose(tall).astype(I32)
    most = jnp.zeros((PLANES, 1), I32)
    for goal in range(PLANES):
        found = jnp.sum((goals == goal).astype(I32), axis=1, keepdims=True)
        most = jnp.maximum(most, found)
    most_ref[...] = jnp.broadcast_to(jnp.max(most, axis=0, keepdims=True), (8, 128))


def receiver_spots(here, plan):
    return call(
        receiver_kernel,
        (
            jax.ShapeDtypeStruct((PLANES, FULL_CAP), I32),
            jax.ShapeDtypeStruct((PLANES, FULL_CAP, WIDTH), I32),
            jax.ShapeDtypeStruct((8, 128), I32),
        ),
        n_in_smem=1,
        n_in=1,
        flops=2 * 64 * 2**20,
        bytes_accessed=2 * 2**20,
    )(here, plan)


def parcels_shape(cap, ring):
    if ring:
        return tuple(jax.ShapeDtypeStruct((STREAMS, cap, WIDTH), BF) for _ in range(PLANES))
    return (jax.ShapeDtypeStruct((PLANES, STREAMS, cap, WIDTH), BF),)


def take_parcels(refs, ring):
    count = PLANES if ring else 1
    return (refs[:PLANES] if ring else [refs[0].at[p] for p in range(PLANES)]), refs[count:]


def fetch_parcels(parcels, field_ref, cap, sems):
    copies = []
    for step in range(PLANES):
        for stream in range(STREAMS):
            copies.append(
                pltpu.make_async_copy(
                    parcels[step].at[stream],
                    field_ref.at[
                        pl.ds(step * cap, cap), pl.ds(stream * WIDTH, WIDTH)
                    ],
                    sems.at[step * STREAMS + stream],
                )
            )
            copies[-1].start()
    return copies


def plane_at(plane, step, ring, way=1):
    return (plane + PLANES + way * step) % PLANES if ring else step


def pack_kernel(cap, ring, here_ref, rows_ref, code_ref, after_ref, *rest):
    outs, (field_ref, pick_ref) = take_parcels(rest, ring)
    for stream in range(STREAMS):
        field_ref[:, stream * WIDTH : (stream + 1) * WIDTH] = rows_ref[
            :, stream * OWN_ROWS : (stream + 1) * OWN_ROWS, :
        ].reshape(PLANE_ROWS, WIDTH)
    code = code_ref[...]
    for step in range(PLANES):
        goal = plane_at(here_ref[0], step, ring)
        wanted = iota((cap, PLANE_ROWS), 0) + goal * FULL_CAP
        pick_ref[step * cap : (step + 1) * cap, :] = one_hot(wanted == code)
    for step in range(PLANES):
        packed = jnp.dot(
            pick_ref[step * cap : (step + 1) * cap, :],
            field_ref[...],
            preferred_element_type=F32,
        ).astype(BF)
        for stream in range(STREAMS):
            outs[step][stream] = packed[:, stream * WIDTH : (stream + 1) * WIDTH]


def pack(cap, ring, here, rows, code_row, after):
    return list(call(
        functools.partial(pack_kernel, cap, ring),
        parcels_shape(cap, ring),
        n_in_smem=1,
        n_in=2,
        n_any=1,
        scratch=[
            pltpu.VMEM((PLANE_ROWS, STREAMS * WIDTH), BF),
            pltpu.VMEM((PLANES * cap, PLANE_ROWS), BF),
        ],
        flops=2 * PLANES * cap * PLANE_ROWS * STREAMS * WIDTH,
        bytes_accessed=3 * 2**20,
    )(here, rows, code_row, after))


def unpack_kernel(cap, ring, here_ref, code_ref, *rest):
    parcels, (*_, out_ref, field_ref, pick_ref) = take_parcels(rest, ring)
    code = code_ref[...]
    blocks = -(-cap // WIDTH)
    for step in range(PLANES):
        goal = plane_at(here_ref[0], step, ring)
        for stream in range(STREAMS):
            field_ref[
                step * cap : (step + 1) * cap, stream * WIDTH : (stream + 1) * WIDTH
            ] = parcels[step][stream]
        for block in range(blocks):
            first = block * WIDTH
            width = min(WIDTH, cap - first)
            wanted = iota((PLANE_ROWS, WIDTH), 1) + (goal * FULL_CAP + first)
            pick_ref[:, step * cap + first : step * cap + first + width] = one_hot(
                wanted == code
            )[:, :width]
    for part in range(4):
        rows = PLANE_ROWS // 4
        found = jnp.dot(
            pick_ref[part * rows : (part + 1) * rows, :],
            field_ref[...],
            preferred_element_type=F32,
        ).astype(BF)
        peers = rows // OWN_ROWS
        for stream in range(STREAMS):
            out_ref[
                part * peers : (part + 1) * peers,
                stream * OWN_ROWS : (stream + 1) * OWN_ROWS,
                :,
            ] = found[:, stream * WIDTH : (stream + 1) * WIDTH].reshape(
                peers, OWN_ROWS, WIDTH
            )


def unpack(cap, ring, here, code_col, parcels, *after):
    return call(
        functools.partial(unpack_kernel, cap, ring),
        jax.ShapeDtypeStruct((PEERS, STREAMS * OWN_ROWS, WIDTH), BF),
        n_in_smem=1,
        n_in=1 + len(parcels),
        n_any=len(after),
        scratch=[
            pltpu.VMEM((PLANES * cap, STREAMS * WIDTH), BF),
            pltpu.VMEM((PLANE_ROWS, PLANES * cap), BF),
        ],
        flops=2 * PLANES * cap * PLANE_ROWS * STREAMS * WIDTH,
        bytes_accessed=3 * 2**20,
    )(here, code_col, *parcels, *after)


def starts_of(rows, lengths_ref):
    first, second, third = lengths_ref[0], lengths_ref[1], lengths_ref[2]
    total = jnp.where(rows >= first, first, 0)
    total = total + jnp.where(rows >= first + second, second, 0)
    return total + jnp.where(rows >= first + second + third, third, 0)


def band(base_row, rows):
    wide = jnp.broadcast_to(base_row, (rows, SPAN))
    return pltpu.roll(wide, 0, 1, stride=1, stride_axis=0).astype(BF)


def forward_mask(anchor, lengths_ref):
    shape = (TAPS, SPAN)
    begin = starts_of(anchor + iota(shape, 0), lengths_ref)
    return anchor - TAPS + iota(shape, 1) >= begin


def backward_mask(anchor, rows, lengths_ref):
    shape = (rows, SPAN)
    begin = starts_of(anchor + iota(shape, 1), lengths_ref)
    return anchor + iota(shape, 0) >= begin


def by_group(stacked, rows):
    lane_group = iota((rows, WIDTH), 1) // PER_GROUP
    total = stacked[0:rows]
    for group in range(1, GROUPS):
        total = jnp.where(
            lane_group == group, stacked[group * rows : (group + 1) * rows], total
        )
    return total


def short_sum(window, weights, anchor, rows, lengths_ref):
    targets = anchor + iota((rows, WIDTH), 0)
    reach = targets - starts_of(targets, lengths_ref)
    total = jnp.zeros((rows, WIDTH), F32)
    for lag in range(SHORT):
        source = window[8:] if lag == 0 else pltpu.roll(window, lag, 0)[8:]
        total = total + jnp.where(reach >= lag, source * weights[lag : lag + 1, :], 0.0)
    return total


def context_kernel(
    cap, ring, here_ref, lengths_ref, spot_ref, cot_ref, se_ref, back_ref, *rest
):
    parcels, rest = take_parcels(rest, ring)
    ctx_ref, ahead_ref, behind_ref, field_ref, pick_ref, sems = rest[1:]
    copies = fetch_parcels(parcels, field_ref, cap, sems)
    plane = here_ref[0]
    for step in range(PLANES):
        source = plane_at(plane, step, ring, -1)
        spot = spot_ref[pl.ds(source, 1), :][:, :cap]
        pick_ref[:, step * cap : (step + 1) * cap] = one_hot(
            iota((PLANE_ROWS, cap), 0) == spot
        )
    for copy in copies:
        copy.wait()
    for part in range(4):
        rows = PLANE_ROWS // 4
        found = jnp.dot(
            pick_ref[part * rows : (part + 1) * rows, :],
            field_ref[...],
            preferred_element_type=F32,
        ).astype(BF)
        for stream in range(STREAMS):
            ctx_ref[stream, part * rows : (part + 1) * rows, :] = found[
                :, stream * WIDTH : (stream + 1) * WIDTH
            ]
    weights = se_ref[...]
    anchor = plane * PLANE_ROWS
    tail = PLANE_ROWS - TAPS
    low = tail - 16
    inner = (ctx_ref[1, low:, :].astype(F32) * ctx_ref[2, low:, :].astype(F32)).astype(BF)
    window = inner.astype(F32)[8:]
    mix = short_sum(window, weights, anchor + tail, TAPS, lengths_ref)
    middle = (ctx_ref[0, tail:, :].astype(F32) * mix).astype(BF)
    ahead_ref[0:TAPS, :] = (
        ctx_ref[4, tail:, :].astype(F32) * middle.astype(F32)
    ).astype(BF)
    ahead_ref[TAPS : TAPS + 16, :] = inner[TAPS:]
    grad_two = (
        cot_ref[0:SPAN, :].astype(F32) * ctx_ref[3, 0:SPAN, :].astype(F32)
    ).astype(BF)
    behind_ref[0:TAPS, :] = grad_two[0:TAPS]
    mask = backward_mask(anchor, 16, lengths_ref)
    tiles = []
    for group in range(GROUPS):
        tile = band(back_ref[group : group + 1, :], 16).astype(F32)
        tiles.append(jnp.where(mask, tile, 0.0).astype(BF))
    stacked = jnp.dot(
        jnp.concatenate(tiles, axis=0), grad_two, preferred_element_type=F32
    )
    grad_inner = by_group(stacked, 16)
    grad_middle = grad_inner * ctx_ref[4, 0:16, :].astype(F32)
    behind_ref[TAPS : TAPS + 16, :] = (
        grad_middle * ctx_ref[0, 0:16, :].astype(F32)
    ).astype(BF)


def context(cap, ring, here, lengths, spot_row, cot, weights, back_base, parcels, after):
    return call(
        functools.partial(context_kernel, cap, ring),
        (
            jax.ShapeDtypeStruct((STREAMS, PLANE_ROWS, WIDTH), BF),
            jax.ShapeDtypeStruct((TAPS + 16, WIDTH), BF),
            jax.ShapeDtypeStruct((TAPS + 16, WIDTH), BF),
        ),
        n_in_smem=2,
        n_in=4,
        n_any=len(parcels) + 1,
        outer=pltpu.HBM,
        scratch=[
            pltpu.VMEM((PLANES * cap, STREAMS * WIDTH), BF),
            pltpu.VMEM((PLANE_ROWS, PLANES * cap), BF),
            pltpu.SemaphoreType.DMA((PLANES * STREAMS,)),
        ],
        flops=2 * PLANES * cap * PLANE_ROWS * STREAMS * WIDTH,
        bytes_accessed=3 * 2**20,
    )(here, lengths, spot_row, cot, weights, back_base, *parcels, after)


def operator_kernel(
    cap, ring, here_ref, lengths_ref, spot_ref, cot_ref, se_ref, fore_ref, back_ref,
    ctx_ref, ahead_ref, behind_ref, after_ref, *rest,
):
    outs, rest = take_parcels(rest, ring)
    (
        long_ref, short_ref, one_ref, mix_ref, mid_ref, two_ref, gtwo_ref, gone_ref,
        fore_tile_ref, back_tile_ref, grid_ref, grads_ref, pick_ref,
    ) = rest
    plane = here_ref[0]
    origin = plane * PLANE_ROWS
    weights = se_ref[...]
    for group in range(GROUPS):
        at = slice(group * TAPS, (group + 1) * TAPS)
        fore_tile_ref[at, :] = band(fore_ref[group : group + 1, :], TAPS)
        back_tile_ref[at, :] = band(back_ref[group : group + 1, :], TAPS)
    for step in range(PLANES):
        source = plane_at(plane, step, ring, -1)
        for block in range(PLANE_ROWS // WIDTH):
            spots = spot_ref[source, :cap, :]
            pick_ref[
                step * cap : (step + 1) * cap, block * WIDTH : (block + 1) * WIDTH
            ] = one_hot(iota((cap, WIDTH), 1) + block * WIDTH == spots)
    one_ref[0:8, :] = ahead_ref[TAPS : TAPS + 16, :].astype(F32)[8:]
    two_ref[0:TAPS, :] = ahead_ref[0:TAPS, :]
    gtwo_ref[PLANE_ROWS:, :] = behind_ref[0:TAPS, :]
    gone_ref[PLANE_ROWS:, :] = behind_ref[TAPS : TAPS + 16, :].astype(F32)[0:8]
    grid_ref[...] = jnp.zeros_like(grid_ref)
    short_ref[...] = jnp.zeros_like(short_ref)

    def first_pass(slab, carry):
        at = pl.multiple_of(slab * TAPS, TAPS)
        here = pl.ds(at, TAPS)
        inner = (ctx_ref[1, here, :].astype(F32) * ctx_ref[2, here, :].astype(F32)).astype(BF)
        one_ref[pl.ds(at + 8, TAPS), :] = inner.astype(F32)
        window = one_ref[pl.ds(at, TAPS + 8), :]
        mix = short_sum(window, weights, origin + at, TAPS, lengths_ref)
        mix_ref[here, :] = mix
        middle = (ctx_ref[0, here, :].astype(F32) * mix).astype(BF)
        mid_ref[here, :] = middle
        two_ref[pl.ds(at + TAPS, TAPS), :] = (
            ctx_ref[4, here, :].astype(F32) * middle.astype(F32)
        ).astype(BF)
        gtwo_ref[here, :] = (
            cot_ref[here, :].astype(F32) * ctx_ref[3, here, :].astype(F32)
        ).astype(BF)
        return carry

    lax.fori_loop(0, SLABS, first_pass, 0)
    lane_group = iota((TAPS, WIDTH), 1) // PER_GROUP

    def second_pass(slab, carry):
        at = pl.multiple_of(slab * TAPS, TAPS)
        here = pl.ds(at, TAPS)
        anchor = origin + at
        keep_fore = forward_mask(anchor, lengths_ref)
        keep_back = backward_mask(anchor, TAPS, lengths_ref)
        fore = one_hot(keep_fore)
        back = one_hot(keep_back)
        past = two_ref[pl.ds(at, SPAN), :]
        later = gtwo_ref[pl.ds(at, SPAN), :]
        fore_tiles = jnp.concatenate(
            [fore_tile_ref[g * TAPS : (g + 1) * TAPS, :] * fore for g in range(GROUPS)], axis=0
        )
        long_mix = by_group(jnp.dot(fore_tiles, past, preferred_element_type=F32), TAPS)
        back_tiles = jnp.concatenate(
            [back_tile_ref[g * TAPS : (g + 1) * TAPS, :] * back for g in range(GROUPS)], axis=0
        )
        grad_inner = by_group(jnp.dot(back_tiles, later, preferred_element_type=F32), TAPS)
        cot = cot_ref[here, :].astype(F32)
        grads_ref[here, 3 * WIDTH : 4 * WIDTH] = (cot * long_mix).astype(BF)
        grads_ref[here, 4 * WIDTH : 5 * WIDTH] = (
            grad_inner * mid_ref[here, :].astype(F32)
        ).astype(BF)
        grad_middle = grad_inner * ctx_ref[4, here, :].astype(F32)
        mix = mix_ref[here, :]
        grads_ref[here, 0:WIDTH] = (grad_middle * mix).astype(BF)
        grad_one = (grad_middle * ctx_ref[0, here, :].astype(F32)).astype(BF).astype(F32)
        gone_ref[here, :] = grad_one
        window = one_ref[pl.ds(at, TAPS + 8), :]
        targets = anchor + iota((TAPS, WIDTH), 0)
        reach = targets - starts_of(targets, lengths_ref)
        for lag in range(SHORT):
            source = window[8:] if lag == 0 else pltpu.roll(window, lag, 0)[8:]
            terms = jnp.where(reach >= lag, source * grad_one, 0.0)
            short_ref[lag : lag + 1, :] += jnp.sum(terms, axis=0, keepdims=True)
        now = later[0:TAPS]
        split = jnp.concatenate(
            [now * one_hot(lane_group == g) for g in range(GROUPS)], axis=0
        )
        grid = lax.dot_general(
            split, past, (((1,), (1,)), ((), ())), preferred_element_type=F32
        )
        for g in range(GROUPS):
            rows = slice(g * TAPS, (g + 1) * TAPS)
            grid_ref[rows, :] += jnp.where(keep_fore, grid[rows], 0.0)
        return carry

    lax.fori_loop(0, SLABS, second_pass, 0)

    def third_pass(slab, carry):
        at = pl.multiple_of(slab * TAPS, TAPS)
        here = pl.ds(at, TAPS)
        window = gone_ref[pl.ds(at, TAPS + 8), :]
        rows = origin + at + iota((TAPS, WIDTH), 0)
        total = jnp.zeros((TAPS, WIDTH), F32)
        for lag in range(SHORT):
            later = window if lag == 0 else pltpu.roll(window, TAPS + 8 - lag, 0)
            keep = rows >= starts_of(rows + lag, lengths_ref)
            total = total + jnp.where(
                keep, later[0:TAPS] * weights[lag : lag + 1, :], 0.0
            )
        grad_inner = total.astype(BF).astype(F32)
        grads_ref[here, WIDTH : 2 * WIDTH] = (
            grad_inner * ctx_ref[2, here, :].astype(F32)
        ).astype(BF)
        grads_ref[here, 2 * WIDTH : 3 * WIDTH] = (
            grad_inner * ctx_ref[1, here, :].astype(F32)
        ).astype(BF)
        return carry

    lax.fori_loop(0, SLABS, third_pass, 0)
    for step in range(PLANES):
        packed = jnp.dot(
            pick_ref[step * cap : (step + 1) * cap, :],
            grads_ref[...],
            preferred_element_type=F32,
        ).astype(BF)
        for stream in range(STREAMS):
            outs[step][stream] = packed[:, stream * WIDTH : (stream + 1) * WIDTH]
    for group in range(GROUPS):
        total = jnp.zeros((8, SPAN), F32)
        for block in range(TAPS // 8):
            first = group * TAPS + block * 8
            piece = grid_ref[first : first + 8, :]
            piece = jnp.where(in_band(block), piece, 0.0)
            total = total + (piece if block == 0 else pltpu.roll(piece, SPAN - 8 * block, 1))
        line = total[0:1]
        for row in range(1, 8):
            line = line + pltpu.roll(total, SPAN - row, 1)[row : row + 1]
        long_ref[group : group + 1, :] = line


def in_band(block):
    lag = block * 8 + iota((8, SPAN), 0) + TAPS - iota((8, SPAN), 1)
    return (lag >= 0) & (lag < TAPS)


def operators(
    cap, ring, here, lengths, spot_col, cot, weights, fore_base, back_base, ctx, ahead, behind, after
):
    dense = PLANE_ROWS * WIDTH
    return call(
        functools.partial(operator_kernel, cap, ring),
        parcels_shape(cap, ring)
        + (
            jax.ShapeDtypeStruct((GROUPS, SPAN), F32),
            jax.ShapeDtypeStruct((8, WIDTH), F32),
        ),
        n_in_smem=2,
        n_in=8,
        n_any=1,
        scratch=[
            pltpu.VMEM((PLANE_ROWS + 8, WIDTH), F32),
            pltpu.VMEM((PLANE_ROWS, WIDTH), F32),
            pltpu.VMEM((PLANE_ROWS, WIDTH), BF),
            pltpu.VMEM((PLANE_ROWS + TAPS, WIDTH), BF),
            pltpu.VMEM((PLANE_ROWS + TAPS, WIDTH), BF),
            pltpu.VMEM((PLANE_ROWS + 8, WIDTH), F32),
            pltpu.VMEM((GROUPS * TAPS, SPAN), BF),
            pltpu.VMEM((GROUPS * TAPS, SPAN), BF),
            pltpu.VMEM((GROUPS * TAPS, SPAN), F32),
            pltpu.VMEM((PLANE_ROWS, STREAMS * WIDTH), BF),
            pltpu.VMEM((PLANES * cap, PLANE_ROWS), BF),
        ],
        flops=2 * dense * (PLANES * cap * STREAMS + 3 * GROUPS * SPAN),
        bytes_accessed=6 * 2**20,
    )(here, lengths, spot_col, cot, weights, fore_base, back_base, ctx, ahead, behind, after)


def around(value, step, axis, length):
    return lax.ppermute(value, axis, [(i, (i + step) % length) for i in range(length)])


def onward(value, step):
    pairs = [(i, i + step) for i in range(PLANES) if 0 <= i + step < PLANES]
    return lax.ppermute(value, "z", pairs)


def swap_in_plane(value):
    return lax.all_to_all(value, IN_PLANE, 0, 0, tiled=True)


def in_order(part, axis, length, pieces=None):
    at = lax.axis_index(axis)
    parts = [pieces[s] if pieces else part for s in range(length)]
    parts = parts[:1] + [around(parts[s], s, axis, length) for s in range(1, length)]
    turned = jnp.concatenate(
        [parts[(length - 1 - k) % length] for k in range(2 * length - 1)], axis=0
    )
    rows = parts[0].shape[0]
    return lax.dynamic_slice_in_dim(turned, (length - 1 - at) * rows, length * rows, 0)


def cotangent_of_plane(grad_out):
    quarter = lax.axis_index("y")
    width = CHUNKS * WIDTH
    pieces = [
        lax.dynamic_slice_in_dim(grad_out, ((quarter + s) % QUARTERS) * width, width, 1)
        for s in range(QUARTERS)
    ]
    return in_order(None, "y", QUARTERS, pieces)


def filters_of_device(se_filter, mr_filter):
    quarter = lax.axis_index("y")
    groups = CHUNKS * GROUPS
    short_taps = lax.dynamic_slice_in_dim(se_filter, quarter * groups, groups, 1)
    short_taps = jnp.repeat(short_taps.astype(F32), PER_GROUP, axis=1)
    short_taps = jnp.concatenate([short_taps, jnp.zeros((1, CHUNKS * WIDTH), F32)], axis=0)
    taps = lax.dynamic_slice_in_dim(mr_filter, quarter * groups, groups, 1)
    taps = jnp.transpose(taps.astype(F32))
    fore_base = jnp.pad(taps[:, ::-1], ((0, 0), (1, TAPS - 1)))
    back_base = jnp.pad(taps, ((0, 0), (0, TAPS)))
    return short_taps, fore_base, back_base


def filter_sums(long_parts, short_parts):
    groups = CHUNKS * GROUPS
    long_here = jnp.concatenate(long_parts, axis=0)[:, 1 : TAPS + 1][:, ::-1]
    short_here = jnp.concatenate(short_parts, axis=1).reshape(8, groups, PER_GROUP).sum(axis=2)
    together = jnp.concatenate(
        [long_here, jnp.pad(short_here, ((0, 0), (0, TAPS - groups)))], axis=0
    )
    return jnp.sum(in_order(together[None], "z", PLANES), axis=0)


def filter_totals(sums):
    groups = CHUNKS * GROUPS
    summed = lax.all_gather(sums, "y") * (PLANES * PLANE_ROWS * PER_GROUP) ** -0.5
    long_total = jnp.transpose(summed[:, :groups, :], (2, 0, 1)).reshape(TAPS, QUARTERS * groups)
    short_total = jnp.transpose(summed[:, groups : groups + SHORT, :groups], (1, 0, 2)).reshape(
        SHORT, QUARTERS * groups
    )
    return short_total, long_total


def exchange_and_operate(cap, here, lengths, codes, spots, cot, filters, rows, sent_a):
    short_taps, fore_base, back_base = filters
    lanes = [slice(c * WIDTH, (c + 1) * WIDTH) for c in range(CHUNKS)]
    mine = [slice(c * GROUPS, (c + 1) * GROUPS) for c in range(CHUNKS)]

    def exchange(ring, parts, way):
        if not ring:
            return [lax.all_to_all(parts[0], "z", 0, 0, tiled=True)]
        moved = {s: around(parts[s], way * s, "z", PLANES) for s in (1, 7, 4, 3, 5, 2, 6)}
        return [parts[0]] + [moved[s] for s in range(1, PLANES)]

    def arrive(ring, chunk, parcels, after):
        ctx, ahead, behind = context(
            cap, ring, here, lengths, spots[0], cot[:, lanes[chunk]],
            short_taps[:, lanes[chunk]], back_base[mine[chunk]], parcels, after,
        )
        return ctx, onward(ahead, 1), onward(behind, -1)

    def operate(ring, chunk, after, ctx, ahead, behind):
        *parcels, longs, shorts = operators(
            cap, ring, here, lengths, spots[1], cot[:, lanes[chunk]],
            short_taps[:, lanes[chunk]], fore_base[mine[chunk]], back_base[mine[chunk]],
            ctx, ahead, behind, after,
        )
        return parcels, longs, shorts

    if sent_a is None:
        sent_a = pack(cap, True, here, rows[0], codes[0], here)
    parcels_a = exchange(True, sent_a, 1)
    sent_b = pack(cap, RING_B, here, rows[1], codes[0], here)
    sent_b[0] = pass_on(sent_b[0], *parcels_a[1:], *spots, *filters)
    parcels_b = exchange(RING_B, sent_b, 1)
    arrived_a = arrive(True, 0, parcels_a, sent_b[0])
    arrived_b = arrive(RING_B, 1, parcels_b, arrived_a[0])
    made_a, long_a, short_a = operate(RING_BACK_A, 0, arrived_b[0], *arrived_a)
    made_a[0] = pass_on(made_a[0], *arrived_b[1:])
    returned_a = exchange(RING_BACK_A, made_a, -1)
    made_b, long_b, short_b = operate(True, 1, here, *arrived_b)
    sums = filter_sums([long_a, long_b], [short_a, short_b])
    made_b[4] = pass_on(made_b[4], returned_a[-1], sums)
    returned_b = exchange(True, made_b, -1)
    back_a = swap_in_plane(unpack(cap, RING_BACK_A, here, codes[1], returned_a, made_b[4]))
    back_b = swap_in_plane(unpack(cap, True, here, codes[1], returned_b, back_a))
    totals = filter_totals(sums)
    return (back_a, back_b), totals


def on_device(loaded, row_plan, lengths, se_filter, mr_filter, grad_out):
    here = lax.axis_index("z").astype(I32).reshape(1)
    own = row_plan.reshape(1, OWN_ROWS)
    rows_a = swap_in_plane(split_channels(loaded, 0, write_note(own), lengths))
    along = own
    for step in (4, 2, 1):
        along = jnp.concatenate([along, around(along, step, "z", PLANES)], axis=0)
    along = along.reshape(2, 2, 2, OWN_ROWS).transpose(2, 1, 0, 3).reshape(2, WIDTH)
    cot = cotangent_of_plane(grad_out)
    filters = filters_of_device(se_filter, mr_filter)
    mine = read_note(rows_a, 1, OWN_ROWS).reshape(1, PLANE_ROWS)
    codes = sender_codes(mine)
    sent_a = pack(LEAN_CAP, True, here, rows_a, codes[0], cot)
    rows_b = swap_in_plane(split_channels(loaded, 1, write_note(along), sent_a[1]))
    plan = read_note(rows_b, 2, WIDTH).reshape(PEERS, PLANES, OWN_ROWS)
    plan = jnp.transpose(plan, (1, 0, 2)).reshape(PLANES, PLANE_ROWS)
    spot_row, spot_col, most = receiver_spots(here, plan)
    given = (here, lengths, codes, (spot_row, spot_col), cot, filters, (rows_a, rows_b))
    lean = exchange_and_operate(LEAN_CAP, *given, sent_a)

    def finish(lean, given):
        return (merge_channels(lean[0]),) + lean[1]

    def again(lean, given):
        return finish(exchange_and_operate(FULL_CAP, *given, None), given)

    return lax.cond(most[0, 0] <= LEAN_CAP, finish, again, lean, given)


def solution(mesh):
    grid = Mesh(mesh.devices.reshape(PLANES, QUARTERS, 4, 2), ALL_AXES)
    placed = (
        P(None, ALL_AXES, None),
        P(ALL_AXES),
        P(),
        P(None, ("x", "c")),
        P(None, ("x", "c")),
        P(("z", "y"), ("x", "c")),
    )
    return jax.shard_map(
        on_device,
        mesh=grid,
        in_specs=placed,
        out_specs=(P(None, ALL_AXES, None), P(None, ("x", "c")), P(None, ("x", "c"))),
        check_vma=False,
    )
```
